128 devices in a mesh: scene: 32 (over x, z, core), dp: 4 (over y).
Axes of the slice: x: 4, y: 4, z: 4, core: 2. Of those that a mesh axis runs over, the one named last changes fastest.
Arguments:
- points_feat: bfloat16 [4, 16384, 512], P('dp', 'scene'), may hold values from -8 to 8
- neighbours: int32 [4, 16384, 4], P('dp', 'scene'), may hold values from 0 to 767, as said below
- block_dest: int32 [4, 512], P('dp'), may hold values from 0 to 511, as said below
- lengths: int32 [4, 32], P('dp', 'scene'), may hold values from 1 to 512, 12288 in all within a row
- conv_weight: bfloat16 [4, 512, 512], replicated, may hold values from -0.125 to 0.125
- norm_gain: float32 [512], replicated, may hold values from 0.1 to 1.9
- qkv_weight: bfloat16 [512, 1536], replicated, may hold values from -0.26516504 to 0.26516504
- proj_weight: bfloat16 [512, 512], replicated, may hold values from -0.25 to 0.25
- out_grad: bfloat16 [4, 16384, 512], P('dp', 'scene'), may hold values from -6 to 6
Outputs:
- block_out: bfloat16 [4, 16384, 512], P('dp', 'scene')
- feat_grad: bfloat16 [4, 16384, 512], P('dp', 'scene')
- conv_grad: float32 [4, 512, 512], P(None, 'scene')
- qkv_grad: float32 [512, 1536], P('scene')
- proj_grad: float32 [512, 512], P('scene')
The draws below stay inside these ranges and needn't reach their ends.
Inputs may be any that keep to these rules, and one draw needn't show every extreme that they name: `neighbours`: entries index a device's 128 rows of the preceding region, its own 512 rows, then 128 rows of the following region; tap 0 is the point itself and the other taps lie within 128 rows of it. `block_dest`: each tile's row is a permutation of its 512 blocks; within a tile, block j of every device moves the same number of devices forward along scene, cyclically, and one device sends exactly 1 block to some device and never more to any.
All inputs are finite; a program needn't handle non-finite values. No bound on the sum of `lengths` on one device may be relied on, other than what follows from the above.
Results may differ from the reference program's by a relative error of at most 0.034.
Values may be sent and summed in bfloat16 or wider, within the bound.
No kernel may reach another device: no remote copies, remote signals or barrier semaphores. Data moves between devices by JAX's collectives and lax.ppermute only.
A program may use at most 128 MiB of HBM per device.

```python
import math
import jax
import jax.numpy as jnp
import numpy as np
from jax import lax

C = 512
HEADS = 32
PATCH = 512
BLOCK = 32
TAPS = 4
HALO = 128
PATCHES_DEV = 1
ROWS = 512
BLK_DEV = 16
NBLK = 512
POINTS = 16384
BATCH = 4
N_SCENE = 32


def draw_points_feat(key, part):
    key = jax.random.fold_in(key, 31)
    return jax.random.truncated_normal(key, -6.0, 6.0, (BATCH, POINTS, C), jnp.float32).astype(jnp.bfloat16)


def draw_qkv_weight(key, part):
    key = jax.random.fold_in(key, 37)
    return (jax.random.truncated_normal(key, -6.0, 6.0, (C, 3 * C), jnp.float32) * C ** (-0.5)).astype(jnp.bfloat16)


def draw_neighbours(key, part):
    key = jax.random.fold_in(key, 11)
    spots = jnp.arange(POINTS, dtype=jnp.int32) % ROWS
    offsets = jax.random.randint(key, (BATCH, POINTS, TAPS), -HALO, HALO + 1, dtype=jnp.int32)
    taps = jnp.arange(TAPS, dtype=jnp.int32)
    offsets = jnp.where(taps[None, None, :] == 0, 0, offsets)
    index = spots[None, :, None] + HALO + offsets
    first = (spots[None, :, None] == 0) & (taps[None, None, :] == 1)
    final = (spots[None, :, None] == ROWS - 1) & (taps[None, None, :] == 1)
    index = jnp.where(first, 0, index)
    index = jnp.where(final, ROWS + 2 * HALO - 1, index)
    return index.astype(jnp.int32)


def draw_block_dest(key, part):
    key = jax.random.fold_in(key, 23)
    shift_keys = jax.random.split(jax.random.fold_in(key, 1), BATCH)
    orders = jax.vmap(lambda one_key: jax.random.permutation(one_key, N_SCENE))(shift_keys)
    shifts = orders[:, jnp.arange(BLK_DEV) % N_SCENE]
    slot_keys = jax.random.split(jax.random.fold_in(key, 2), BATCH * N_SCENE)
    slots = jax.vmap(lambda one_key: jax.random.permutation(one_key, BLK_DEV))(slot_keys).reshape(BATCH, N_SCENE, BLK_DEV)
    source = jnp.arange(N_SCENE, dtype=jnp.int32)[None, :, None]
    target = (source + shifts[:, None, :]) % N_SCENE
    tiles = jnp.arange(BATCH, dtype=jnp.int32)[:, None, None]
    columns = jnp.arange(BLK_DEV, dtype=jnp.int32)[None, None, :]
    slot = slots[tiles, target, columns]
    return (target * BLK_DEV + slot).reshape(BATCH, NBLK).astype(jnp.int32)


def steps_of(own_key, extent, cuts, low, largest):
    def one(axis_at, shards_of):
        draws = jax.random.uniform(jax.random.fold_in(jax.random.fold_in(own_key, 6), axis_at), (shards_of,), jnp.float32, low / len(cuts), largest / len(cuts))
        return jnp.repeat(jnp.exp(draws), extent[axis_at] // shards_of).reshape((-1,) + (1,) * (len(extent) - axis_at - 1))

    loudness = one(*cuts[0])
    for cut in cuts[1:]:
        loudness = loudness * one(*cut)
    return loudness


def profile(count, total, bound, skew):
    portions = [(1 << 20) // math.isqrt(standing ** skew) + 1 for standing in range(2, count + 1)]
    rest, counts = total - bound - (count - 1), [1] * (count - 1)
    while rest > 0:
        candidates = [i for i in range(count - 1) if counts[i] < bound]
        whole, left = sum([portions[i] for i in candidates]), rest
        for i in candidates:
            addition = min(bound - counts[i], max(1, left * portions[i] // whole), rest)
            counts[i] = counts[i] + addition
            rest = rest - addition
    return np.array([bound] + counts)


def uneven_parts(stream_key, count, total, bound, slope):
    if count == 2:
        one = jax.random.randint(stream_key, (), max(1, total - bound), min(bound, total - 1) + 1)
        return jnp.stack([one, total - one])
    tallies = jnp.asarray(profile(count, total, bound, slope), jnp.int32)
    twos = (count - 1) // 2
    source_of, receiver = tallies[1:1 + 2 * twos:2], tallies[2:2 + 2 * twos:2]
    room = jnp.minimum(source_of - 1, bound - receiver)
    moved = jax.random.randint(jax.random.fold_in(stream_key, 1), (twos,), 0, 1 << 20) % (room + 1)
    tallies = tallies.at[1:1 + 2 * twos:2].set(source_of - moved).at[2:2 + 2 * twos:2].set(receiver + moved)
    return tallies[jax.random.permutation(jax.random.fold_in(stream_key, 2), count)]


def scatter_about(stream_key, shape, scale, most, cuts=(), kind=jnp.bfloat16):
    gain = steps_of(stream_key, shape, cuts, -0.22, 0.18) if cuts else 1.0
    entries = jax.random.normal(stream_key, shape, jnp.float32) * scale * gain
    return jnp.minimum(jnp.maximum(entries, -most), most).astype(kind)


def setup_inputs(seed: int = 0) -> dict:
    streams_of = jax.random.split(jax.random.key(seed), 10)
    return {
        "points_feat": draw_points_feat(jax.random.fold_in(streams_of[9], 71), 0),
        "neighbours": draw_neighbours(jax.random.fold_in(streams_of[9], 71), 0),
        "block_dest": draw_block_dest(jax.random.fold_in(streams_of[9], 71), 0),
        "lengths": jax.vmap(lambda own: uneven_parts(own, N_SCENE * PATCHES_DEV, N_SCENE * PATCHES_DEV * PATCH * 3 // 4, PATCH, 1))(jax.random.split(streams_of[3], BATCH)).reshape((BATCH, N_SCENE * PATCHES_DEV)).astype(jnp.int32),
        "conv_weight": scatter_about(streams_of[4], (TAPS, C, C), (TAPS * C) ** -0.5, 0.125),
        "norm_gain": jnp.clip(1.0 + 0.18 * jax.random.normal(streams_of[5], (C,), jnp.float32), 0.1, 1.9),
        "qkv_weight": draw_qkv_weight(jax.random.fold_in(streams_of[9], 71), 0),
        "proj_weight": scatter_about(streams_of[7], (C, C), C ** -0.5, 0.25),
        "out_grad": scatter_about(streams_of[8], (BATCH, POINTS, C), 1.0, 6.0, ((0, 4), (1, 32))),
    }


EPS = 1e-05

def product(form, left, right):
    return jnp.einsum(form, left.astype(jnp.float32), right.astype(jnp.float32))

def split_heads(flat):
    patches, prow, channels = flat.shape
    group = min(4, HEADS)
    parts = flat.reshape(patches, prow, HEADS // group, group, channels // HEADS)
    return jnp.transpose(parts, (2, 0, 1, 3, 4))

def join_heads(parts):
    groups, patches, prow, group, head_size = parts.shape
    return jnp.transpose(parts, (1, 2, 0, 3, 4)).reshape(patches, prow, groups * group * head_size)

def live_rows(lengths_here, prow):
    return (jnp.arange(prow, dtype=jnp.int32)[None, :] < lengths_here[:, None])[..., None]

def probabilities(query_rows, key_rows, lengths_here):
    head_size = query_rows.shape[-1]
    prow = key_rows.shape[1]
    scores = product('nqhd,nkhd->nhqk', query_rows, key_rows) * head_size ** (-0.5)
    allowed = jnp.arange(prow, dtype=jnp.int32)[None, None, None, :] < lengths_here[:, None, None, None]
    scores = jnp.where(allowed, scores, -1e+30)
    highest = lax.optimization_barrier(jnp.max(scores, axis=-1, keepdims=True))
    raised = jnp.exp(scores - highest)
    return raised / lax.optimization_barrier(jnp.sum(raised, axis=-1, keepdims=True))

def attend(rows_here, lengths_here, norm_multiplier, qkv_weight, proj_weight):
    channels = rows_here.shape[2]
    values_f = rows_here.astype(jnp.float32)
    centre = lax.optimization_barrier(jnp.mean(values_f, axis=-1, keepdims=True))
    centered_rows = values_f - centre
    inverse_deviation = lax.rsqrt(lax.optimization_barrier(jnp.mean(centered_rows * centered_rows, axis=-1, keepdims=True)) + EPS)
    standardized_input = centered_rows * inverse_deviation
    normalized_rows = (standardized_input * norm_multiplier).astype(jnp.bfloat16)
    query_key_value = product('npc,cd->npd', normalized_rows, qkv_weight).astype(jnp.bfloat16)
    query_all = split_heads(query_key_value[..., :channels])
    key_all = split_heads(query_key_value[..., channels:2 * channels])
    value_all = split_heads(query_key_value[..., 2 * channels:])

    def one_group(pieces):
        query_rows, key_rows, value_rows = pieces
        probs_b = probabilities(query_rows, key_rows, lengths_here).astype(jnp.bfloat16)
        return product('nhqk,nkhd->nqhd', probs_b, value_rows)
    heads_f = join_heads(lax.map(one_group, (query_all, key_all, value_all)))
    merged_head_output = jnp.where(live_rows(lengths_here, rows_here.shape[1]), heads_f, 0.0).astype(jnp.bfloat16)
    attention_result = product('npc,cd->npd', merged_head_output, proj_weight).astype(jnp.bfloat16)
    return (attention_result, (normalized_rows, standardized_input, inverse_deviation, query_key_value, merged_head_output))

def attend_back(cot_here, lengths_here, norm_multiplier, qkv_weight, proj_weight, residuals_kept):
    normalized_rows, standardized_input, inverse_deviation, query_key_value, merged_head_output = residuals_kept
    channels = cot_here.shape[2]
    part_proj = product('npc,npd->cd', merged_head_output, cot_here)
    d_full = product('npd,cd->npc', cot_here, proj_weight)
    d_heads = jnp.where(live_rows(lengths_here, cot_here.shape[1]), d_full, 0.0).astype(jnp.bfloat16)
    query_all = split_heads(query_key_value[..., :channels])
    key_all = split_heads(query_key_value[..., channels:2 * channels])
    value_all = split_heads(query_key_value[..., 2 * channels:])

    def one_group(pieces):
        query_rows, key_rows, value_rows, row_gradient, out_rows = pieces
        probs = probabilities(query_rows, key_rows, lengths_here)
        probs_b = probs.astype(jnp.bfloat16)
        head_size = query_rows.shape[-1]
        d_value = product('nhqk,nqhd->nkhd', probs_b, row_gradient)
        d_probs = product('nqhd,nkhd->nhqk', row_gradient, value_rows)
        row_dot = lax.optimization_barrier(jnp.sum(row_gradient.astype(jnp.float32) * out_rows.astype(jnp.float32), axis=-1))
        row_dot = jnp.transpose(row_dot, (0, 2, 1))[..., None]
        d_scores = (probs * (d_probs - row_dot) * head_size ** (-0.5)).astype(jnp.bfloat16)
        d_query = product('nhqk,nkhd->nqhd', d_scores, key_rows)
        d_key = product('nhqk,nqhd->nkhd', d_scores, query_rows)
        return (d_query, d_key, d_value)
    d_query, d_key, d_value = lax.map(one_group, (query_all, key_all, value_all, split_heads(d_heads), split_heads(merged_head_output)))
    d_qkv = jnp.concatenate([join_heads(d_query), join_heads(d_key), join_heads(d_value)], axis=-1).astype(jnp.bfloat16)
    part_qkv = product('npc,npd->cd', normalized_rows, d_qkv)
    scaled_rows = product('npd,cd->npc', d_qkv, qkv_weight) * norm_multiplier
    row_gradient = inverse_deviation * (scaled_rows - lax.optimization_barrier(jnp.mean(scaled_rows, axis=-1, keepdims=True)) - standardized_input * lax.optimization_barrier(jnp.mean(scaled_rows * standardized_input, axis=-1, keepdims=True)))
    return (row_gradient.astype(jnp.bfloat16), part_qkv, part_proj)

def reference(points_feat, neighbours, block_dest, lengths, conv_weight, norm_gain, qkv_weight, proj_weight, out_grad):
    channels = points_feat.shape[2]
    points = points_feat.shape[1]
    conv_total = jnp.zeros((TAPS, channels, channels), jnp.float32)
    qkv_total = jnp.zeros((channels, 3 * channels), jnp.float32)
    proj_total = jnp.zeros((channels, channels), jnp.float32)
    outputs = []
    feat_grads = []
    for tile in range(BATCH):
        feats = points_feat[tile]
        spots = jnp.arange(points, dtype=jnp.int32)
        owner = spots // ROWS
        index = owner[:, None] * ROWS + neighbours[tile] - HALO
        inside = (index >= 0) & (index < points)
        safe = jnp.clip(index, 0, points - 1)
        gathered = jnp.where(inside[..., None], feats[safe], jnp.zeros((), jnp.bfloat16))
        hidden = (feats.astype(jnp.float32) + product('rkc,kcd->rd', gathered, conv_weight)).astype(jnp.bfloat16)
        dest = block_dest[tile]
        zorder = jnp.zeros((NBLK, BLOCK, channels), jnp.bfloat16).at[dest].set(hidden.reshape(NBLK, BLOCK, channels))
        cot_z = jnp.zeros((NBLK, BLOCK, channels), jnp.bfloat16).at[dest].set(out_grad[tile].reshape(NBLK, BLOCK, channels))
        patch_rows = zorder.reshape(N_SCENE, PATCHES_DEV, PATCH, channels)
        cot_rows = cot_z.reshape(N_SCENE, PATCHES_DEV, PATCH, channels)
        tile_lengths = lengths[tile].reshape(N_SCENE, PATCHES_DEV)

        def one_region(pieces):
            rows_here, cot_here, lengths_here = pieces
            attention_result, residuals_kept = attend(rows_here, lengths_here, norm_gain, qkv_weight, proj_weight)
            row_gradient, part_qkv, part_proj = attend_back(cot_here, lengths_here, norm_gain, qkv_weight, proj_weight, residuals_kept)
            return (attention_result, row_gradient, part_qkv, part_proj)
        attention_result, row_gradient, part_qkv, part_proj = lax.map(one_region, (patch_rows, cot_rows, tile_lengths))
        qkv_total = qkv_total + lax.optimization_barrier(jnp.sum(part_qkv, axis=0))
        proj_total = proj_total + lax.optimization_barrier(jnp.sum(part_proj, axis=0))
        attended_scan = attention_result.reshape(NBLK, BLOCK, channels)[dest].reshape(points, channels)
        d_scan = row_gradient.reshape(NBLK, BLOCK, channels)[dest].reshape(points, channels)
        outputs.append((hidden.astype(jnp.float32) + attended_scan.astype(jnp.float32)).astype(jnp.bfloat16))
        d_hidden = out_grad[tile].astype(jnp.float32) + d_scan.astype(jnp.float32)
        d_hidden_b = d_hidden.astype(jnp.bfloat16)
        conv_total = conv_total + product('rkc,rd->kcd', gathered, d_hidden_b)
        spread = product('rd,kcd->rkc', d_hidden_b, conv_weight)
        spread = jnp.where(inside[..., None], spread, 0.0)
        moved = jnp.zeros((points, channels), jnp.float32).at[safe].add(spread)
        feat_grads.append((d_hidden + moved).astype(jnp.bfloat16))
    return (jnp.stack(outputs), jnp.stack(feat_grads), conv_total, qkv_total, proj_total)
```

```python
import jax
import jax.numpy as jnp
from jax import lax
from jax.experimental import pallas as pl
from jax.experimental.pallas import tpu as pltpu
from jax.sharding import Mesh
from jax.sharding import PartitionSpec as P

HEADS = 32
HEAD = 16
PATCH = 512
BLOCK = 32
BLOCKS = 16
HALO = 128
TAPS = 4
GROUP = 4
EPS = 1e-05
F32 = jnp.float32
BF16 = jnp.bfloat16
SCENE = ("x", "z", "core")


def dot(left, right, left_dim=1, right_dim=0):
    return lax.dot_general(
        left, right, (((left_dim,), (right_dim,)), ((), ())), preferred_element_type=F32
    )


def call(kernel, outs, operands, smem=0, flops=0, moved=0, transcendentals=0, scratch=()):
    memory = [pltpu.SMEM] * smem + [pltpu.VMEM] * (len(operands) - smem)
    return pl.pallas_call(
        kernel,
        out_shape=[jax.ShapeDtypeStruct(shape, dtype) for shape, dtype in outs],
        in_specs=[pl.BlockSpec(memory_space=space) for space in memory],
        out_specs=[pl.BlockSpec(memory_space=pltpu.VMEM) for _ in outs],
        scratch_shapes=list(scratch),
        compiler_params=pltpu.CompilerParams(vmem_limit_bytes=48 << 20),
        cost_estimate=pl.CostEstimate(
            flops=flops, bytes_accessed=moved, transcendentals=transcendentals
        ),
    )(*operands)


def target_of(dest, me, block):
    return dest[me * BLOCKS + block] // BLOCKS


def source_of(dest, me, block, scenes):
    shift = dest[block] // BLOCKS
    source = lax.rem(me - shift + scenes, scenes)
    return source, lax.rem(dest[source * BLOCKS + block], BLOCKS)


def pack_kernel(dest, here, blocks, packed):
    packed[...] = jnp.zeros_like(packed)
    for block in range(BLOCKS):
        packed[target_of(dest, here[0], block)] = blocks[pl.ds(block * BLOCK, BLOCK), :]


def conv_kernel(dest, here, low, feats, high, nearby, weight, gathered, hidden, packed, near):
    near[0:HALO, :] = low[...]
    near[HALO : HALO + PATCH, :] = feats[...]
    near[HALO + PATCH :, :] = high[...]
    spots = lax.broadcasted_iota(jnp.int32, (HALO, 3 * HALO), 1)
    packed[...] = jnp.zeros_like(packed)
    for part in range(PATCH // HALO):
        rows = pl.ds(part * HALO, HALO)
        window = near[pl.ds(part * HALO, 3 * HALO), :]
        own = feats[rows, :]
        total = own.astype(F32) + dot(own, weight[0])
        for tap in range(1, TAPS):
            index = nearby[rows, pl.ds(tap, 1)] - part * HALO
            chosen = jnp.where(spots == index, 1.0, 0.0).astype(BF16)
            picked = dot(chosen, window).astype(BF16)
            gathered[tap - 1, rows, :] = picked
            total = total + dot(picked, weight[tap])
        hidden[rows, :] = total.astype(BF16)
        for block in range(part * HALO // BLOCK, (part + 1) * HALO // BLOCK):
            packed[target_of(dest, here[0], block)] = hidden[pl.ds(block * BLOCK, BLOCK), :]


def forward_kernel(
    dest, here, got, got_cot, gain, qkv_weight_t, proj_weight,
    packed, probs, recip, qkv, normed, xhat, inverse, heads, d_heads, part_proj,
    rows_f, cot_z, attended,
):
    step = pl.program_id(0)
    scenes = got.shape[0]
    length = here[1]

    @pl.when(step == 0)
    def _():
        for block in range(BLOCKS):
            source, slot = source_of(dest, here[0], block, scenes)
            rows = pl.ds(pl.multiple_of(slot * BLOCK, BLOCK), BLOCK)
            rows_f[rows, :] = got[source].astype(F32)
        rows_t = rows_f[...].T
        centred = rows_t - jnp.mean(rows_t, axis=0, keepdims=True)
        scale = lax.rsqrt(jnp.mean(centred * centred, axis=0, keepdims=True) + EPS)
        standard = centred * scale
        inverse[...] = scale
        xhat[...] = standard
        normed[...] = (standard * gain[...]).astype(BF16)
        qkv[...] = dot(qkv_weight_t[...], normed[...]).astype(BF16)

    sub = lax.broadcasted_iota(jnp.int32, (HEAD, PATCH), 0)
    spot = lax.broadcasted_iota(jnp.int32, (HEAD, PATCH), 1)
    dead = jnp.where((sub == 0) & (spot >= length), -1e30, 0.0).astype(BF16)
    ones = jnp.where(sub == 0, 1.0, 0.0).astype(BF16)
    live = lax.broadcasted_iota(jnp.int32, (1, PATCH), 1) < length
    channels = HEADS * HEAD
    for one in range(GROUP):
        row = pl.multiple_of((step * GROUP + one) * HEAD, HEAD)
        query = (qkv[pl.ds(row, HEAD), :].astype(F32) * HEAD ** (-0.5)).astype(BF16)
        key = qkv[pl.ds(channels + row, HEAD), :]
        value = qkv[pl.ds(2 * channels + row, HEAD), :]
        scores = dot(
            jnp.concatenate([key, dead], axis=0), jnp.concatenate([query, ones], axis=0), 0, 0
        )
        raised = jnp.exp(scores - jnp.max(scores, axis=0, keepdims=True)).astype(BF16)
        probs[one] = raised
        out = dot(jnp.concatenate([value, ones], axis=0), raised)
        over = 1.0 / out[HEAD : HEAD + 1]
        recip[one] = over
        heads[pl.ds(row, HEAD), :] = jnp.where(live, out[:HEAD] * over, 0.0).astype(BF16)

    @pl.when(step == pl.num_programs(0) - 1)
    def _():
        packed[...] = jnp.zeros_like(packed)
        attended[...] = dot(heads[...], proj_weight[...], 0, 0).astype(BF16)
        for block in range(BLOCKS):
            source, slot = source_of(dest, here[0], block, scenes)
            rows = pl.ds(pl.multiple_of(slot * BLOCK, BLOCK), BLOCK)
            packed[source] = attended[rows, :]
            cot_z[rows, :] = got_cot[source]
        part_proj[...] = dot(heads[...], cot_z[...]).astype(BF16)
        d_full = dot(proj_weight[...], cot_z[...], 1, 1)
        d_heads[...] = jnp.where(live, d_full, 0.0).astype(BF16)


def backward_kernel(
    dest, here, probs, recip, qkv, normed, xhat, inverse, heads, d_heads, gain, qkv_weight,
    packed, part_qkv,
    d_qkv, d_rows,
):
    step = pl.program_id(0)
    scenes = packed.shape[0]
    channels = HEADS * HEAD
    sub = lax.broadcasted_iota(jnp.int32, (HEAD, PATCH), 0)
    ones = jnp.where(sub < 3, 1.0, 0.0).astype(BF16)
    for one in range(GROUP):
        row = pl.multiple_of((step * GROUP + one) * HEAD, HEAD)
        query = qkv[pl.ds(row, HEAD), :].astype(F32)
        key = qkv[pl.ds(channels + row, HEAD), :]
        value = qkv[pl.ds(2 * channels + row, HEAD), :]
        over = recip[one]
        d_out = d_heads[pl.ds(row, HEAD), :]
        d_out_f = d_out.astype(F32)
        row_dot = jnp.sum(
            d_out_f * heads[pl.ds(row, HEAD), :].astype(F32), axis=0, keepdims=True
        )
        first = row_dot.astype(BF16).astype(F32)
        second = (row_dot - first).astype(BF16).astype(F32)
        third = row_dot - first - second
        minus = -jnp.where(sub == 0, first, jnp.where(sub == 1, second, jnp.where(sub == 2, third, 0.0)))
        raised = probs[one]
        d_value = dot((d_out_f * over).astype(BF16), raised, 1, 1)
        d_probs = dot(
            jnp.concatenate([value, ones], axis=0),
            jnp.concatenate([d_out, minus.astype(BF16)], axis=0), 0, 0,
        )
        d_scores = (raised.astype(F32) * d_probs).astype(BF16)
        scaled = over * HEAD ** (-0.5)
        d_query = dot(key, d_scores) * scaled
        d_key = dot((query * scaled).astype(BF16), d_scores, 1, 1)
        d_qkv[pl.ds(row, HEAD), :] = d_query.astype(BF16)
        d_qkv[pl.ds(channels + row, HEAD), :] = d_key.astype(BF16)
        d_qkv[pl.ds(2 * channels + row, HEAD), :] = d_value.astype(BF16)

    @pl.when(step == pl.num_programs(0) - 1)
    def _():
        spread = dot(qkv_weight[...], d_qkv[...]) * gain[...]
        standard = xhat[...]
        row_gradient = inverse[...] * (
            spread
            - jnp.mean(spread, axis=0, keepdims=True)
            - standard * jnp.mean(spread * standard, axis=0, keepdims=True)
        )
        d_rows[...] = row_gradient.T.astype(BF16)
        packed[...] = jnp.zeros_like(packed)
        for block in range(BLOCKS):
            source, slot = source_of(dest, here[0], block, scenes)
            packed[source] = d_rows[pl.ds(pl.multiple_of(slot * BLOCK, BLOCK), BLOCK), :]
        part_qkv[...] = dot(normed[...], d_qkv[...], 1, 1).astype(BF16)


def hidden_grad_kernel(dest, here, got, cot, d_hidden, d_hidden_b):
    for block in range(BLOCKS):
        rows = pl.ds(block * BLOCK, BLOCK)
        total = cot[rows, :].astype(F32) + got[target_of(dest, here[0], block)].astype(F32)
        d_hidden[rows, :] = total
        d_hidden_b[rows, :] = total.astype(BF16)


def conv_grad_kernel(feats, gathered, d_hidden_b, part):
    for tap in range(TAPS):
        picked = feats[...] if tap == 0 else gathered[tap - 1]
        part[tap] = dot(picked, d_hidden_b[...], 0, 0).astype(BF16)


def feat_grad_kernel(
    dest, here, low, d_hidden_b, high, targets, weight, d_hidden, hidden, got,
    feat_grad, block_out, near,
):
    near[0:HALO, :] = low[...]
    near[HALO : HALO + PATCH, :] = d_hidden_b[...]
    near[HALO + PATCH :, :] = high[...]
    spots = lax.broadcasted_iota(jnp.int32, (HALO, 3 * HALO), 0)
    for part in range(PATCH // HALO):
        rows = pl.ds(part * HALO, HALO)
        around = pl.ds(part * HALO, 3 * HALO)
        window = near[around, :]
        total = d_hidden[rows, :] + dot(d_hidden_b[rows, :], weight[0], 1, 1)
        for tap in range(1, TAPS):
            index = targets[pl.ds(tap, 1), around] - part * HALO
            chosen = jnp.where(spots == index, 1.0, 0.0).astype(BF16)
            total = total + dot(dot(chosen, window).astype(BF16), weight[tap], 1, 1)
        feat_grad[rows, :] = total.astype(BF16)
    for block in range(BLOCKS):
        rows = pl.ds(block * BLOCK, BLOCK)
        block_out[rows, :] = (
            hidden[rows, :].astype(F32) + got[target_of(dest, here[0], block)].astype(F32)
        ).astype(BF16)


def halo(first, last, axis):
    count = lax.axis_size(axis)
    forward = [(i, i + 1) for i in range(count - 1)]
    backward = [(i + 1, i) for i in range(count - 1)]
    return lax.ppermute(last, axis, forward), lax.ppermute(first, axis, backward)


def moved(packed):
    return lax.all_to_all(packed, SCENE, split_axis=0, concat_axis=0, tiled=True)


def whole(shape):
    return pl.BlockSpec(shape, lambda step: (0,) * len(shape))


def per_group(shape):
    return pl.BlockSpec(shape, lambda step: (step,) + (0,) * (len(shape) - 1))


def grid_call(kernel, ins, in_specs, outs, out_specs, scratch, flops, bytes_moved, exps):
    return pl.pallas_call(
        kernel,
        grid=(HEADS // GROUP,),
        out_shape=[jax.ShapeDtypeStruct(shape, dtype) for shape, dtype in outs],
        in_specs=in_specs,
        out_specs=out_specs,
        scratch_shapes=scratch,
        compiler_params=pltpu.CompilerParams(
            vmem_limit_bytes=56 << 20, dimension_semantics=("arbitrary",)
        ),
        cost_estimate=pl.CostEstimate(
            flops=flops, bytes_accessed=bytes_moved, transcendentals=exps
        ),
    )(*ins)


def body(
    points_feat, neighbours, block_dest, lengths, conv_weight, norm_gain, qkv_weight, proj_weight,
    out_grad,
):
    feats = points_feat[0]
    cotangent = out_grad[0]
    nearby = neighbours[0]
    dest = block_dest[0]
    channels = feats.shape[1]
    scenes = lax.axis_size(SCENE)
    here = jnp.stack([lax.axis_index(SCENE).astype(jnp.int32), lengths[0, 0]])
    gain = norm_gain[:, None]
    rows_c = (PATCH, channels)
    square = (channels, channels)
    slots = (scenes, BLOCK, channels)

    low, high = halo(feats[:HALO], feats[PATCH - HALO :], SCENE)
    (packed_cot,) = call(pack_kernel, [(slots, BF16)], [dest, here, cotangent], smem=2, moved=1 << 21)
    got_cot = moved(packed_cot)
    gathered, hidden, packed_hidden = call(
        conv_kernel,
        [((TAPS - 1,) + rows_c, BF16), (rows_c, BF16), (slots, BF16)],
        [dest, here, low, feats, high, nearby, conv_weight],
        smem=2, flops=2 * PATCH * channels * (TAPS * channels + 9 * HALO), moved=8 << 20,
        scratch=[pltpu.VMEM((PATCH + 2 * HALO, channels), BF16)],
    )
    got_hidden = moved(packed_hidden)
    turned = nearby.T
    targets_low, targets_high = halo(turned[:, :HALO], turned[:, PATCH - HALO :], SCENE)
    at_scene = here[0]
    targets = jnp.concatenate(
        [
            jnp.where(at_scene > 0, targets_low - HALO - PATCH, -1 << 20),
            turned - HALO,
            jnp.where(at_scene < scenes - 1, targets_high - HALO + PATCH, -1 << 20),
        ],
        axis=1,
    )
    probs_shape = (HEADS, PATCH, PATCH)
    recip_shape = (HEADS, 1, PATCH)
    smem = pl.BlockSpec(memory_space=pltpu.SMEM)
    pair = HEADS * PATCH * PATCH
    packed_att, probs, recip, qkv, normed, xhat, inverse, heads, d_heads, part_proj = grid_call(
        forward_kernel,
        [dest, here, got_hidden, got_cot, gain, qkv_weight.T, proj_weight],
        [smem, smem, whole(slots), whole(slots), whole((channels, 1)), whole((3 * channels, channels)),
         whole(square)],
        [(slots, BF16), (probs_shape, BF16), (recip_shape, F32), ((3 * channels, PATCH), BF16),
         ((channels, PATCH), BF16), ((channels, PATCH), F32), ((1, PATCH), F32),
         ((channels, PATCH), BF16), ((channels, PATCH), BF16), (square, BF16)],
        [whole(slots), per_group((GROUP, PATCH, PATCH)), per_group((GROUP, 1, PATCH)),
         whole((3 * channels, PATCH)), whole((channels, PATCH)), whole((channels, PATCH)),
         whole((1, PATCH)), whole((channels, PATCH)), whole((channels, PATCH)), whole(square)],
        [pltpu.VMEM(rows_c, F32), pltpu.VMEM(rows_c, BF16), pltpu.VMEM(rows_c, BF16)],
        flops=2 * pair * 64 * 8, bytes_moved=32 << 20, exps=pair,
    )
    got_att = moved(packed_att)
    packed_dz, part_qkv = grid_call(
        backward_kernel,
        [dest, here, probs, recip, qkv, normed, xhat, inverse, heads, d_heads, gain, qkv_weight],
        [smem, smem, per_group((GROUP, PATCH, PATCH)), per_group((GROUP, 1, PATCH)),
         whole((3 * channels, PATCH)), whole((channels, PATCH)), whole((channels, PATCH)),
         whole((1, PATCH)), whole((channels, PATCH)), whole((channels, PATCH)), whole((channels, 1)),
         whole((channels, 3 * channels))],
        [(slots, BF16), ((channels, 3 * channels), BF16)],
        [whole(slots), whole((channels, 3 * channels))],
        [pltpu.VMEM((3 * channels, PATCH), BF16), pltpu.VMEM(rows_c, BF16)],
        flops=4 * pair * 64 * 8, bytes_moved=32 << 20, exps=0,
    )
    got_dz = moved(packed_dz)
    d_hidden, d_hidden_b = call(
        hidden_grad_kernel, [(rows_c, F32), (rows_c, BF16)], [dest, here, got_dz, cotangent],
        smem=2, moved=4 << 20,
    )
    d_low, d_high = halo(d_hidden_b[:HALO], d_hidden_b[PATCH - HALO :], SCENE)
    (part_conv,) = call(
        conv_grad_kernel, [((TAPS,) + square, BF16)], [feats, gathered, d_hidden_b],
        flops=2 * TAPS * PATCH * channels * channels, moved=6 << 20,
    )
    feat_grad, block_out = call(
        feat_grad_kernel, [(rows_c, BF16), (rows_c, BF16)],
        [dest, here, d_low, d_hidden_b, d_high, targets, conv_weight, d_hidden, hidden, got_att],
        smem=2, flops=2 * PATCH * channels * (TAPS * channels + 9 * HALO), moved=8 << 20,
        scratch=[pltpu.VMEM((PATCH + 2 * HALO, channels), BF16)],
    )
    conv_grad = lax.psum(
        lax.psum_scatter(part_conv, SCENE, scatter_dimension=1, tiled=True), "dp"
    ).astype(F32)
    qkv_grad = lax.psum(
        lax.psum_scatter(part_qkv, SCENE, scatter_dimension=0, tiled=True), "dp"
    ).astype(F32)
    proj_grad = lax.psum(
        lax.psum_scatter(part_proj, SCENE, scatter_dimension=0, tiled=True), "dp"
    ).astype(F32)
    return (block_out[None], feat_grad[None], conv_grad, qkv_grad, proj_grad)


def solution(mesh):
    fine = Mesh(mesh.devices.reshape(4, 4, 2, 4), ("x", "z", "core", "dp"))
    return jax.shard_map(
        body,
        mesh=fine,
        in_specs=(
            P("dp", SCENE, None),
            P("dp", SCENE, None),
            P("dp", None),
            P("dp", SCENE),
            P(),
            P(),
            P(),
            P(),
            P("dp", SCENE, None),
        ),
        out_specs=(
            P("dp", SCENE, None),
            P("dp", SCENE, None),
            P(None, SCENE, None),
            P(SCENE, None),
            P(SCENE, None),
        ),
        check_vma=False,
    )
```

```python
import jax
import jax.numpy as jnp
from jax import lax
from jax.experimental import pallas as pl
from jax.experimental.pallas import tpu as pltpu
from jax.sharding import Mesh
from jax.sharding import PartitionSpec as P

HEADS = 32
HEAD = 16
PATCH = 512
BLOCK = 32
BLOCKS = 16
HALO = 128
TAPS = 4
GROUP = 4
EPS = 1e-05
F32 = jnp.float32
BF16 = jnp.bfloat16
SCENE = ("x", "z", "core")


def dot(left, right, left_dim=1, right_dim=0):
    return lax.dot_general(
        left, right, (((left_dim,), (right_dim,)), ((), ())), preferred_element_type=F32
    )


def call(kernel, outs, operands, smem=0, flops=0, moved=0, transcendentals=0, scratch=()):
    memory = [pltpu.SMEM] * smem + [pltpu.VMEM] * (len(operands) - smem)
    return pl.pallas_call(
        kernel,
        out_shape=[jax.ShapeDtypeStruct(shape, dtype) for shape, dtype in outs],
        in_specs=[pl.BlockSpec(memory_space=space) for space in memory],
        out_specs=[pl.BlockSpec(memory_space=pltpu.VMEM) for _ in outs],
        scratch_shapes=list(scratch),
        compiler_params=pltpu.CompilerParams(vmem_limit_bytes=48 << 20),
        cost_estimate=pl.CostEstimate(
            flops=flops, bytes_accessed=moved, transcendentals=transcendentals
        ),
    )(*operands)


def target_of(dest, me, block):
    return dest[me * BLOCKS + block] // BLOCKS


def source_of(dest, me, block, scenes):
    shift = dest[block] // BLOCKS
    source = lax.rem(me - shift + scenes, scenes)
    return source, lax.rem(dest[source * BLOCKS + block], BLOCKS)


def split_parts(here, part, halves):
    core = lax.rem(here[0], 2)
    shard = part.shape[0] // halves[0].shape[0] // 2
    for pair in range(halves[0].shape[0]):
        for half, owner in zip(halves, (1 - core, core)):
            start = pl.multiple_of((2 * pair + owner) * shard, shard)
            half[pair] = part[pl.ds(start, shard), :]


def pack_kernel(dest, here, blocks, packed):
    packed[...] = jnp.zeros_like(packed)
    for block in range(BLOCKS):
        packed[target_of(dest, here[0], block)] = blocks[pl.ds(block * BLOCK, BLOCK), :]


def conv_kernel(dest, here, low, feats, high, nearby, weight, gathered, hidden, packed, near):
    near[0:HALO, :] = low[...]
    near[HALO : HALO + PATCH, :] = feats[...]
    near[HALO + PATCH :, :] = high[...]
    spots = lax.broadcasted_iota(jnp.int32, (HALO, 3 * HALO), 1)
    packed[...] = jnp.zeros_like(packed)
    for part in range(PATCH // HALO):
        rows = pl.ds(part * HALO, HALO)
        window = near[pl.ds(part * HALO, 3 * HALO), :]
        own = feats[rows, :]
        total = own.astype(F32) + dot(own, weight[0])
        for tap in range(1, TAPS):
            index = nearby[rows, pl.ds(tap, 1)] - part * HALO
            chosen = jnp.where(spots == index, 1.0, 0.0).astype(BF16)
            picked = dot(chosen, window).astype(BF16)
            gathered[tap - 1, rows, :] = picked
            total = total + dot(picked, weight[tap])
        hidden[rows, :] = total.astype(BF16)
        for block in range(part * HALO // BLOCK, (part + 1) * HALO // BLOCK):
            packed[target_of(dest, here[0], block)] = hidden[pl.ds(block * BLOCK, BLOCK), :]


def forward_kernel(
    dest, here, got, gain, qkv_weight_t, proj_weight,
    packed, probs, recip, qkv, normed, xhat, inverse, heads,
    rows_f, attended,
):
    step = pl.program_id(0)
    scenes = got.shape[0]
    length = here[1]

    @pl.when(step == 0)
    def _():
        for block in range(BLOCKS):
            source, slot = source_of(dest, here[0], block, scenes)
            rows = pl.ds(pl.multiple_of(slot * BLOCK, BLOCK), BLOCK)
            rows_f[rows, :] = got[source].astype(F32)
        rows_t = rows_f[...].T
        centred = rows_t - jnp.mean(rows_t, axis=0, keepdims=True)
        scale = lax.rsqrt(jnp.mean(centred * centred, axis=0, keepdims=True) + EPS)
        standard = centred * scale
        inverse[...] = scale
        xhat[...] = standard
        normed[...] = (standard * gain[...]).astype(BF16)
        qkv[...] = dot(qkv_weight_t[...], normed[...]).astype(BF16)

    sub = lax.broadcasted_iota(jnp.int32, (HEAD, PATCH), 0)
    spot = lax.broadcasted_iota(jnp.int32, (HEAD, PATCH), 1)
    dead = jnp.where((sub == 0) & (spot >= length), -1e30, 0.0).astype(BF16)
    ones = jnp.where(sub == 0, 1.0, 0.0).astype(BF16)
    live = lax.broadcasted_iota(jnp.int32, (1, PATCH), 1) < length
    channels = HEADS * HEAD
    for one in range(GROUP):
        row = pl.multiple_of((step * GROUP + one) * HEAD, HEAD)
        query = (qkv[pl.ds(row, HEAD), :].astype(F32) * HEAD ** (-0.5)).astype(BF16)
        key = qkv[pl.ds(channels + row, HEAD), :]
        value = qkv[pl.ds(2 * channels + row, HEAD), :]
        scores = dot(
            jnp.concatenate([key, dead], axis=0), jnp.concatenate([query, ones], axis=0), 0, 0
        )
        raised = jnp.exp(scores - jnp.max(scores, axis=0, keepdims=True)).astype(BF16)
        probs[one] = raised
        out = dot(jnp.concatenate([value, ones], axis=0), raised)
        over = 1.0 / out[HEAD : HEAD + 1]
        recip[one] = over
        heads[pl.ds(row, HEAD), :] = jnp.where(live, out[:HEAD] * over, 0.0).astype(BF16)

    @pl.when(step == pl.num_programs(0) - 1)
    def _():
        packed[...] = jnp.zeros_like(packed)
        attended[...] = dot(heads[...], proj_weight[...], 0, 0).astype(BF16)
        for block in range(BLOCKS):
            source, slot = source_of(dest, here[0], block, scenes)
            rows = pl.ds(pl.multiple_of(slot * BLOCK, BLOCK), BLOCK)
            packed[source] = attended[rows, :]


def backward_kernel(
    dest, here, got_cot, probs, recip, qkv, normed, xhat, inverse, heads, gain, qkv_weight,
    proj_weight,
    packed, sent, kept,
    d_qkv, d_rows, d_heads, part,
):
    step = pl.program_id(0)
    scenes = packed.shape[0]
    channels = HEADS * HEAD

    @pl.when(step == 0)
    def _():
        for block in range(BLOCKS):
            source, slot = source_of(dest, here[0], block, scenes)
            rows = pl.ds(pl.multiple_of(slot * BLOCK, BLOCK), BLOCK)
            d_rows[rows, :] = got_cot[source]
        live = lax.broadcasted_iota(jnp.int32, (1, PATCH), 1) < here[1]
        d_full = dot(proj_weight[...], d_rows[...], 1, 1)
        d_heads[...] = jnp.where(live, d_full, 0.0).astype(BF16)
        part[...] = dot(heads[...], d_rows[...]).astype(BF16)
        split_parts(here, part, [sent.at[3], kept.at[3]])

    sub = lax.broadcasted_iota(jnp.int32, (HEAD, PATCH), 0)
    ones = jnp.where(sub < 3, 1.0, 0.0).astype(BF16)
    for one in range(GROUP):
        row = pl.multiple_of((step * GROUP + one) * HEAD, HEAD)
        query = qkv[pl.ds(row, HEAD), :].astype(F32)
        key = qkv[pl.ds(channels + row, HEAD), :]
        value = qkv[pl.ds(2 * channels + row, HEAD), :]
        over = recip[one]
        d_out = d_heads[pl.ds(row, HEAD), :]
        d_out_f = d_out.astype(F32)
        row_dot = jnp.sum(
            d_out_f * heads[pl.ds(row, HEAD), :].astype(F32), axis=0, keepdims=True
        )
        first = row_dot.astype(BF16).astype(F32)
        second = (row_dot - first).astype(BF16).astype(F32)
        third = row_dot - first - second
        minus = -jnp.where(sub == 0, first, jnp.where(sub == 1, second, jnp.where(sub == 2, third, 0.0)))
        raised = probs[one]
        d_value = dot((d_out_f * over).astype(BF16), raised, 1, 1)
        d_probs = dot(
            jnp.concatenate([value, ones], axis=0),
            jnp.concatenate([d_out, minus.astype(BF16)], axis=0), 0, 0,
        )
        d_scores = (raised.astype(F32) * d_probs).astype(BF16)
        scaled = over * HEAD ** (-0.5)
        d_query = dot(key, d_scores) * scaled
        d_key = dot((query * scaled).astype(BF16), d_scores, 1, 1)
        d_qkv[pl.ds(row, HEAD), :] = d_query.astype(BF16)
        d_qkv[pl.ds(channels + row, HEAD), :] = d_key.astype(BF16)
        d_qkv[pl.ds(2 * channels + row, HEAD), :] = d_value.astype(BF16)

    @pl.when(step == pl.num_programs(0) - 1)
    def _():
        spread = dot(qkv_weight[...], d_qkv[...]) * gain[...]
        standard = xhat[...]
        row_gradient = inverse[...] * (
            spread
            - jnp.mean(spread, axis=0, keepdims=True)
            - standard * jnp.mean(spread * standard, axis=0, keepdims=True)
        )
        d_rows[...] = row_gradient.T.astype(BF16)
        packed[...] = jnp.zeros_like(packed)
        for block in range(BLOCKS):
            source, slot = source_of(dest, here[0], block, scenes)
            packed[source] = d_rows[pl.ds(pl.multiple_of(slot * BLOCK, BLOCK), BLOCK), :]
        for third in range(3):
            columns = d_qkv[pl.ds(third * channels, channels), :]
            part[...] = dot(normed[...], columns, 1, 1).astype(BF16)
            split_parts(here, part, [sent.at[third], kept.at[third]])


def hidden_grad_kernel(dest, here, got, cot, d_hidden, d_hidden_b):
    for block in range(BLOCKS):
        rows = pl.ds(block * BLOCK, BLOCK)
        total = cot[rows, :].astype(F32) + got[target_of(dest, here[0], block)].astype(F32)
        d_hidden[rows, :] = total
        d_hidden_b[rows, :] = total.astype(BF16)


def conv_grad_kernel(here, feats, gathered, d_hidden_b, sent, kept, part):
    for tap in range(TAPS):
        picked = feats[...] if tap == 0 else gathered[tap - 1]
        part[...] = dot(picked, d_hidden_b[...], 0, 0).astype(BF16)
        split_parts(here, part, [sent.at[:, tap], kept.at[:, tap]])


def feat_grad_kernel(
    dest, here, low, d_hidden_b, high, targets, weight, d_hidden, hidden, got,
    feat_grad, block_out, near,
):
    near[0:HALO, :] = low[...]
    near[HALO : HALO + PATCH, :] = d_hidden_b[...]
    near[HALO + PATCH :, :] = high[...]
    spots = lax.broadcasted_iota(jnp.int32, (HALO, 3 * HALO), 0)
    for part in range(PATCH // HALO):
        rows = pl.ds(part * HALO, HALO)
        around = pl.ds(part * HALO, 3 * HALO)
        window = near[around, :]
        total = d_hidden[rows, :] + dot(d_hidden_b[rows, :], weight[0], 1, 1)
        for tap in range(1, TAPS):
            index = targets[pl.ds(tap, 1), around] - part * HALO
            chosen = jnp.where(spots == index, 1.0, 0.0).astype(BF16)
            total = total + dot(dot(chosen, window).astype(BF16), weight[tap], 1, 1)
        feat_grad[rows, :] = total.astype(BF16)
    for block in range(BLOCKS):
        rows = pl.ds(block * BLOCK, BLOCK)
        block_out[rows, :] = (
            hidden[rows, :].astype(F32) + got[target_of(dest, here[0], block)].astype(F32)
        ).astype(BF16)


def halo(first, last, axis):
    count = lax.axis_size(axis)
    forward = [(i, i + 1) for i in range(count - 1)]
    backward = [(i + 1, i) for i in range(count - 1)]
    return lax.ppermute(last, axis, forward), lax.ppermute(first, axis, backward)


def moved(packed):
    return lax.all_to_all(packed, SCENE, split_axis=0, concat_axis=0, tiled=True)


def over_cores(sent, kept):
    other = lax.ppermute(sent, "core", [(0, 1), (1, 0)])
    return (kept.astype(F32) + other.astype(F32)).astype(BF16)


def summed(parts, axis, dtype=BF16):
    got = lax.all_to_all(parts, axis, split_axis=0, concat_axis=0, tiled=True)
    return jnp.sum(got.astype(F32), axis=0).astype(dtype)


def from_others(mine):
    count = lax.axis_size("dp")
    return [
        lax.ppermute(mine, "dp", [(i, (i + step) % count) for i in range(count)])
        for step in range(1, count)
    ]


def whole(shape):
    return pl.BlockSpec(shape, lambda step: (0,) * len(shape))


def per_group(shape):
    return pl.BlockSpec(shape, lambda step: (step,) + (0,) * (len(shape) - 1))


def grid_call(kernel, ins, in_specs, outs, out_specs, scratch, flops, bytes_moved, exps):
    return pl.pallas_call(
        kernel,
        grid=(HEADS // GROUP,),
        out_shape=[jax.ShapeDtypeStruct(shape, dtype) for shape, dtype in outs],
        in_specs=in_specs,
        out_specs=out_specs,
        scratch_shapes=scratch,
        compiler_params=pltpu.CompilerParams(
            vmem_limit_bytes=56 << 20, dimension_semantics=("arbitrary",)
        ),
        cost_estimate=pl.CostEstimate(
            flops=flops, bytes_accessed=bytes_moved, transcendentals=exps
        ),
    )(*ins)


def body(
    points_feat, neighbours, block_dest, lengths, conv_weight, norm_gain, qkv_weight, proj_weight,
    out_grad,
):
    feats = points_feat[0]
    cotangent = out_grad[0]
    nearby = neighbours[0]
    dest = block_dest[0]
    channels = feats.shape[1]
    scenes = lax.axis_size(SCENE)
    here = jnp.stack([lax.axis_index(SCENE).astype(jnp.int32), lengths[0, 0]])
    gain = norm_gain[:, None]
    rows_c = (PATCH, channels)
    square = (channels, channels)
    slots = (scenes, BLOCK, channels)

    low, high = halo(feats[:HALO], feats[PATCH - HALO :], SCENE)
    gathered, hidden, packed_hidden = call(
        conv_kernel,
        [((TAPS - 1,) + rows_c, BF16), (rows_c, BF16), (slots, BF16)],
        [dest, here, low, feats, high, nearby, conv_weight],
        smem=2, flops=2 * PATCH * channels * (TAPS * channels + 9 * HALO), moved=8 << 20,
        scratch=[pltpu.VMEM((PATCH + 2 * HALO, channels), BF16)],
    )
    got_hidden = moved(packed_hidden)
    cot_after, _ = lax.optimization_barrier((cotangent, hidden))
    (packed_cot,) = call(pack_kernel, [(slots, BF16)], [dest, here, cot_after], smem=2, moved=1 << 21)
    got_cot = moved(packed_cot)
    turned = nearby.T
    targets_low, targets_high = halo(turned[:, :HALO], turned[:, PATCH - HALO :], SCENE)
    at_scene = here[0]
    targets = jnp.concatenate(
        [
            jnp.where(at_scene > 0, targets_low - HALO - PATCH, -1 << 20),
            turned - HALO,
            jnp.where(at_scene < scenes - 1, targets_high - HALO + PATCH, -1 << 20),
        ],
        axis=1,
    )
    probs_shape = (HEADS, PATCH, PATCH)
    recip_shape = (HEADS, 1, PATCH)
    smem = pl.BlockSpec(memory_space=pltpu.SMEM)
    pair = HEADS * PATCH * PATCH
    packed_att, probs, recip, qkv, normed, xhat, inverse, heads = grid_call(
        forward_kernel,
        [dest, here, got_hidden, gain, qkv_weight.T, proj_weight],
        [smem, smem, whole(slots), whole((channels, 1)), whole((3 * channels, channels)),
         whole(square)],
        [(slots, BF16), (probs_shape, BF16), (recip_shape, F32), ((3 * channels, PATCH), BF16),
         ((channels, PATCH), BF16), ((channels, PATCH), F32), ((1, PATCH), F32),
         ((channels, PATCH), BF16)],
        [whole(slots), per_group((GROUP, PATCH, PATCH)), per_group((GROUP, 1, PATCH)),
         whole((3 * channels, PATCH)), whole((channels, PATCH)), whole((channels, PATCH)),
         whole((1, PATCH)), whole((channels, PATCH))],
        [pltpu.VMEM(rows_c, F32), pltpu.VMEM(rows_c, BF16)],
        flops=2 * pair * 64 * 8, bytes_moved=32 << 20, exps=pair,
    )
    got_att = moved(packed_att)
    chips = scenes // 2
    shard = channels // scenes
    parts_shape = (4, chips, shard, channels)
    packed_dz, sent, kept = grid_call(
        backward_kernel,
        [dest, here, got_cot, probs, recip, qkv, normed, xhat, inverse, heads, gain, qkv_weight,
         proj_weight],
        [smem, smem, whole(slots), per_group((GROUP, PATCH, PATCH)), per_group((GROUP, 1, PATCH)),
         whole((3 * channels, PATCH)), whole((channels, PATCH)), whole((channels, PATCH)),
         whole((1, PATCH)), whole((channels, PATCH)), whole((channels, 1)),
         whole((channels, 3 * channels)), whole(square)],
        [(slots, BF16), (parts_shape, BF16), (parts_shape, BF16)],
        [whole(slots), whole(parts_shape), whole(parts_shape)],
        [pltpu.VMEM((3 * channels, PATCH), BF16), pltpu.VMEM(rows_c, BF16),
         pltpu.VMEM((channels, PATCH), BF16), pltpu.VMEM(square, BF16)],
        flops=4 * pair * 64 * 8, bytes_moved=32 << 20, exps=0,
    )
    got_dz = moved(packed_dz)
    d_hidden, d_hidden_b = call(
        hidden_grad_kernel, [(rows_c, F32), (rows_c, BF16)], [dest, here, got_dz, cotangent],
        smem=2, moved=4 << 20,
    )
    d_low, d_high = halo(d_hidden_b[:HALO], d_hidden_b[PATCH - HALO :], SCENE)
    conv_shape = (chips, TAPS, shard, channels)
    conv_sent, conv_kept = call(
        conv_grad_kernel, [(conv_shape, BF16), (conv_shape, BF16)],
        [here, feats, gathered, d_hidden_b],
        smem=1, flops=2 * TAPS * PATCH * channels * channels, moved=6 << 20,
        scratch=[pltpu.VMEM(square, BF16)],
    )
    conv_mine = summed(over_cores(conv_sent, conv_kept), ("x", "z"))
    feat_grad, block_out = call(
        feat_grad_kernel, [(rows_c, BF16), (rows_c, BF16)],
        [dest, here, d_low, d_hidden_b, d_high, targets, conv_weight, d_hidden, hidden, got_att],
        smem=2, flops=2 * PATCH * channels * (TAPS * channels + 9 * HALO), moved=8 << 20,
        scratch=[pltpu.VMEM((PATCH + 2 * HALO, channels), BF16)],
    )
    conv_grad = conv_mine.astype(F32)
    for other in from_others(conv_mine):
        conv_grad = conv_grad + other.astype(F32)
    mine = summed(summed(over_cores(sent, kept), "dp"), ("x", "z"))
    arrived = jnp.stack([mine] + from_others(mine))
    rank = lax.axis_index("dp")
    thirds = jnp.take(arrived, (rank - jnp.arange(4) + 4) % 4, axis=0).astype(F32)
    qkv_grad = jnp.concatenate([thirds[0], thirds[1], thirds[2]], axis=1)
    proj_grad = thirds[3]
    return (block_out[None], feat_grad[None], conv_grad, qkv_grad, proj_grad)


def solution(mesh):
    fine = Mesh(mesh.devices.reshape(4, 4, 2, 4), ("x", "z", "core", "dp"))
    return jax.shard_map(
        body,
        mesh=fine,
        in_specs=(
            P("dp", SCENE, None),
            P("dp", SCENE, None),
            P("dp", None),
            P("dp", SCENE),
            P(),
            P(),
            P(),
            P(),
            P("dp", SCENE, None),
        ),
        out_specs=(
            P("dp", SCENE, None),
            P("dp", SCENE, None),
            P(None, SCENE, None),
            P(SCENE, None),
            P(SCENE, None),
        ),
        check_vma=False,
    )
```

```python
import jax
import jax.numpy as jnp
from jax import lax
from jax.experimental import pallas as pl
from jax.experimental.pallas import tpu as pltpu
from jax.sharding import Mesh
from jax.sharding import PartitionSpec as P

HEADS = 32
HEAD = 16
PATCH = 512
BLOCK = 32
BLOCKS = 16
HALO = 128
TAPS = 4
GROUP = 4
EPS = 1e-05
F32 = jnp.float32
BF16 = jnp.bfloat16
SCENE = ("x", "z", "core")


def dot(left, right, left_dim=1, right_dim=0):
    return lax.dot_general(
        left, right, (((left_dim,), (right_dim,)), ((), ())), preferred_element_type=F32
    )


def call(kernel, outs, operands, smem=0, flops=0, moved=0, transcendentals=0, scratch=()):
    memory = [pltpu.SMEM] * smem + [pltpu.VMEM] * (len(operands) - smem)
    return pl.pallas_call(
        kernel,
        out_shape=[jax.ShapeDtypeStruct(shape, dtype) for shape, dtype in outs],
        in_specs=[pl.BlockSpec(memory_space=space) for space in memory],
        out_specs=[pl.BlockSpec(memory_space=pltpu.VMEM) for _ in outs],
        scratch_shapes=list(scratch),
        compiler_params=pltpu.CompilerParams(vmem_limit_bytes=48 << 20),
        cost_estimate=pl.CostEstimate(
            flops=flops, bytes_accessed=moved, transcendentals=transcendentals
        ),
    )(*operands)


def target_of(dest, me, block):
    return dest[me * BLOCKS + block] // BLOCKS


def source_of(dest, me, block, scenes):
    shift = dest[block] // BLOCKS
    source = lax.rem(me - shift + scenes, scenes)
    return source, lax.rem(dest[source * BLOCKS + block], BLOCKS)


def split_parts(here, part, halves):
    core = lax.rem(here[0], 2)
    shard = part.shape[0] // halves[0].shape[0] // 2
    for pair in range(halves[0].shape[0]):
        for half, owner in zip(halves, (1 - core, core)):
            start = pl.multiple_of((2 * pair + owner) * shard, shard)
            half[pair] = part[pl.ds(start, shard), :]


def pack_kernel(
    dest, here, blocks, feats, inner, outer, qkv_weight, packed, gathered_t, qkv_weight_t
):
    packed[...] = jnp.zeros_like(packed)
    for block in range(BLOCKS):
        packed[target_of(dest, here[0], block)] = blocks[pl.ds(block * BLOCK, BLOCK), :]
    gathered_t[0] = feats[...].T
    for tap in range(TAPS - 1):
        for part in range(PATCH // HALO):
            kept, first = (inner, 1) if part in (1, 2) else (outer, 0)
            place = (part - first) * HALO if first else (part // 3) * HALO
            gathered_t[tap + 1, :, pl.ds(part * HALO, HALO)] = kept[tap, pl.ds(place, HALO), :].T
    qkv_weight_t[...] = qkv_weight[...].T


def conv_rows(part, own, window, index, weight, gathered, place):
    spots = lax.broadcasted_iota(jnp.int32, (HALO, 3 * HALO), 1)
    total = own.astype(F32) + dot(own, weight[0])
    for tap in range(1, TAPS):
        chosen = jnp.where(spots == index[:, tap : tap + 1] - part * HALO, 1.0, 0.0).astype(BF16)
        picked = dot(chosen, window).astype(BF16)
        gathered[tap - 1, place, :] = picked
        total = total + dot(picked, weight[tap])
    return total.astype(BF16)


def inner_kernel(feats, nearby, weight, gathered, hidden):
    for part in (1, 2):
        rows = pl.ds(part * HALO, HALO)
        place = pl.ds((part - 1) * HALO, HALO)
        window = feats[pl.ds((part - 1) * HALO, 3 * HALO), :]
        hidden[place, :] = conv_rows(
            part, feats[rows, :], window, nearby[rows, :], weight, gathered, place
        )


def outer_kernel(
    dest, here, low, feats, high, nearby, weight, inner_hidden, gathered, hidden, packed
):
    packed[...] = jnp.zeros_like(packed)
    hidden[pl.ds(HALO, 2 * HALO), :] = inner_hidden[...]
    for part in (0, 3):
        rows = pl.ds(part * HALO, HALO)
        if part == 0:
            window = jnp.concatenate([low[...], feats[0 : 2 * HALO, :]], axis=0)
        else:
            window = jnp.concatenate([feats[PATCH - 2 * HALO :, :], high[...]], axis=0)
        hidden[rows, :] = conv_rows(
            part, feats[rows, :], window, nearby[rows, :], weight, gathered,
            pl.ds((part // 3) * HALO, HALO),
        )
    for block in range(BLOCKS):
        packed[target_of(dest, here[0], block)] = hidden[pl.ds(block * BLOCK, BLOCK), :]


def forward_kernel(
    dest, here, got, gain, qkv_weight_t, proj_weight,
    packed, probs, recip, qkv, normed, xhat, inverse, heads,
    rows_f, attended,
):
    step = pl.program_id(0)
    scenes = got.shape[0]
    length = here[1]

    @pl.when(step == 0)
    def _():
        for block in range(BLOCKS):
            source, slot = source_of(dest, here[0], block, scenes)
            rows = pl.ds(pl.multiple_of(slot * BLOCK, BLOCK), BLOCK)
            rows_f[rows, :] = got[source].astype(F32)
        rows_t = rows_f[...].T
        centred = rows_t - jnp.mean(rows_t, axis=0, keepdims=True)
        scale = lax.rsqrt(jnp.mean(centred * centred, axis=0, keepdims=True) + EPS)
        standard = centred * scale
        inverse[...] = scale
        xhat[...] = standard
        normed[...] = (standard * gain[...]).astype(BF16)
        qkv[...] = dot(qkv_weight_t[...], normed[...]).astype(BF16)

    sub = lax.broadcasted_iota(jnp.int32, (HEAD, PATCH), 0)
    spot = lax.broadcasted_iota(jnp.int32, (HEAD, PATCH), 1)
    dead = jnp.where((sub == 0) & (spot >= length), -1e30, 0.0).astype(BF16)
    ones = jnp.where(sub == 0, 1.0, 0.0).astype(BF16)
    live = lax.broadcasted_iota(jnp.int32, (1, PATCH), 1) < length
    channels = HEADS * HEAD
    for one in range(GROUP):
        row = pl.multiple_of((step * GROUP + one) * HEAD, HEAD)
        query = (qkv[pl.ds(row, HEAD), :].astype(F32) * HEAD ** (-0.5)).astype(BF16)
        key = qkv[pl.ds(channels + row, HEAD), :]
        value = qkv[pl.ds(2 * channels + row, HEAD), :]
        scores = dot(
            jnp.concatenate([key, dead], axis=0), jnp.concatenate([query, ones], axis=0), 0, 0
        )
        raised = jnp.exp(scores - jnp.max(scores, axis=0, keepdims=True)).astype(BF16)
        probs[one] = raised
        out = dot(jnp.concatenate([value, ones], axis=0), raised)
        over = 1.0 / out[HEAD : HEAD + 1]
        recip[one] = over
        heads[pl.ds(row, HEAD), :] = jnp.where(live, out[:HEAD] * over, 0.0).astype(BF16)

    @pl.when(step == pl.num_programs(0) - 1)
    def _():
        packed[...] = jnp.zeros_like(packed)
        attended[...] = dot(heads[...], proj_weight[...], 0, 0).astype(BF16)
        for block in range(BLOCKS):
            source, slot = source_of(dest, here[0], block, scenes)
            rows = pl.ds(pl.multiple_of(slot * BLOCK, BLOCK), BLOCK)
            packed[source] = attended[rows, :]


def backward_kernel(
    dest, here, got_cot, probs, recip, qkv, normed, xhat, inverse, heads, gain, qkv_weight,
    proj_weight,
    packed, sent, kept,
    d_qkv, d_rows, d_heads, part,
):
    step = pl.program_id(0)
    scenes = packed.shape[0]
    channels = HEADS * HEAD

    @pl.when(step == 0)
    def _():
        for block in range(BLOCKS):
            source, slot = source_of(dest, here[0], block, scenes)
            rows = pl.ds(pl.multiple_of(slot * BLOCK, BLOCK), BLOCK)
            d_rows[rows, :] = got_cot[source]
        live = lax.broadcasted_iota(jnp.int32, (1, PATCH), 1) < here[1]
        d_full = dot(proj_weight[...], d_rows[...], 1, 1)
        d_heads[...] = jnp.where(live, d_full, 0.0).astype(BF16)
        part[...] = dot(heads[...], d_rows[...]).astype(BF16)
        split_parts(here, part, [sent.at[3], kept.at[3]])

    sub = lax.broadcasted_iota(jnp.int32, (HEAD, PATCH), 0)
    ones = jnp.where(sub < 3, 1.0, 0.0).astype(BF16)
    for one in range(GROUP):
        row = pl.multiple_of((step * GROUP + one) * HEAD, HEAD)
        query = qkv[pl.ds(row, HEAD), :].astype(F32)
        key = qkv[pl.ds(channels + row, HEAD), :]
        value = qkv[pl.ds(2 * channels + row, HEAD), :]
        over = recip[one]
        d_out = d_heads[pl.ds(row, HEAD), :]
        d_out_f = d_out.astype(F32)
        row_dot = jnp.sum(
            d_out_f * heads[pl.ds(row, HEAD), :].astype(F32), axis=0, keepdims=True
        )
        first = row_dot.astype(BF16).astype(F32)
        second = (row_dot - first).astype(BF16).astype(F32)
        third = row_dot - first - second
        minus = -jnp.where(sub == 0, first, jnp.where(sub == 1, second, jnp.where(sub == 2, third, 0.0)))
        raised = probs[one]
        d_value = dot((d_out_f * over).astype(BF16), raised, 1, 1)
        d_probs = dot(
            jnp.concatenate([value, ones], axis=0),
            jnp.concatenate([d_out, minus.astype(BF16)], axis=0), 0, 0,
        )
        d_scores = (raised.astype(F32) * d_probs).astype(BF16)
        scaled = over * HEAD ** (-0.5)
        d_query = dot(key, d_scores) * scaled
        d_key = dot((query * scaled).astype(BF16), d_scores, 1, 1)
        d_qkv[pl.ds(row, HEAD), :] = d_query.astype(BF16)
        d_qkv[pl.ds(channels + row, HEAD), :] = d_key.astype(BF16)
        d_qkv[pl.ds(2 * channels + row, HEAD), :] = d_value.astype(BF16)

    @pl.when(step == pl.num_programs(0) - 1)
    def _():
        spread = dot(qkv_weight[...], d_qkv[...]) * gain[...]
        standard = xhat[...]
        row_gradient = inverse[...] * (
            spread
            - jnp.mean(spread, axis=0, keepdims=True)
            - standard * jnp.mean(spread * standard, axis=0, keepdims=True)
        )
        d_rows[...] = row_gradient.T.astype(BF16)
        packed[...] = jnp.zeros_like(packed)
        for block in range(BLOCKS):
            source, slot = source_of(dest, here[0], block, scenes)
            packed[source] = d_rows[pl.ds(pl.multiple_of(slot * BLOCK, BLOCK), BLOCK), :]
        for third in range(3):
            columns = d_qkv[pl.ds(third * channels, channels), :]
            part[...] = dot(normed[...], columns, 1, 1).astype(BF16)
            split_parts(here, part, [sent.at[third], kept.at[third]])


def hidden_grad_kernel(dest, here, got, cot, d_hidden, d_hidden_b):
    for block in range(BLOCKS):
        rows = pl.ds(block * BLOCK, BLOCK)
        total = cot[rows, :].astype(F32) + got[target_of(dest, here[0], block)].astype(F32)
        d_hidden[rows, :] = total
        d_hidden_b[rows, :] = total.astype(BF16)


def conv_grad_kernel(here, gathered_t, d_hidden_b, sent, kept, part):
    for tap in range(TAPS):
        part[...] = dot(gathered_t[tap], d_hidden_b[...]).astype(BF16)
        split_parts(here, part, [sent.at[:, tap], kept.at[:, tap]])


def feat_grad_kernel(
    dest, here, low, d_hidden_b, high, targets, weight, d_hidden, hidden, got,
    feat_grad, block_out, near,
):
    near[0:HALO, :] = low[...]
    near[HALO : HALO + PATCH, :] = d_hidden_b[...]
    near[HALO + PATCH :, :] = high[...]
    spots = lax.broadcasted_iota(jnp.int32, (HALO, 3 * HALO), 0)
    for part in range(PATCH // HALO):
        rows = pl.ds(part * HALO, HALO)
        around = pl.ds(part * HALO, 3 * HALO)
        window = near[around, :]
        total = d_hidden[rows, :] + dot(d_hidden_b[rows, :], weight[0], 1, 1)
        for tap in range(1, TAPS):
            index = targets[pl.ds(tap, 1), around] - part * HALO
            chosen = jnp.where(spots == index, 1.0, 0.0).astype(BF16)
            total = total + dot(dot(chosen, window).astype(BF16), weight[tap], 1, 1)
        feat_grad[rows, :] = total.astype(BF16)
    for block in range(BLOCKS):
        rows = pl.ds(block * BLOCK, BLOCK)
        block_out[rows, :] = (
            hidden[rows, :].astype(F32) + got[target_of(dest, here[0], block)].astype(F32)
        ).astype(BF16)


def halo(first, last, axis):
    count = lax.axis_size(axis)
    forward = [(i, i + 1) for i in range(count - 1)]
    backward = [(i + 1, i) for i in range(count - 1)]
    return lax.ppermute(last, axis, forward), lax.ppermute(first, axis, backward)


def moved(packed):
    return lax.all_to_all(packed, SCENE, split_axis=0, concat_axis=0, tiled=True)


def over_cores(sent, kept):
    other = lax.ppermute(sent, "core", [(0, 1), (1, 0)])
    return (kept.astype(F32) + other.astype(F32)).astype(BF16)


def summed(parts, axis, dtype=BF16):
    got = lax.all_to_all(parts, axis, split_axis=0, concat_axis=0, tiled=True)
    return jnp.sum(got.astype(F32), axis=0).astype(dtype)


def across_tiles(parts):
    count = lax.axis_size("dp")
    rank = lax.axis_index("dp")
    total = lax.dynamic_index_in_dim(parts, rank, 0, keepdims=False).astype(F32)
    for step in range(1, count):
        part = lax.dynamic_index_in_dim(parts, (rank + step) % count, 0, keepdims=False)
        path = [(i, (i + step) % count) for i in range(count)]
        total = total + lax.ppermute(part, "dp", path).astype(F32)
    return total.astype(BF16)


def from_others(mine):
    count = lax.axis_size("dp")
    return [
        lax.ppermute(mine, "dp", [(i, (i + step) % count) for i in range(count)])
        for step in range(1, count)
    ]


def whole(shape):
    return pl.BlockSpec(shape, lambda step: (0,) * len(shape))


def per_group(shape):
    return pl.BlockSpec(shape, lambda step: (step,) + (0,) * (len(shape) - 1))


def grid_call(kernel, ins, in_specs, outs, out_specs, scratch, flops, bytes_moved, exps):
    return pl.pallas_call(
        kernel,
        grid=(HEADS // GROUP,),
        out_shape=[jax.ShapeDtypeStruct(shape, dtype) for shape, dtype in outs],
        in_specs=in_specs,
        out_specs=out_specs,
        scratch_shapes=scratch,
        compiler_params=pltpu.CompilerParams(
            vmem_limit_bytes=56 << 20, dimension_semantics=("arbitrary",)
        ),
        cost_estimate=pl.CostEstimate(
            flops=flops, bytes_accessed=bytes_moved, transcendentals=exps
        ),
    )(*ins)


def body(
    points_feat, neighbours, block_dest, lengths, conv_weight, norm_gain, qkv_weight, proj_weight,
    out_grad,
):
    feats = points_feat[0]
    cotangent = out_grad[0]
    nearby = neighbours[0]
    dest = block_dest[0]
    channels = feats.shape[1]
    scenes = lax.axis_size(SCENE)
    here = jnp.stack([lax.axis_index(SCENE).astype(jnp.int32), lengths[0, 0]])
    gain = norm_gain[:, None]
    rows_c = (PATCH, channels)
    square = (channels, channels)
    slots = (scenes, BLOCK, channels)

    low, high = halo(feats[:HALO], feats[PATCH - HALO :], SCENE)
    half = (2 * HALO, channels)
    work = PATCH * channels * (TAPS * channels + 9 * HALO)
    inner, inner_hidden = call(
        inner_kernel, [((TAPS - 1,) + half, BF16), (half, BF16)], [feats, nearby, conv_weight],
        flops=work, moved=4 << 20,
    )
    outer, hidden, packed_hidden = call(
        outer_kernel,
        [((TAPS - 1,) + half, BF16), (rows_c, BF16), (slots, BF16)],
        [dest, here, low, feats, high, nearby, conv_weight, inner_hidden],
        smem=2, flops=work, moved=5 << 20,
    )
    got_hidden = moved(packed_hidden)
    packed_cot, gathered_t, qkv_weight_t = call(
        pack_kernel,
        [(slots, BF16), ((TAPS,) + square, BF16), ((3 * channels, channels), BF16)],
        [dest, here, cotangent, feats, inner, outer, qkv_weight], smem=2, moved=8 << 20,
    )
    got_cot = moved(packed_cot)
    turned = nearby.T
    targets_low, targets_high = halo(turned[:, :HALO], turned[:, PATCH - HALO :], SCENE)
    at_scene = here[0]
    targets = jnp.concatenate(
        [
            jnp.where(at_scene > 0, targets_low - HALO - PATCH, -1 << 20),
            turned - HALO,
            jnp.where(at_scene < scenes - 1, targets_high - HALO + PATCH, -1 << 20),
        ],
        axis=1,
    )
    probs_shape = (HEADS, PATCH, PATCH)
    recip_shape = (HEADS, 1, PATCH)
    smem = pl.BlockSpec(memory_space=pltpu.SMEM)
    pair = HEADS * PATCH * PATCH
    packed_att, probs, recip, qkv, normed, xhat, inverse, heads = grid_call(
        forward_kernel,
        [dest, here, got_hidden, gain, qkv_weight_t, proj_weight],
        [smem, smem, whole(slots), whole((channels, 1)), whole((3 * channels, channels)),
         whole(square)],
        [(slots, BF16), (probs_shape, BF16), (recip_shape, F32), ((3 * channels, PATCH), BF16),
         ((channels, PATCH), BF16), ((channels, PATCH), F32), ((1, PATCH), F32),
         ((channels, PATCH), BF16)],
        [whole(slots), per_group((GROUP, PATCH, PATCH)), per_group((GROUP, 1, PATCH)),
         whole((3 * channels, PATCH)), whole((channels, PATCH)), whole((channels, PATCH)),
         whole((1, PATCH)), whole((channels, PATCH))],
        [pltpu.VMEM(rows_c, F32), pltpu.VMEM(rows_c, BF16)],
        flops=2 * pair * 64 * 8, bytes_moved=32 << 20, exps=pair,
    )
    got_att = moved(packed_att)
    chips = scenes // 2
    shard = channels // scenes
    parts_shape = (4, chips, shard, channels)
    packed_dz, sent, kept = grid_call(
        backward_kernel,
        [dest, here, got_cot, probs, recip, qkv, normed, xhat, inverse, heads, gain, qkv_weight,
         proj_weight],
        [smem, smem, whole(slots), per_group((GROUP, PATCH, PATCH)), per_group((GROUP, 1, PATCH)),
         whole((3 * channels, PATCH)), whole((channels, PATCH)), whole((channels, PATCH)),
         whole((1, PATCH)), whole((channels, PATCH)), whole((channels, 1)),
         whole((channels, 3 * channels)), whole(square)],
        [(slots, BF16), (parts_shape, BF16), (parts_shape, BF16)],
        [whole(slots), whole(parts_shape), whole(parts_shape)],
        [pltpu.VMEM((3 * channels, PATCH), BF16), pltpu.VMEM(rows_c, BF16),
         pltpu.VMEM((channels, PATCH), BF16), pltpu.VMEM(square, BF16)],
        flops=4 * pair * 64 * 8, bytes_moved=32 << 20, exps=0,
    )
    packed_dz, got_att = lax.optimization_barrier((packed_dz, got_att))
    got_dz = moved(packed_dz)
    mine = across_tiles(over_cores(sent, kept))
    d_hidden, d_hidden_b = call(
        hidden_grad_kernel, [(rows_c, F32), (rows_c, BF16)], [dest, here, got_dz, cotangent],
        smem=2, moved=4 << 20,
    )
    d_low, d_high = halo(d_hidden_b[:HALO], d_hidden_b[PATCH - HALO :], SCENE)
    conv_shape = (chips, TAPS, shard, channels)
    conv_sent, conv_kept = call(
        conv_grad_kernel, [(conv_shape, BF16), (conv_shape, BF16)],
        [here, gathered_t, d_hidden_b],
        smem=1, flops=2 * TAPS * PATCH * channels * channels, moved=6 << 20,
        scratch=[pltpu.VMEM(square, BF16)],
    )
    conv_rows_here = TAPS * shard
    conv_mine = over_cores(conv_sent, conv_kept).reshape(chips, conv_rows_here, channels)
    total = summed(jnp.concatenate([conv_mine, mine], axis=1), ("x", "z"))
    feat_grad, block_out = call(
        feat_grad_kernel, [(rows_c, BF16), (rows_c, BF16)],
        [dest, here, d_low, d_hidden_b, d_high, targets, conv_weight, d_hidden, hidden, got_att],
        smem=2, flops=2 * PATCH * channels * (TAPS * channels + 9 * HALO), moved=8 << 20,
        scratch=[pltpu.VMEM((PATCH + 2 * HALO, channels), BF16)],
    )
    total, feat_grad, block_out = lax.optimization_barrier((total, feat_grad, block_out))
    arrived = [total] + from_others(total)
    conv_grad = sum(one[:conv_rows_here].astype(F32) for one in arrived)
    conv_grad = conv_grad.reshape(TAPS, shard, channels)
    rank = lax.axis_index("dp")
    thirds = jnp.stack([one[conv_rows_here:] for one in arrived])
    thirds = jnp.take(thirds, (rank - jnp.arange(4) + 4) % 4, axis=0).astype(F32)
    qkv_grad = jnp.concatenate([thirds[0], thirds[1], thirds[2]], axis=1)
    proj_grad = thirds[3]
    return (block_out[None], feat_grad[None], conv_grad, qkv_grad, proj_grad)


def solution(mesh):
    fine = Mesh(mesh.devices.reshape(4, 4, 2, 4), ("x", "z", "core", "dp"))
    return jax.shard_map(
        body,
        mesh=fine,
        in_specs=(
            P("dp", SCENE, None),
            P("dp", SCENE, None),
            P("dp", None),
            P("dp", SCENE),
            P(),
            P(),
            P(),
            P(),
            P("dp", SCENE, None),
        ),
        out_specs=(
            P("dp", SCENE, None),
            P("dp", SCENE, None),
            P(None, SCENE, None),
            P(SCENE, None),
            P(SCENE, None),
        ),
        check_vma=False,
    )
```

```python
import jax
import jax.numpy as jnp
from jax import lax
from jax.experimental import pallas as pl
from jax.experimental.pallas import tpu as pltpu
from jax.sharding import Mesh
from jax.sharding import PartitionSpec as P

HEADS = 32
HEAD = 16
PATCH = 512
BLOCK = 32
BLOCKS = 16
HALO = 128
TAPS = 4
GROUP = 4
EPS = 1e-05
F32 = jnp.float32
BF16 = jnp.bfloat16
SCENE = ("x", "z", "core")


def dot(left, right, left_dim=1, right_dim=0):
    return lax.dot_general(
        left, right, (((left_dim,), (right_dim,)), ((), ())), preferred_element_type=F32
    )


VMEM_LIMIT = 60 << 20


def whole(shape):
    return pl.BlockSpec(shape, lambda step: (0,) * len(shape))


def per_group(shape):
    return pl.BlockSpec(shape, lambda step: (step,) + (0,) * (len(shape) - 1))


def call(kernel, outs, operands, smem=0, flops=0, moved=0, scratch=()):
    in_specs = [pl.BlockSpec(memory_space=pltpu.SMEM)] * smem
    in_specs += [whole(operand.shape) for operand in operands[smem:]]
    return pl.pallas_call(
        kernel,
        grid=(1,),
        out_shape=[jax.ShapeDtypeStruct(shape, dtype) for shape, dtype in outs],
        in_specs=in_specs,
        out_specs=[whole(shape) for shape, _ in outs],
        scratch_shapes=list(scratch),
        compiler_params=pltpu.CompilerParams(
            vmem_limit_bytes=VMEM_LIMIT, dimension_semantics=("arbitrary",)
        ),
        cost_estimate=pl.CostEstimate(flops=flops, bytes_accessed=moved, transcendentals=0),
    )(*operands)


def target_of(dest, me, block):
    return dest[me * BLOCKS + block] // BLOCKS


def source_of(dest, me, block, scenes):
    shift = dest[block] // BLOCKS
    source = lax.rem(me - shift + scenes, scenes)
    return source, lax.rem(dest[source * BLOCKS + block], BLOCKS)


def split_parts(here, part, halves):
    core = lax.rem(here[0], 2)
    shard = part.shape[0] // halves[0].shape[0] // 2
    for pair in range(halves[0].shape[0]):
        for half, owner in zip(halves, (1 - core, core)):
            start = pl.multiple_of((2 * pair + owner) * shard, shard)
            half[pair] = part[pl.ds(start, shard), :]


def pack_kernel(
    dest, here, blocks, feats, inner, outer, qkv_weight, packed, gathered_t, qkv_weight_t
):
    packed[...] = jnp.zeros_like(packed)
    for block in range(BLOCKS):
        packed[target_of(dest, here[0], block)] = blocks[pl.ds(block * BLOCK, BLOCK), :]
    gathered_t[0] = feats[...].T
    for tap in range(TAPS - 1):
        for part in range(PATCH // HALO):
            kept, first = (inner, 1) if part in (1, 2) else (outer, 0)
            place = (part - first) * HALO if first else (part // 3) * HALO
            gathered_t[tap + 1, :, pl.ds(part * HALO, HALO)] = kept[tap, pl.ds(place, HALO), :].T
    qkv_weight_t[...] = qkv_weight[...].T


def conv_rows(part, own, window, index, weight, gathered, place):
    spots = lax.broadcasted_iota(jnp.int32, (HALO, 3 * HALO), 1)
    total = own.astype(F32) + dot(own, weight[0])
    for tap in range(1, TAPS):
        chosen = jnp.where(spots == index[:, tap : tap + 1] - part * HALO, 1.0, 0.0).astype(BF16)
        picked = dot(chosen, window).astype(BF16)
        gathered[tap - 1, place, :] = picked
        total = total + dot(picked, weight[tap])
    return total.astype(BF16)


def inner_kernel(feats, nearby, weight, gathered, hidden):
    for part in (1, 2):
        rows = pl.ds(part * HALO, HALO)
        place = pl.ds((part - 1) * HALO, HALO)
        window = feats[pl.ds((part - 1) * HALO, 3 * HALO), :]
        hidden[place, :] = conv_rows(
            part, feats[rows, :], window, nearby[rows, :], weight, gathered, place
        )


def outer_kernel(
    dest, here, low, feats, high, nearby, weight, inner_hidden, gathered, hidden, packed
):
    packed[...] = jnp.zeros_like(packed)
    hidden[pl.ds(HALO, 2 * HALO), :] = inner_hidden[...]
    for part in (0, 3):
        rows = pl.ds(part * HALO, HALO)
        if part == 0:
            window = jnp.concatenate([low[...], feats[0 : 2 * HALO, :]], axis=0)
        else:
            window = jnp.concatenate([feats[PATCH - 2 * HALO :, :], high[...]], axis=0)
        hidden[rows, :] = conv_rows(
            part, feats[rows, :], window, nearby[rows, :], weight, gathered,
            pl.ds((part // 3) * HALO, HALO),
        )
    for block in range(BLOCKS):
        packed[target_of(dest, here[0], block)] = hidden[pl.ds(block * BLOCK, BLOCK), :]


def forward_kernel(
    dest, here, got, gain, qkv_weight_t, proj_weight,
    packed, probs, recip, qkv, normed, xhat, inverse, heads,
    rows_f, attended,
):
    step = pl.program_id(0)
    scenes = got.shape[0]
    length = here[1]

    @pl.when(step == 0)
    def _():
        for block in range(BLOCKS):
            source, slot = source_of(dest, here[0], block, scenes)
            rows = pl.ds(pl.multiple_of(slot * BLOCK, BLOCK), BLOCK)
            rows_f[rows, :] = got[source].astype(F32)
        rows_t = rows_f[...].T
        centred = rows_t - jnp.mean(rows_t, axis=0, keepdims=True)
        scale = lax.rsqrt(jnp.mean(centred * centred, axis=0, keepdims=True) + EPS)
        standard = centred * scale
        inverse[...] = scale
        xhat[...] = standard
        normed[...] = (standard * gain[...]).astype(BF16)
        qkv[...] = dot(qkv_weight_t[...], normed[...]).astype(BF16)

    sub = lax.broadcasted_iota(jnp.int32, (HEAD, PATCH), 0)
    spot = lax.broadcasted_iota(jnp.int32, (HEAD, PATCH), 1)
    dead = jnp.where((sub == 0) & (spot >= length), -1e30, 0.0).astype(BF16)
    ones = jnp.where(sub == 0, 1.0, 0.0).astype(BF16)
    live = lax.broadcasted_iota(jnp.int32, (1, PATCH), 1) < length
    channels = HEADS * HEAD
    for one in range(GROUP):
        row = pl.multiple_of((step * GROUP + one) * HEAD, HEAD)
        query = (qkv[pl.ds(row, HEAD), :].astype(F32) * HEAD ** (-0.5)).astype(BF16)
        key = qkv[pl.ds(channels + row, HEAD), :]
        value = qkv[pl.ds(2 * channels + row, HEAD), :]
        scores = dot(
            jnp.concatenate([key, dead], axis=0), jnp.concatenate([query, ones], axis=0), 0, 0
        )
        raised = jnp.exp(scores - jnp.max(scores, axis=0, keepdims=True)).astype(BF16)
        probs[one] = raised
        out = dot(jnp.concatenate([value, ones], axis=0), raised)
        over = 1.0 / out[HEAD : HEAD + 1]
        recip[one] = over
        heads[pl.ds(row, HEAD), :] = jnp.where(live, out[:HEAD] * over, 0.0).astype(BF16)

    @pl.when(step == pl.num_programs(0) - 1)
    def _():
        packed[...] = jnp.zeros_like(packed)
        attended[...] = dot(heads[...], proj_weight[...], 0, 0).astype(BF16)
        for block in range(BLOCKS):
            source, slot = source_of(dest, here[0], block, scenes)
            rows = pl.ds(pl.multiple_of(slot * BLOCK, BLOCK), BLOCK)
            packed[source] = attended[rows, :]


def backward_kernel(
    dest, here, got_cot, probs, recip, qkv, normed, xhat, inverse, heads, gain, qkv_weight,
    proj_weight,
    packed, sent, kept,
    d_qkv, d_rows, d_heads, part,
):
    step = pl.program_id(0)
    scenes = packed.shape[0]
    channels = HEADS * HEAD

    @pl.when(step == 0)
    def _():
        for block in range(BLOCKS):
            source, slot = source_of(dest, here[0], block, scenes)
            rows = pl.ds(pl.multiple_of(slot * BLOCK, BLOCK), BLOCK)
            d_rows[rows, :] = got_cot[source]
        live = lax.broadcasted_iota(jnp.int32, (1, PATCH), 1) < here[1]
        d_full = dot(proj_weight[...], d_rows[...], 1, 1)
        d_heads[...] = jnp.where(live, d_full, 0.0).astype(BF16)
        part[...] = dot(heads[...], d_rows[...]).astype(BF16)
        split_parts(here, part, [sent.at[3], kept.at[3]])

    sub = lax.broadcasted_iota(jnp.int32, (HEAD, PATCH), 0)
    ones = jnp.where(sub < 3, 1.0, 0.0).astype(BF16)
    for one in range(GROUP):
        row = pl.multiple_of((step * GROUP + one) * HEAD, HEAD)
        query = qkv[pl.ds(row, HEAD), :].astype(F32)
        key = qkv[pl.ds(channels + row, HEAD), :]
        value = qkv[pl.ds(2 * channels + row, HEAD), :]
        over = recip[one]
        d_out = d_heads[pl.ds(row, HEAD), :]
        d_out_f = d_out.astype(F32)
        row_dot = jnp.sum(
            d_out_f * heads[pl.ds(row, HEAD), :].astype(F32), axis=0, keepdims=True
        )
        first = row_dot.astype(BF16).astype(F32)
        second = (row_dot - first).astype(BF16).astype(F32)
        third = row_dot - first - second
        minus = -jnp.where(sub == 0, first, jnp.where(sub == 1, second, jnp.where(sub == 2, third, 0.0)))
        raised = probs[one]
        d_value = dot((d_out_f * over).astype(BF16), raised, 1, 1)
        d_probs = dot(
            jnp.concatenate([value, ones], axis=0),
            jnp.concatenate([d_out, minus.astype(BF16)], axis=0), 0, 0,
        )
        d_scores = (raised.astype(F32) * d_probs).astype(BF16)
        scaled = over * HEAD ** (-0.5)
        d_query = dot(key, d_scores) * scaled
        d_key = dot((query * scaled).astype(BF16), d_scores, 1, 1)
        d_qkv[pl.ds(row, HEAD), :] = d_query.astype(BF16)
        d_qkv[pl.ds(channels + row, HEAD), :] = d_key.astype(BF16)
        d_qkv[pl.ds(2 * channels + row, HEAD), :] = d_value.astype(BF16)

    @pl.when(step == pl.num_programs(0) - 1)
    def _():
        spread = dot(qkv_weight[...], d_qkv[...]) * gain[...]
        standard = xhat[...]
        row_gradient = inverse[...] * (
            spread
            - jnp.mean(spread, axis=0, keepdims=True)
            - standard * jnp.mean(spread * standard, axis=0, keepdims=True)
        )
        d_rows[...] = row_gradient.T.astype(BF16)
        packed[...] = jnp.zeros_like(packed)
        for block in range(BLOCKS):
            source, slot = source_of(dest, here[0], block, scenes)
            packed[source] = d_rows[pl.ds(pl.multiple_of(slot * BLOCK, BLOCK), BLOCK), :]
        for third in range(3):
            columns = d_qkv[pl.ds(third * channels, channels), :]
            part[...] = dot(normed[...], columns, 1, 1).astype(BF16)
            split_parts(here, part, [sent.at[third], kept.at[third]])


def conv_grad_kernel(
    dest, here, got, cot, gathered_t, d_hidden, d_hidden_b, sent, kept, part
):
    @pl.when(pl.program_id(0) == 0)
    def _():
        for block in range(BLOCKS):
            rows = pl.ds(block * BLOCK, BLOCK)
            total = cot[rows, :].astype(F32) + got[target_of(dest, here[0], block)].astype(F32)
            d_hidden[rows, :] = total
            d_hidden_b[rows, :] = total.astype(BF16)

    part[...] = dot(gathered_t[0], d_hidden_b[...]).astype(BF16)
    split_parts(here, part, [sent.at[:, 0], kept.at[:, 0]])


def feat_grad_kernel(
    dest, here, low, d_hidden_b, high, targets, weight, d_hidden, hidden, got,
    feat_grad, block_out, near,
):
    near[0:HALO, :] = low[...]
    near[HALO : HALO + PATCH, :] = d_hidden_b[...]
    near[HALO + PATCH :, :] = high[...]
    spots = lax.broadcasted_iota(jnp.int32, (HALO, 3 * HALO), 0)
    for part in range(PATCH // HALO):
        rows = pl.ds(part * HALO, HALO)
        around = pl.ds(part * HALO, 3 * HALO)
        window = near[around, :]
        total = d_hidden[rows, :] + dot(d_hidden_b[rows, :], weight[0], 1, 1)
        for tap in range(1, TAPS):
            index = targets[pl.ds(tap, 1), around] - part * HALO
            chosen = jnp.where(spots == index, 1.0, 0.0).astype(BF16)
            total = total + dot(dot(chosen, window).astype(BF16), weight[tap], 1, 1)
        feat_grad[rows, :] = total.astype(BF16)
    for block in range(BLOCKS):
        rows = pl.ds(block * BLOCK, BLOCK)
        block_out[rows, :] = (
            hidden[rows, :].astype(F32) + got[target_of(dest, here[0], block)].astype(F32)
        ).astype(BF16)


def last_kernel(rank, mine, first, second, third, conv_grad, qkv_grad, proj_grad):
    arrived = [mine, first, second, third]
    shard = proj_grad.shape[0]
    channels = proj_grad.shape[1]
    for tap in range(TAPS):
        rows = pl.ds(tap * shard, shard)
        conv_grad[tap] = sum(one[rows, :].astype(F32) for one in arrived)
    for step, one in enumerate(arrived):
        block = one[pl.ds(TAPS * shard, shard), :].astype(F32)
        origin = lax.rem(rank[0] - step + len(arrived), len(arrived))
        for third_at in range(3):
            @pl.when(origin == third_at)
            def _(block=block, third_at=third_at):
                qkv_grad[:, pl.ds(third_at * channels, channels)] = block

        @pl.when(origin == 3)
        def _(block=block):
            proj_grad[...] = block


def halo(first, last, axis):
    count = lax.axis_size(axis)
    forward = [(i, i + 1) for i in range(count - 1)]
    backward = [(i + 1, i) for i in range(count - 1)]
    return lax.ppermute(last, axis, forward), lax.ppermute(first, axis, backward)


def moved(packed):
    return lax.all_to_all(packed, SCENE, split_axis=0, concat_axis=0, tiled=True)


def over_cores(sent, kept):
    other = lax.ppermute(sent, "core", [(0, 1), (1, 0)])
    return (kept.astype(F32) + other.astype(F32)).astype(BF16)


def summed(parts, axis, dtype=BF16):
    got = lax.all_to_all(parts, axis, split_axis=0, concat_axis=0, tiled=True)
    return jnp.sum(got.astype(F32), axis=0).astype(dtype)


def tile_parts(parts):
    count = lax.axis_size("dp")
    rank = lax.axis_index("dp")
    return [
        lax.dynamic_index_in_dim(parts, (rank + step) % count, 0, keepdims=False)
        for step in range(count)
    ]


def across_tiles(parts):
    count = len(parts)
    return [
        lax.ppermute(parts[step], "dp", [(i, (i + step) % count) for i in range(count)])
        for step in range(1, count)
    ]


def from_others(mine):
    count = lax.axis_size("dp")
    return [
        lax.ppermute(mine, "dp", [(i, (i + step) % count) for i in range(count)])
        for step in range(1, count)
    ]


def grid_call(
    kernel, ins, in_specs, outs, out_specs, scratch, flops, bytes_moved, exps,
    steps=HEADS // GROUP,
):
    return pl.pallas_call(
        kernel,
        grid=(steps,),
        out_shape=[jax.ShapeDtypeStruct(shape, dtype) for shape, dtype in outs],
        in_specs=in_specs,
        out_specs=out_specs,
        scratch_shapes=scratch,
        compiler_params=pltpu.CompilerParams(
            vmem_limit_bytes=VMEM_LIMIT, dimension_semantics=("arbitrary",)
        ),
        cost_estimate=pl.CostEstimate(
            flops=flops, bytes_accessed=bytes_moved, transcendentals=exps
        ),
    )(*ins)


def body(
    points_feat, neighbours, block_dest, lengths, conv_weight, norm_gain, qkv_weight, proj_weight,
    out_grad,
):
    feats = points_feat[0]
    cotangent = out_grad[0]
    nearby = neighbours[0]
    dest = block_dest[0]
    channels = feats.shape[1]
    scenes = lax.axis_size(SCENE)
    here = jnp.stack([lax.axis_index(SCENE).astype(jnp.int32), lengths[0, 0]])
    gain = norm_gain[:, None]
    rows_c = (PATCH, channels)
    square = (channels, channels)
    slots = (scenes, BLOCK, channels)

    low, high = halo(feats[:HALO], feats[PATCH - HALO :], SCENE)
    half = (2 * HALO, channels)
    work = PATCH * channels * (TAPS * channels + 9 * HALO)
    inner, inner_hidden = call(
        inner_kernel, [((TAPS - 1,) + half, BF16), (half, BF16)], [feats, nearby, conv_weight],
        flops=work, moved=4 << 20,
    )
    outer, hidden, packed_hidden = call(
        outer_kernel,
        [((TAPS - 1,) + half, BF16), (rows_c, BF16), (slots, BF16)],
        [dest, here, low, feats, high, nearby, conv_weight, inner_hidden],
        smem=2, flops=work, moved=5 << 20,
    )
    got_hidden = moved(packed_hidden)
    packed_cot, gathered_t, qkv_weight_t = call(
        pack_kernel,
        [(slots, BF16), ((TAPS,) + square, BF16), ((3 * channels, channels), BF16)],
        [dest, here, cotangent, feats, inner, outer, qkv_weight], smem=2, moved=8 << 20,
    )
    got_cot = moved(packed_cot)
    late_nearby, _ = lax.optimization_barrier((nearby, hidden))
    turned = late_nearby.T
    targets_low, targets_high = halo(turned[:, :HALO], turned[:, PATCH - HALO :], SCENE)
    at_scene = here[0]
    targets = jnp.concatenate(
        [
            jnp.where(at_scene > 0, targets_low - HALO - PATCH, -1 << 20),
            turned - HALO,
            jnp.where(at_scene < scenes - 1, targets_high - HALO + PATCH, -1 << 20),
        ],
        axis=1,
    )
    probs_shape = (HEADS, PATCH, PATCH)
    recip_shape = (HEADS, 1, PATCH)
    smem = pl.BlockSpec(memory_space=pltpu.SMEM)
    pair = HEADS * PATCH * PATCH
    got_hidden, targets = lax.optimization_barrier((got_hidden, targets))
    packed_att, probs, recip, qkv, normed, xhat, inverse, heads = grid_call(
        forward_kernel,
        [dest, here, got_hidden, gain, qkv_weight_t, proj_weight],
        [smem, smem, whole(slots), whole((channels, 1)), whole((3 * channels, channels)),
         whole(square)],
        [(slots, BF16), (probs_shape, BF16), (recip_shape, F32), ((3 * channels, PATCH), BF16),
         ((channels, PATCH), BF16), ((channels, PATCH), F32), ((1, PATCH), F32),
         ((channels, PATCH), BF16)],
        [whole(slots), per_group((GROUP, PATCH, PATCH)), per_group((GROUP, 1, PATCH)),
         whole((3 * channels, PATCH)), whole((channels, PATCH)), whole((channels, PATCH)),
         whole((1, PATCH)), whole((channels, PATCH))],
        [pltpu.VMEM(rows_c, F32), pltpu.VMEM(rows_c, BF16)],
        flops=2 * pair * 64 * 8, bytes_moved=32 << 20, exps=pair,
    )
    got_att = moved(packed_att)
    chips = scenes // 2
    shard = channels // scenes
    parts_shape = (4, chips, shard, channels)
    packed_dz, sent, kept = grid_call(
        backward_kernel,
        [dest, here, got_cot, probs, recip, qkv, normed, xhat, inverse, heads, gain, qkv_weight,
         proj_weight],
        [smem, smem, whole(slots), per_group((GROUP, PATCH, PATCH)), per_group((GROUP, 1, PATCH)),
         whole((3 * channels, PATCH)), whole((channels, PATCH)), whole((channels, PATCH)),
         whole((1, PATCH)), whole((channels, PATCH)), whole((channels, 1)),
         whole((channels, 3 * channels)), whole(square)],
        [(slots, BF16), (parts_shape, BF16), (parts_shape, BF16)],
        [whole(slots), whole(parts_shape), whole(parts_shape)],
        [pltpu.VMEM((3 * channels, PATCH), BF16), pltpu.VMEM(rows_c, BF16),
         pltpu.VMEM((channels, PATCH), BF16), pltpu.VMEM(square, BF16)],
        flops=4 * pair * 64 * 8, bytes_moved=32 << 20, exps=0,
    )
    packed_dz, got_att = lax.optimization_barrier((packed_dz, got_att))
    got_dz = moved(packed_dz)
    tile_rows = tile_parts(over_cores(sent, kept))
    got_dz, received = lax.optimization_barrier((got_dz, across_tiles(tile_rows)))
    conv_shape = (chips, TAPS, shard, channels)
    by_tap = pl.BlockSpec((chips, 1, shard, channels), lambda step: (0, step, 0, 0))
    d_hidden, d_hidden_b, conv_sent, conv_kept = grid_call(
        conv_grad_kernel,
        [dest, here, got_dz, cotangent, gathered_t],
        [smem, smem, whole(slots), whole(rows_c), per_group((1,) + square)],
        [(rows_c, F32), (rows_c, BF16), (conv_shape, BF16), (conv_shape, BF16)],
        [whole(rows_c), whole(rows_c), by_tap, by_tap],
        [pltpu.VMEM(square, BF16)],
        flops=2 * TAPS * PATCH * channels * channels, bytes_moved=8 << 20, exps=0, steps=TAPS,
    )
    edge_rows, conv_sent = lax.optimization_barrier((d_hidden_b, conv_sent))
    conv_other = lax.ppermute(conv_sent, "core", [(0, 1), (1, 0)])
    d_low, d_high = halo(edge_rows[:HALO], edge_rows[PATCH - HALO :], SCENE)
    received, conv_kept = lax.optimization_barrier((received, conv_kept))
    mine = sum(one.astype(F32) for one in [tile_rows[0]] + received).astype(BF16)
    rows_here = TAPS * shard
    ahead = ((0, 0, 0), (0, shard, 0), (0, 0, 0))
    behind = ((0, 0, 0), (rows_here, 0, 0), (0, 0, 0))
    zero = jnp.zeros((), BF16)
    chip_parts = sum(
        lax.pad(one.reshape(chips, -1, channels), zero, where).astype(F32)
        for one, where in ((conv_kept, ahead), (conv_other, ahead), (mine, behind))
    ).astype(BF16)
    chip_parts, d_low, d_high = lax.optimization_barrier((chip_parts, d_low, d_high))
    total = summed(chip_parts, ("x", "z"))
    feat_grad, block_out = call(
        feat_grad_kernel, [(rows_c, BF16), (rows_c, BF16)],
        [dest, here, d_low, d_hidden_b, d_high, targets, conv_weight, d_hidden, hidden, got_att],
        smem=2, flops=2 * PATCH * channels * (TAPS * channels + 9 * HALO), moved=8 << 20,
        scratch=[pltpu.VMEM((PATCH + 2 * HALO, channels), BF16)],
    )
    total, feat_grad, block_out = lax.optimization_barrier((total, feat_grad, block_out))
    rank = lax.axis_index("dp").astype(jnp.int32)
    conv_grad, qkv_grad, proj_grad = call(
        last_kernel,
        [((TAPS, shard, channels), F32), ((shard, 3 * channels), F32), ((shard, channels), F32)],
        [rank[None], total] + from_others(total), smem=1, moved=1 << 20,
    )
    return (block_out[None], feat_grad[None], conv_grad, qkv_grad, proj_grad)


def solution(mesh):
    fine = Mesh(mesh.devices.reshape(4, 4, 2, 4), ("x", "z", "core", "dp"))
    return jax.shard_map(
        body,
        mesh=fine,
        in_specs=(
            P("dp", SCENE, None),
            P("dp", SCENE, None),
            P("dp", None),
            P("dp", SCENE),
            P(),
            P(),
            P(),
            P(),
            P("dp", SCENE, None),
        ),
        out_specs=(
            P("dp", SCENE, None),
            P("dp", SCENE, None),
            P(None, SCENE, None),
            P(SCENE, None),
            P(SCENE, None),
        ),
        check_vma=False,
    )
```

```python
import jax
import jax.numpy as jnp
from jax import lax
from jax.experimental import pallas as pl
from jax.experimental.pallas import tpu as pltpu
from jax.sharding import Mesh
from jax.sharding import PartitionSpec as P

HEADS = 32
HEAD = 16
PATCH = 512
BLOCK = 32
BLOCKS = 16
HALO = 128
TAPS = 4
GROUP = 4
EPS = 1e-05
F32 = jnp.float32
BF16 = jnp.bfloat16
SCENE = ("x", "z", "core")


def dot(left, right, left_dim=1, right_dim=0):
    return lax.dot_general(
        left, right, (((left_dim,), (right_dim,)), ((), ())), preferred_element_type=F32
    )


VMEM_LIMIT = 60 << 20


def whole(shape):
    return pl.BlockSpec(shape, lambda step: (0,) * len(shape))


def per_group(shape):
    return pl.BlockSpec(shape, lambda step: (step,) + (0,) * (len(shape) - 1))


def call(kernel, outs, operands, smem=0, flops=0, moved=0, scratch=()):
    in_specs = [pl.BlockSpec(memory_space=pltpu.SMEM)] * smem
    in_specs += [whole(operand.shape) for operand in operands[smem:]]
    return pl.pallas_call(
        kernel,
        grid=(1,),
        out_shape=[jax.ShapeDtypeStruct(shape, dtype) for shape, dtype in outs],
        in_specs=in_specs,
        out_specs=[whole(shape) for shape, _ in outs],
        scratch_shapes=list(scratch),
        compiler_params=pltpu.CompilerParams(
            vmem_limit_bytes=VMEM_LIMIT, dimension_semantics=("arbitrary",)
        ),
        cost_estimate=pl.CostEstimate(flops=flops, bytes_accessed=moved, transcendentals=0),
    )(*operands)


def target_of(dest, me, block):
    return dest[me * BLOCKS + block] // BLOCKS


def source_of(dest, me, block, scenes):
    shift = dest[block] // BLOCKS
    source = lax.rem(me - shift + scenes, scenes)
    return source, lax.rem(dest[source * BLOCKS + block], BLOCKS)


def split_parts(here, part, halves):
    core = lax.rem(here[0], 2)
    shard = part.shape[0] // halves[0].shape[0] // 2
    for pair in range(halves[0].shape[0]):
        for half, owner in zip(halves, (1 - core, core)):
            start = pl.multiple_of((2 * pair + owner) * shard, shard)
            half[pair] = part[pl.ds(start, shard), :]


def columns_of(index):
    padded = jnp.concatenate([index, jnp.zeros((8 - TAPS, index.shape[1]), F32)], axis=0)
    return padded.T


def picked_rows(part, window, columns, tap):
    spots = lax.broadcasted_iota(jnp.int32, (HALO, 3 * HALO), 1).astype(F32)
    index = columns[part * HALO : (part + 1) * HALO, tap : tap + 1] - part * HALO
    return dot(jnp.where(spots == index, 1.0, 0.0).astype(BF16), window).astype(BF16)


def window_of(part, low, feats, high):
    if part == 0:
        return jnp.concatenate([low[...], feats[0 : 2 * HALO, :]], axis=0)
    if part == PATCH // HALO - 1:
        return jnp.concatenate([feats[PATCH - 2 * HALO :, :], high[...]], axis=0)
    return feats[pl.ds((part - 1) * HALO, 3 * HALO), :]


def conv_rows(part, own, window, columns, weight):
    total = own.astype(F32) + dot(own, weight[0])
    for tap in range(1, TAPS):
        total = total + dot(picked_rows(part, window, columns, tap), weight[tap])
    return total.astype(BF16)


def inner_kernel(feats, nearby, weight, hidden):
    columns = columns_of(nearby[...].astype(F32))
    for part in (1, 2):
        hidden[pl.ds((part - 1) * HALO, HALO), :] = conv_rows(
            part, feats[pl.ds(part * HALO, HALO), :], window_of(part, None, feats, None),
            columns, weight,
        )


def outer_kernel(dest, here, low, feats, high, nearby, weight, inner_hidden, hidden, packed):
    packed[...] = jnp.zeros_like(packed)
    hidden[pl.ds(HALO, 2 * HALO), :] = inner_hidden[...]
    columns = columns_of(nearby[...].astype(F32))
    for part in (0, 3):
        rows = pl.ds(part * HALO, HALO)
        hidden[rows, :] = conv_rows(
            part, feats[rows, :], window_of(part, low, feats, high), columns, weight
        )
    for block in range(BLOCKS):
        packed[target_of(dest, here[0], block)] = hidden[pl.ds(block * BLOCK, BLOCK), :]


def pack_kernel(
    dest, here, blocks, low, feats, high, nearby, qkv_weight, packed, gathered_t, qkv_weight_t
):
    packed[...] = jnp.zeros_like(packed)
    for block in range(BLOCKS):
        packed[target_of(dest, here[0], block)] = blocks[pl.ds(block * BLOCK, BLOCK), :]
    columns = columns_of(nearby[...].astype(F32))
    gathered_t[0] = feats[...].T
    for part in range(PATCH // HALO):
        window = window_of(part, low, feats, high)
        for tap in range(1, TAPS):
            picked = picked_rows(part, window, columns, tap)
            gathered_t[tap, :, pl.ds(part * HALO, HALO)] = picked.T
    qkv_weight_t[...] = qkv_weight[...].T


def forward_kernel(
    dest, here, got, gain, qkv_weight_t, proj_weight,
    packed, probs, recip, qkv, normed, xhat, inverse, heads,
    rows_f, attended,
):
    step = pl.program_id(0)
    scenes = got.shape[0]
    length = here[1]

    @pl.when(step == 0)
    def _():
        for block in range(BLOCKS):
            source, slot = source_of(dest, here[0], block, scenes)
            rows = pl.ds(pl.multiple_of(slot * BLOCK, BLOCK), BLOCK)
            rows_f[rows, :] = got[source].astype(F32)
        rows_t = rows_f[...].T
        centred = rows_t - jnp.mean(rows_t, axis=0, keepdims=True)
        scale = lax.rsqrt(jnp.mean(centred * centred, axis=0, keepdims=True) + EPS)
        standard = centred * scale
        inverse[...] = scale
        xhat[...] = standard
        normed[...] = (standard * gain[...]).astype(BF16)
        qkv[...] = dot(qkv_weight_t[...], normed[...]).astype(BF16)

    sub = lax.broadcasted_iota(jnp.int32, (HEAD, PATCH), 0)
    spot = lax.broadcasted_iota(jnp.int32, (HEAD, PATCH), 1)
    dead = jnp.where((sub == 0) & (spot >= length), -1e30, 0.0).astype(BF16)
    ones = jnp.where(sub == 0, 1.0, 0.0).astype(BF16)
    live = lax.broadcasted_iota(jnp.int32, (1, PATCH), 1) < length
    channels = HEADS * HEAD

    def scores_of(one):
        row = pl.multiple_of((step * GROUP + one) * HEAD, HEAD)
        query = (qkv[pl.ds(row, HEAD), :].astype(F32) * HEAD ** (-0.5)).astype(BF16)
        key = qkv[pl.ds(channels + row, HEAD), :]
        return dot(
            jnp.concatenate([key, dead], axis=0), jnp.concatenate([query, ones], axis=0), 0, 0
        )

    scores = scores_of(0)
    for one in range(GROUP):
        following = scores_of(one + 1) if one + 1 < GROUP else None
        row = pl.multiple_of((step * GROUP + one) * HEAD, HEAD)
        value = qkv[pl.ds(2 * channels + row, HEAD), :]
        raised = jnp.exp(scores - jnp.max(scores, axis=0, keepdims=True)).astype(BF16)
        probs[one] = raised
        out = dot(jnp.concatenate([value, ones], axis=0), raised)
        over = 1.0 / out[HEAD : HEAD + 1]
        recip[one] = over
        heads[pl.ds(row, HEAD), :] = jnp.where(live, out[:HEAD] * over, 0.0).astype(BF16)
        scores = following

    @pl.when(step == pl.num_programs(0) - 1)
    def _():
        packed[...] = jnp.zeros_like(packed)
        attended[...] = dot(heads[...], proj_weight[...], 0, 0).astype(BF16)
        for block in range(BLOCKS):
            source, slot = source_of(dest, here[0], block, scenes)
            rows = pl.ds(pl.multiple_of(slot * BLOCK, BLOCK), BLOCK)
            packed[source] = attended[rows, :]


def backward_kernel(
    dest, here, got_cot, probs, recip, qkv, normed, xhat, inverse, heads, gain, qkv_weight,
    proj_weight,
    packed, sent, kept,
    d_qkv, d_rows, d_heads, part, normed_here, xhat_here, weight_here, arrivals,
):
    step = pl.program_id(0)
    scenes = packed.shape[0]
    channels = HEADS * HEAD

    late = [
        pltpu.make_async_copy(far, near, arrivals.at[at])
        for at, (far, near) in enumerate(
            ((normed, normed_here), (xhat, xhat_here), (qkv_weight, weight_here))
        )
    ]

    @pl.when(step == 0)
    def _():
        for copy in late:
            copy.start()
        for block in range(BLOCKS):
            source, slot = source_of(dest, here[0], block, scenes)
            rows = pl.ds(pl.multiple_of(slot * BLOCK, BLOCK), BLOCK)
            d_rows[rows, :] = got_cot[source]
        live = lax.broadcasted_iota(jnp.int32, (1, PATCH), 1) < here[1]
        d_full = dot(proj_weight[...], d_rows[...], 1, 1)
        d_heads[...] = jnp.where(live, d_full, 0.0).astype(BF16)
        part[...] = dot(heads[...], d_rows[...]).astype(BF16)
        split_parts(here, part, [sent.at[3], kept.at[3]])

    sub = lax.broadcasted_iota(jnp.int32, (HEAD, PATCH), 0)
    ones = jnp.where(sub < 3, 1.0, 0.0).astype(BF16)

    def d_probs_of(one):
        row = pl.multiple_of((step * GROUP + one) * HEAD, HEAD)
        value = qkv[pl.ds(2 * channels + row, HEAD), :]
        d_out = d_heads[pl.ds(row, HEAD), :]
        row_dot = jnp.sum(
            d_out.astype(F32) * heads[pl.ds(row, HEAD), :].astype(F32), axis=0, keepdims=True
        )
        first = row_dot.astype(BF16).astype(F32)
        second = (row_dot - first).astype(BF16).astype(F32)
        third = row_dot - first - second
        split = jnp.where(sub == 0, first, jnp.where(sub == 1, second, third))
        minus = jnp.where(sub < 3, -split, 0.0).astype(BF16)
        return dot(
            jnp.concatenate([value, ones], axis=0), jnp.concatenate([d_out, minus], axis=0), 0, 0
        )

    d_probs = d_probs_of(0)
    for one in range(GROUP):
        following = d_probs_of(one + 1) if one + 1 < GROUP else None
        row = pl.multiple_of((step * GROUP + one) * HEAD, HEAD)
        query = qkv[pl.ds(row, HEAD), :].astype(F32)
        key = qkv[pl.ds(channels + row, HEAD), :]
        over = recip[one]
        raised = probs[one]
        d_scores = (raised.astype(F32) * d_probs).astype(BF16)
        d_out = (d_heads[pl.ds(row, HEAD), :].astype(F32) * over).astype(BF16)
        d_qkv[pl.ds(2 * channels + row, HEAD), :] = dot(d_out, raised, 1, 1).astype(BF16)
        scaled = over * HEAD ** (-0.5)
        d_qkv[pl.ds(row, HEAD), :] = (dot(key, d_scores) * scaled).astype(BF16)
        d_key = dot((query * scaled).astype(BF16), d_scores, 1, 1)
        d_qkv[pl.ds(channels + row, HEAD), :] = d_key.astype(BF16)
        d_probs = following

    @pl.when(step == pl.num_programs(0) - 1)
    def _():
        for copy in late:
            copy.wait()
        spread = dot(weight_here[...], d_qkv[...]) * gain[...]
        standard = xhat_here[...]
        row_gradient = inverse[...] * (
            spread
            - jnp.mean(spread, axis=0, keepdims=True)
            - standard * jnp.mean(spread * standard, axis=0, keepdims=True)
        )
        d_rows[...] = row_gradient.T.astype(BF16)
        packed[...] = jnp.zeros_like(packed)
        for block in range(BLOCKS):
            source, slot = source_of(dest, here[0], block, scenes)
            packed[source] = d_rows[pl.ds(pl.multiple_of(slot * BLOCK, BLOCK), BLOCK), :]
        for third in range(3):
            columns = d_qkv[pl.ds(third * channels, channels), :]
            part[...] = dot(normed_here[...], columns, 1, 1).astype(BF16)
            split_parts(here, part, [sent.at[third], kept.at[third]])


def conv_grad_kernel(
    dest, here, got, cot, gathered_t, d_hidden, d_hidden_b, sent, kept, part
):
    @pl.when(pl.program_id(0) == 0)
    def _():
        for block in range(BLOCKS):
            rows = pl.ds(block * BLOCK, BLOCK)
            total = cot[rows, :].astype(F32) + got[target_of(dest, here[0], block)].astype(F32)
            d_hidden[rows, :] = total
            d_hidden_b[rows, :] = total.astype(BF16)

    part[...] = dot(gathered_t[0], d_hidden_b[...]).astype(BF16)
    split_parts(here, part, [sent.at[:, 0], kept.at[:, 0]])


def feat_grad_kernel(
    dest, here, nearby, d_hidden_b, weight, d_hidden, hidden, got,
    kept, to_previous, to_next, block_out, spread, landed,
):
    spots = lax.broadcasted_iota(jnp.int32, (HALO, 3 * HALO), 0)
    landing = PATCH // HALO + 2
    landed[...] = jnp.zeros_like(landed)
    for tap in range(1, TAPS):
        for part in range(landing):
            start, stop = max(0, part - 2) * HALO, min(PATCH // HALO, part + 1) * HALO
            index = nearby[pl.ds(tap, 1), pl.ds(start, stop - start)] - part * HALO
            chosen = jnp.where(spots[:, : stop - start] == index, 1.0, 0.0).astype(BF16)
            spread[pl.ds(part * HALO, HALO), :] = dot(
                chosen, d_hidden_b[pl.ds(start, stop - start), :]
            ).astype(BF16)
        landed[...] += dot(spread[...], weight[tap], 1, 1)
    to_previous[...] = landed[0:HALO, :].astype(BF16)
    to_next[...] = landed[HALO + PATCH :, :].astype(BF16)
    kept[...] = (
        d_hidden[...] + landed[HALO : HALO + PATCH, :] + dot(d_hidden_b[...], weight[0], 1, 1)
    )
    for block in range(BLOCKS):
        rows = pl.ds(block * BLOCK, BLOCK)
        block_out[rows, :] = (
            hidden[rows, :].astype(F32) + got[target_of(dest, here[0], block)].astype(F32)
        ).astype(BF16)


def last_kernel(
    rank, mine, first, second, third, conv_far, qkv_far, proj_far, conv_grad, qkv_grad, proj_grad,
    sems,
):
    arrived = [mine, first, second, third]
    shard = proj_grad.shape[0]
    channels = proj_grad.shape[1]
    for tap in range(TAPS):
        rows = pl.ds(tap * shard, shard)
        conv_grad[tap] = sum(one[rows, :].astype(F32) for one in arrived)
    copies = [
        pltpu.make_async_copy(near, far, sems.at[at])
        for at, (near, far) in enumerate(
            ((conv_grad, conv_far), (qkv_grad, qkv_far), (proj_grad, proj_far))
        )
    ]
    copies[0].start()
    for step, one in enumerate(arrived):
        block = one[pl.ds(TAPS * shard, shard), :].astype(F32)
        origin = lax.rem(rank[0] - step + len(arrived), len(arrived))
        for third_at in range(3):
            @pl.when(origin == third_at)
            def _(block=block, third_at=third_at):
                qkv_grad[:, pl.ds(third_at * channels, channels)] = block

        @pl.when(origin == 3)
        def _(block=block):
            proj_grad[...] = block
    copies[1].start()
    copies[2].start()
    for copy in copies:
        copy.wait()


def halo(first, last, axis):
    count = lax.axis_size(axis)
    forward = [(i, i + 1) for i in range(count - 1)]
    backward = [(i + 1, i) for i in range(count - 1)]
    return lax.ppermute(last, axis, forward), lax.ppermute(first, axis, backward)


def moved(packed):
    return lax.all_to_all(packed, SCENE, split_axis=0, concat_axis=0, tiled=True)


def over_cores(sent, kept):
    other = lax.ppermute(sent, "core", [(0, 1), (1, 0)])
    return (kept.astype(F32) + other.astype(F32)).astype(BF16)


def summed(parts, axis, dtype=BF16):
    got = lax.all_to_all(parts, axis, split_axis=0, concat_axis=0, tiled=True)
    return jnp.sum(got.astype(F32), axis=0).astype(dtype)


def tile_parts(parts):
    count = lax.axis_size("dp")
    rank = lax.axis_index("dp")
    return [
        lax.dynamic_index_in_dim(parts, (rank + step) % count, 0, keepdims=False)
        for step in range(count)
    ]


def across_tiles(parts):
    count = len(parts)
    return [
        lax.ppermute(parts[step], "dp", [(i, (i + step) % count) for i in range(count)])
        for step in range(1, count)
    ]


def from_others(mine):
    count = lax.axis_size("dp")
    return [
        lax.ppermute(mine, "dp", [(i, (i + step) % count) for i in range(count)])
        for step in range(1, count)
    ]


def grid_call(
    kernel, ins, in_specs, outs, out_specs, scratch, flops, bytes_moved, exps,
    steps=HEADS // GROUP,
):
    return pl.pallas_call(
        kernel,
        grid=(steps,),
        out_shape=[jax.ShapeDtypeStruct(shape, dtype) for shape, dtype in outs],
        in_specs=in_specs,
        out_specs=out_specs,
        scratch_shapes=scratch,
        compiler_params=pltpu.CompilerParams(
            vmem_limit_bytes=VMEM_LIMIT, dimension_semantics=("arbitrary",)
        ),
        cost_estimate=pl.CostEstimate(
            flops=flops, bytes_accessed=bytes_moved, transcendentals=exps
        ),
    )(*ins)


def body(
    points_feat, neighbours, block_dest, lengths, conv_weight, norm_gain, qkv_weight, proj_weight,
    out_grad,
):
    feats = points_feat[0]
    cotangent = out_grad[0]
    nearby = neighbours[0]
    dest = block_dest[0]
    channels = feats.shape[1]
    scenes = lax.axis_size(SCENE)
    here = jnp.stack([lax.axis_index(SCENE).astype(jnp.int32), lengths[0, 0]])
    gain = norm_gain[:, None]
    rows_c = (PATCH, channels)
    square = (channels, channels)
    slots = (scenes, BLOCK, channels)

    low, high = halo(feats[:HALO], feats[PATCH - HALO :], SCENE)
    half = (2 * HALO, channels)
    work = PATCH * channels * (TAPS * channels + 9 * HALO)
    turned = nearby.T
    (inner_hidden,) = call(
        inner_kernel, [(half, BF16)], [feats, turned, conv_weight], flops=work, moved=4 << 20,
    )
    hidden, packed_hidden = call(
        outer_kernel, [(rows_c, BF16), (slots, BF16)],
        [dest, here, low, feats, high, turned, conv_weight, inner_hidden],
        smem=2, flops=work, moved=5 << 20,
    )
    got_hidden = moved(packed_hidden)
    cot_after, _ = lax.optimization_barrier((cotangent, hidden))
    packed_cot, gathered_t, qkv_weight_t = call(
        pack_kernel,
        [(slots, BF16), ((TAPS,) + square, BF16), ((3 * channels, channels), BF16)],
        [dest, here, cot_after, low, feats, high, turned, qkv_weight], smem=2, moved=8 << 20,
    )
    got_cot = moved(packed_cot)
    probs_shape = (HEADS, PATCH, PATCH)
    recip_shape = (HEADS, 1, PATCH)
    smem = pl.BlockSpec(memory_space=pltpu.SMEM)
    far = pl.BlockSpec(memory_space=pl.ANY)
    pair = HEADS * PATCH * PATCH
    packed_att, probs, recip, qkv, normed, xhat, inverse, heads = grid_call(
        forward_kernel,
        [dest, here, got_hidden, gain, qkv_weight_t, proj_weight],
        [smem, smem, whole(slots), whole((channels, 1)), whole((3 * channels, channels)),
         whole(square)],
        [(slots, BF16), (probs_shape, BF16), (recip_shape, F32), ((3 * channels, PATCH), BF16),
         ((channels, PATCH), BF16), ((channels, PATCH), F32), ((1, PATCH), F32),
         ((channels, PATCH), BF16)],
        [whole(slots), per_group((GROUP, PATCH, PATCH)), per_group((GROUP, 1, PATCH)),
         whole((3 * channels, PATCH)), whole((channels, PATCH)), whole((channels, PATCH)),
         whole((1, PATCH)), whole((channels, PATCH))],
        [pltpu.VMEM(rows_c, F32), pltpu.VMEM(rows_c, BF16)],
        flops=2 * pair * 64 * 8, bytes_moved=32 << 20, exps=pair,
    )
    got_att = moved(packed_att)
    chips = scenes // 2
    shard = channels // scenes
    parts_shape = (4, chips, shard, channels)
    packed_dz, sent, kept = grid_call(
        backward_kernel,
        [dest, here, got_cot, probs, recip, qkv, normed, xhat, inverse, heads, gain, qkv_weight,
         proj_weight],
        [smem, smem, whole(slots), per_group((GROUP, PATCH, PATCH)), per_group((GROUP, 1, PATCH)),
         whole((3 * channels, PATCH)), far, far, whole((1, PATCH)), whole((channels, PATCH)),
         whole((channels, 1)), far, whole(square)],
        [(slots, BF16), (parts_shape, BF16), (parts_shape, BF16)],
        [whole(slots), whole(parts_shape), whole(parts_shape)],
        [pltpu.VMEM((3 * channels, PATCH), BF16), pltpu.VMEM(rows_c, BF16),
         pltpu.VMEM((channels, PATCH), BF16), pltpu.VMEM(square, BF16),
         pltpu.VMEM((channels, PATCH), BF16), pltpu.VMEM((channels, PATCH), F32),
         pltpu.VMEM((channels, 3 * channels), BF16), pltpu.SemaphoreType.DMA((3,))],
        flops=4 * pair * 64 * 8, bytes_moved=32 << 20, exps=0,
    )
    packed_dz, got_att = lax.optimization_barrier((packed_dz, got_att))
    got_dz = moved(packed_dz)
    tile_rows = tile_parts(over_cores(sent, kept))
    got_dz, received = lax.optimization_barrier((got_dz, across_tiles(tile_rows)))
    conv_shape = (chips, TAPS, shard, channels)
    by_tap = pl.BlockSpec((chips, 1, shard, channels), lambda step: (0, step, 0, 0))
    d_hidden, d_hidden_b, conv_sent, conv_kept = grid_call(
        conv_grad_kernel,
        [dest, here, got_dz, cotangent, gathered_t],
        [smem, smem, whole(slots), whole(rows_c), per_group((1,) + square)],
        [(rows_c, F32), (rows_c, BF16), (conv_shape, BF16), (conv_shape, BF16)],
        [whole(rows_c), whole(rows_c), by_tap, by_tap],
        [pltpu.VMEM(square, BF16)],
        flops=2 * TAPS * PATCH * channels * channels, bytes_moved=8 << 20, exps=0, steps=TAPS,
    )
    conv_other = lax.ppermute(conv_sent, "core", [(0, 1), (1, 0)])
    received, conv_kept = lax.optimization_barrier((received, conv_kept))
    mine = sum(one.astype(F32) for one in [tile_rows[0]] + received).astype(BF16)
    rows_here = TAPS * shard
    ahead = ((0, 0, 0), (0, shard, 0), (0, 0, 0))
    behind = ((0, 0, 0), (rows_here, 0, 0), (0, 0, 0))
    zero = jnp.zeros((), BF16)
    chip_parts = sum(
        lax.pad(one.reshape(chips, -1, channels), zero, where).astype(F32)
        for one, where in ((conv_kept, ahead), (conv_other, ahead), (mine, behind))
    ).astype(BF16)
    total = summed(chip_parts, ("x", "z"))
    edge = (HALO, channels)
    feat_kept, to_previous, to_next, block_out = call(
        feat_grad_kernel, [(rows_c, F32), (edge, BF16), (edge, BF16), (rows_c, BF16)],
        [dest, here, turned, d_hidden_b, conv_weight, d_hidden, hidden, got_att],
        smem=2, flops=3 * work, moved=8 << 20,
        scratch=[
            pltpu.VMEM((PATCH + 2 * HALO, channels), BF16),
            pltpu.VMEM((PATCH + 2 * HALO, channels), F32),
        ],
    )
    from_previous, from_next = halo(to_previous, to_next, SCENE)
    total, feat_kept, block_out = lax.optimization_barrier((total, feat_kept, block_out))
    arrived = from_others(total)
    zero = jnp.zeros((), BF16)
    top = lax.pad(from_previous, zero, ((0, PATCH - HALO, 0), (0, 0, 0)))
    bottom = lax.pad(from_next, zero, ((PATCH - HALO, 0, 0), (0, 0, 0)))
    feat_grad = (feat_kept + top.astype(F32) + bottom.astype(F32)).astype(BF16)
    rank = lax.axis_index("dp").astype(jnp.int32)
    near = pl.BlockSpec(memory_space=pltpu.VMEM)
    grads = [(TAPS, shard, channels), (shard, 3 * channels), (shard, channels)]
    conv_grad, qkv_grad, proj_grad = pl.pallas_call(
        last_kernel,
        out_shape=[jax.ShapeDtypeStruct(shape, F32) for shape in grads],
        in_specs=[smem] + [near] * 4,
        out_specs=[far] * 3,
        scratch_shapes=[pltpu.VMEM(shape, F32) for shape in grads]
        + [pltpu.SemaphoreType.DMA((3,))],
        compiler_params=pltpu.CompilerParams(vmem_limit_bytes=VMEM_LIMIT),
        cost_estimate=pl.CostEstimate(flops=1 << 20, bytes_accessed=1 << 20, transcendentals=0),
    )(rank[None], total, *arrived)
    return (block_out[None], feat_grad[None], conv_grad, qkv_grad, proj_grad)


def solution(mesh):
    fine = Mesh(mesh.devices.reshape(4, 4, 2, 4), ("x", "z", "core", "dp"))
    return jax.shard_map(
        body,
        mesh=fine,
        in_specs=(
            P("dp", SCENE, None),
            P("dp", SCENE, None),
            P("dp", None),
            P("dp", SCENE),
            P(),
            P(),
            P(),
            P(),
            P("dp", SCENE, None),
        ),
        out_specs=(
            P("dp", SCENE, None),
            P("dp", SCENE, None),
            P(None, SCENE, None),
            P(SCENE, None),
            P(SCENE, None),
        ),
        check_vma=False,
    )
```

```python
import jax
import jax.numpy as jnp
from jax import lax
from jax.experimental import pallas as pl
from jax.experimental.pallas import tpu as pltpu
from jax.sharding import Mesh
from jax.sharding import PartitionSpec as P

HEADS = 32
HEAD = 16
PATCH = 512
BLOCK = 32
BLOCKS = 16
HALO = 128
TAPS = 4
GROUP = 4
EPS = 1e-05
F32 = jnp.float32
BF16 = jnp.bfloat16
SCENE = ("x", "z", "core")


def dot(left, right, left_dim=1, right_dim=0):
    return lax.dot_general(
        left, right, (((left_dim,), (right_dim,)), ((), ())), preferred_element_type=F32
    )


VMEM_LIMIT = 60 << 20


def whole(shape):
    return pl.BlockSpec(shape, lambda step: (0,) * len(shape))


def per_group(shape):
    return pl.BlockSpec(shape, lambda step: (step,) + (0,) * (len(shape) - 1))


def call(kernel, outs, operands, smem=0, flops=0, moved=0, scratch=(), limit=VMEM_LIMIT):
    in_specs = [pl.BlockSpec(memory_space=pltpu.SMEM)] * smem
    in_specs += [whole(operand.shape) for operand in operands[smem:]]
    return pl.pallas_call(
        kernel,
        grid=(1,),
        out_shape=[jax.ShapeDtypeStruct(shape, dtype) for shape, dtype in outs],
        in_specs=in_specs,
        out_specs=[whole(shape) for shape, _ in outs],
        scratch_shapes=list(scratch),
        compiler_params=pltpu.CompilerParams(
            vmem_limit_bytes=limit, dimension_semantics=("arbitrary",)
        ),
        cost_estimate=pl.CostEstimate(flops=flops, bytes_accessed=moved, transcendentals=0),
    )(*operands)


def scene_index():
    index = lax.axis_index(SCENE[0])
    for axis in SCENE[1:]:
        index = index * lax.axis_size(axis) + lax.axis_index(axis)
    return index


def target_of(dest, block):
    return dest[scene_index() * BLOCKS + block] // BLOCKS


def source_of(dest, block, scenes):
    shift = dest[block] // BLOCKS
    source = lax.rem(scene_index() - shift + scenes, scenes)
    return source, lax.rem(dest[source * BLOCKS + block], BLOCKS)


def split_parts(part, halves):
    core = lax.axis_index("core")
    shard = part.shape[0] // halves[0].shape[0] // 2
    for pair in range(halves[0].shape[0]):
        for half, owner in zip(halves, (1 - core, core)):
            start = pl.multiple_of((2 * pair + owner) * shard, shard)
            half[pair] = part[pl.ds(start, shard), :]


def column_of(row):
    return jnp.broadcast_to(row[...], (8, row.shape[1])).T[:, 0:1]


def columns_of(index):
    padded = jnp.concatenate([index, jnp.zeros((8 - TAPS, index.shape[1]), F32)], axis=0)
    return padded.T


def picked_rows(part, window, columns, tap):
    spots = lax.broadcasted_iota(jnp.int32, (HALO, 3 * HALO), 1).astype(F32)
    index = columns[part * HALO : (part + 1) * HALO, tap : tap + 1] - part * HALO
    return dot(jnp.where(spots == index, 1.0, 0.0).astype(BF16), window).astype(BF16)


def window_of(part, low, feats, high):
    if part == 0:
        return jnp.concatenate([low[...], feats[0 : 2 * HALO, :]], axis=0)
    if part == PATCH // HALO - 1:
        return jnp.concatenate([feats[PATCH - 2 * HALO :, :], high[...]], axis=0)
    return feats[pl.ds((part - 1) * HALO, 3 * HALO), :]


def conv_rows(part, own, window, columns, weight):
    total = own.astype(F32) + dot(own, weight[0])
    for tap in range(1, TAPS):
        total = total + dot(picked_rows(part, window, columns, tap), weight[tap])
    return total.astype(BF16)


def inner_kernel(feats, nearby, weight, hidden):
    columns = columns_of(nearby[...].astype(F32))
    for part in (1, 2):
        hidden[pl.ds((part - 1) * HALO, HALO), :] = conv_rows(
            part, feats[pl.ds(part * HALO, HALO), :], window_of(part, None, feats, None),
            columns, weight,
        )


def outer_kernel(dest, low, feats, high, nearby, weight, inner_hidden, hidden, packed):
    packed[...] = jnp.zeros_like(packed)
    hidden[pl.ds(HALO, 2 * HALO), :] = inner_hidden[...]
    columns = columns_of(nearby[...].astype(F32))
    for part in (0, 3):
        rows = pl.ds(part * HALO, HALO)
        hidden[rows, :] = conv_rows(
            part, feats[rows, :], window_of(part, low, feats, high), columns, weight
        )
    for block in range(BLOCKS):
        packed[target_of(dest, block)] = hidden[pl.ds(block * BLOCK, BLOCK), :]


def pack_kernel(
    dest, blocks, low, feats, high, nearby, qkv_weight, packed, gathered_t, qkv_weight_t
):
    packed[...] = jnp.zeros_like(packed)
    for block in range(BLOCKS):
        packed[target_of(dest, block)] = blocks[pl.ds(block * BLOCK, BLOCK), :]
    columns = columns_of(nearby[...].astype(F32))
    gathered_t[0] = feats[...].T
    for part in range(PATCH // HALO):
        window = window_of(part, low, feats, high)
        for tap in range(1, TAPS):
            picked = picked_rows(part, window, columns, tap)
            gathered_t[tap, :, pl.ds(part * HALO, HALO)] = picked.T
    qkv_weight_t[...] = qkv_weight[...].T


def forward_kernel(
    dest, lengths, got, gain, weight_far, proj_far,
    packed, probs, recip, qkv_far, normed_far, xhat_far, inverse, heads,
    rows_f, attended, qkv_weight_t, proj_weight, qkv, normed, xhat, arrivals, departures,
):
    step = pl.program_id(0)
    arriving = [
        pltpu.make_async_copy(far, near, arrivals.at[at])
        for at, (far, near) in enumerate(((weight_far, qkv_weight_t), (proj_far, proj_weight)))
    ]
    leaving = [
        pltpu.make_async_copy(near, far, departures.at[at])
        for at, (near, far) in enumerate(
            ((xhat, xhat_far), (normed, normed_far), (qkv, qkv_far))
        )
    ]
    scenes = got.shape[0]
    length = lengths[0, 0]

    @pl.when(step == 0)
    def _():
        for copy in arriving:
            copy.start()
        for block in range(BLOCKS):
            source, slot = source_of(dest, block, scenes)
            rows = pl.ds(pl.multiple_of(slot * BLOCK, BLOCK), BLOCK)
            rows_f[rows, :] = got[source].astype(F32)
        rows_t = rows_f[...].T
        centred = rows_t - jnp.mean(rows_t, axis=0, keepdims=True)
        scale = lax.rsqrt(jnp.mean(centred * centred, axis=0, keepdims=True) + EPS)
        standard = centred * scale
        inverse[...] = scale
        xhat[...] = standard
        normed[...] = (standard * column_of(gain)).astype(BF16)
        leaving[0].start()
        leaving[1].start()
        arriving[0].wait()
        qkv[...] = dot(qkv_weight_t[...], normed[...]).astype(BF16)
        leaving[2].start()

    sub = lax.broadcasted_iota(jnp.int32, (HEAD, PATCH), 0)
    spot = lax.broadcasted_iota(jnp.int32, (HEAD, PATCH), 1)
    dead = jnp.where((sub == 0) & (spot >= length), -1e30, 0.0).astype(BF16)
    ones = jnp.where(sub == 0, 1.0, 0.0).astype(BF16)
    live = lax.broadcasted_iota(jnp.int32, (1, PATCH), 1) < length
    channels = HEADS * HEAD

    def scores_of(one):
        row = pl.multiple_of((step * GROUP + one) * HEAD, HEAD)
        query = (qkv[pl.ds(row, HEAD), :].astype(F32) * HEAD ** (-0.5)).astype(BF16)
        key = qkv[pl.ds(channels + row, HEAD), :]
        return dot(
            jnp.concatenate([key, dead], axis=0), jnp.concatenate([query, ones], axis=0), 0, 0
        )

    scores = scores_of(0)
    for one in range(GROUP):
        following = scores_of(one + 1) if one + 1 < GROUP else None
        row = pl.multiple_of((step * GROUP + one) * HEAD, HEAD)
        value = qkv[pl.ds(2 * channels + row, HEAD), :]
        raised = jnp.exp(scores - jnp.max(scores, axis=0, keepdims=True)).astype(BF16)
        probs[one] = raised
        out = dot(jnp.concatenate([value, ones], axis=0), raised)
        over = 1.0 / out[HEAD : HEAD + 1]
        recip[one] = over
        heads[pl.ds(row, HEAD), :] = jnp.where(live, out[:HEAD] * over, 0.0).astype(BF16)
        scores = following

    @pl.when(step == pl.num_programs(0) - 1)
    def _():
        packed[...] = jnp.zeros_like(packed)
        arriving[1].wait()
        attended[...] = dot(heads[...], proj_weight[...], 0, 0).astype(BF16)
        for block in range(BLOCKS):
            source, slot = source_of(dest, block, scenes)
            rows = pl.ds(pl.multiple_of(slot * BLOCK, BLOCK), BLOCK)
            packed[source] = attended[rows, :]
        for copy in leaving:
            copy.wait()


def backward_kernel(
    dest, lengths, got_cot, probs, recip, qkv_far, normed, xhat, inverse, heads, gain,
    qkv_weight, proj_weight,
    packed_far, sent_far, kept_far,
    d_qkv, d_rows, d_heads, part, normed_here, xhat_here, weight_here, qkv, packed, sent, kept,
    arrivals, departures,
):
    step = pl.program_id(0)
    scenes = packed.shape[0]
    leaving = [
        pltpu.make_async_copy(near.at[at], far.at[at], departures.at[at, half])
        for at in range(sent.shape[0])
        for half, (near, far) in enumerate(((sent, sent_far), (kept, kept_far)))
    ]
    leaving.append(pltpu.make_async_copy(packed, packed_far, departures.at[sent.shape[0], 0]))
    channels = HEADS * HEAD

    late = [
        pltpu.make_async_copy(far, near, arrivals.at[at])
        for at, (far, near) in enumerate(
            (
                (qkv_far, qkv), (normed, normed_here), (xhat, xhat_here),
                (qkv_weight, weight_here),
            )
        )
    ]

    @pl.when(step == 0)
    def _():
        late[0].start()
        for block in range(BLOCKS):
            source, slot = source_of(dest, block, scenes)
            rows = pl.ds(pl.multiple_of(slot * BLOCK, BLOCK), BLOCK)
            d_rows[rows, :] = got_cot[source]
        live = lax.broadcasted_iota(jnp.int32, (1, PATCH), 1) < lengths[0, 0]
        d_full = dot(proj_weight[...], d_rows[...], 1, 1)
        d_heads[...] = jnp.where(live, d_full, 0.0).astype(BF16)
        part[...] = dot(heads[...], d_rows[...]).astype(BF16)
        split_parts(part, [sent.at[3], kept.at[3]])
        leaving[6].start()
        leaving[7].start()
        late[0].wait()
        for copy in late[1:]:
            copy.start()

    sub = lax.broadcasted_iota(jnp.int32, (HEAD, PATCH), 0)
    ones = jnp.where(sub < 3, 1.0, 0.0).astype(BF16)

    def d_probs_of(one):
        row = pl.multiple_of((step * GROUP + one) * HEAD, HEAD)
        value = qkv[pl.ds(2 * channels + row, HEAD), :]
        d_out = d_heads[pl.ds(row, HEAD), :]
        row_dot = jnp.sum(
            d_out.astype(F32) * heads[pl.ds(row, HEAD), :].astype(F32), axis=0, keepdims=True
        )
        first = row_dot.astype(BF16).astype(F32)
        second = (row_dot - first).astype(BF16).astype(F32)
        third = row_dot - first - second
        split = jnp.where(sub == 0, first, jnp.where(sub == 1, second, third))
        minus = jnp.where(sub < 3, -split, 0.0).astype(BF16)
        return dot(
            jnp.concatenate([value, ones], axis=0), jnp.concatenate([d_out, minus], axis=0), 0, 0
        )

    d_probs = d_probs_of(0)
    for one in range(GROUP):
        following = d_probs_of(one + 1) if one + 1 < GROUP else None
        row = pl.multiple_of((step * GROUP + one) * HEAD, HEAD)
        query = qkv[pl.ds(row, HEAD), :].astype(F32)
        key = qkv[pl.ds(channels + row, HEAD), :]
        over = recip[one]
        raised = probs[one]
        d_scores = (raised.astype(F32) * d_probs).astype(BF16)
        d_out = (d_heads[pl.ds(row, HEAD), :].astype(F32) * over).astype(BF16)
        d_qkv[pl.ds(2 * channels + row, HEAD), :] = dot(d_out, raised, 1, 1).astype(BF16)
        scaled = over * HEAD ** (-0.5)
        d_qkv[pl.ds(row, HEAD), :] = (dot(key, d_scores) * scaled).astype(BF16)
        d_key = dot((query * scaled).astype(BF16), d_scores, 1, 1)
        d_qkv[pl.ds(channels + row, HEAD), :] = d_key.astype(BF16)
        d_probs = following

    @pl.when(step == pl.num_programs(0) - 1)
    def _():
        for copy in late[1:]:
            copy.wait()
        spread = dot(weight_here[...], d_qkv[...]) * column_of(gain)
        standard = xhat_here[...]
        row_gradient = inverse[...] * (
            spread
            - jnp.mean(spread, axis=0, keepdims=True)
            - standard * jnp.mean(spread * standard, axis=0, keepdims=True)
        )
        d_rows[...] = row_gradient.T.astype(BF16)
        packed[...] = jnp.zeros_like(packed)
        for block in range(BLOCKS):
            source, slot = source_of(dest, block, scenes)
            packed[source] = d_rows[pl.ds(pl.multiple_of(slot * BLOCK, BLOCK), BLOCK), :]
        leaving[8].start()
        for third in range(3):
            columns = d_qkv[pl.ds(third * channels, channels), :]
            part[...] = dot(normed_here[...], columns, 1, 1).astype(BF16)
            split_parts(part, [sent.at[third], kept.at[third]])
            leaving[2 * third].start()
            leaving[2 * third + 1].start()
        for copy in leaving:
            copy.wait()


def conv_grad_kernel(
    dest, got, cot, gathered_t, d_hidden_b, sent, kept, part
):
    @pl.when(pl.program_id(0) == 0)
    def _():
        for block in range(BLOCKS):
            rows = pl.ds(block * BLOCK, BLOCK)
            total = cot[rows, :].astype(F32) + got[target_of(dest, block)].astype(F32)
            d_hidden_b[rows, :] = total.astype(BF16)

    part[...] = dot(gathered_t[0], d_hidden_b[...]).astype(BF16)
    split_parts(part, [sent.at[:, 0], kept.at[:, 0]])


def feat_grad_kernel(
    dest, nearby, d_hidden_b, weight, cot, got_dz, hidden, got,
    kept, to_previous, to_next, block_out, spread, landed,
):
    spots = lax.broadcasted_iota(jnp.int32, (HALO, 3 * HALO), 0)
    landing = PATCH // HALO + 2
    landed[...] = jnp.zeros_like(landed)
    for tap in range(1, TAPS):
        for part in range(landing):
            start, stop = max(0, part - 2) * HALO, min(PATCH // HALO, part + 1) * HALO
            index = nearby[pl.ds(tap, 1), pl.ds(start, stop - start)] - part * HALO
            chosen = jnp.where(spots[:, : stop - start] == index, 1.0, 0.0).astype(BF16)
            spread[pl.ds(part * HALO, HALO), :] = dot(
                chosen, d_hidden_b[pl.ds(start, stop - start), :]
            ).astype(BF16)
        landed[...] += dot(spread[...], weight[tap], 1, 1)
    to_previous[...] = landed[0:HALO, :].astype(BF16)
    to_next[...] = landed[HALO + PATCH :, :].astype(BF16)
    landed[HALO : HALO + PATCH, :] += dot(d_hidden_b[...], weight[0], 1, 1)
    for block in range(BLOCKS):
        rows = pl.ds(block * BLOCK, BLOCK)
        d_hidden = cot[rows, :].astype(F32) + got_dz[target_of(dest, block)].astype(F32)
        kept[rows, :] = d_hidden + landed[pl.ds(HALO + block * BLOCK, BLOCK), :]
        block_out[rows, :] = (
            hidden[rows, :].astype(F32) + got[target_of(dest, block)].astype(F32)
        ).astype(BF16)


def last_kernel(
    rank, mine, first, second, third, conv_far, qkv_far, proj_far, conv_grad, qkv_grad, proj_grad,
    sems,
):
    arrived = [mine, first, second, third]
    shard = proj_grad.shape[0]
    channels = proj_grad.shape[1]
    for tap in range(TAPS):
        rows = pl.ds(tap * shard, shard)
        conv_grad[tap] = sum(one[rows, :].astype(F32) for one in arrived)
    copies = [
        pltpu.make_async_copy(near, far, sems.at[at])
        for at, (near, far) in enumerate(
            ((conv_grad, conv_far), (qkv_grad, qkv_far), (proj_grad, proj_far))
        )
    ]
    copies[0].start()
    for step, one in enumerate(arrived):
        block = one[pl.ds(TAPS * shard, shard), :].astype(F32)
        origin = lax.rem(rank[0] - step + len(arrived), len(arrived))
        for third_at in range(3):
            @pl.when(origin == third_at)
            def _(block=block, third_at=third_at):
                qkv_grad[:, pl.ds(third_at * channels, channels)] = block

        @pl.when(origin == 3)
        def _(block=block):
            proj_grad[...] = block
    copies[1].start()
    copies[2].start()
    for copy in copies:
        copy.wait()


def halo(first, last, axis):
    count = lax.axis_size(axis)
    forward = [(i, i + 1) for i in range(count - 1)]
    backward = [(i + 1, i) for i in range(count - 1)]
    return lax.ppermute(last, axis, forward), lax.ppermute(first, axis, backward)


def moved(packed):
    return lax.all_to_all(packed, SCENE, split_axis=0, concat_axis=0, tiled=True)


def over_cores(sent, kept):
    other = lax.ppermute(sent, "core", [(0, 1), (1, 0)])
    return (kept.astype(F32) + other.astype(F32)).astype(BF16)


def summed(parts, axis, dtype=BF16):
    got = lax.all_to_all(parts, axis, split_axis=0, concat_axis=0, tiled=True)
    return jnp.sum(got.astype(F32), axis=0).astype(dtype)


def tile_parts(parts):
    count = lax.axis_size("dp")
    rank = lax.axis_index("dp")
    return [
        lax.dynamic_index_in_dim(parts, (rank + step) % count, 0, keepdims=False)
        for step in range(count)
    ]


def across_tiles(parts):
    count = len(parts)
    return [
        lax.ppermute(parts[step], "dp", [(i, (i + step) % count) for i in range(count)])
        for step in range(1, count)
    ]


def from_others(mine):
    count = lax.axis_size("dp")
    return [
        lax.ppermute(mine, "dp", [(i, (i + step) % count) for i in range(count)])
        for step in range(1, count)
    ]


def grid_call(
    kernel, ins, in_specs, outs, out_specs, scratch, flops, bytes_moved, exps,
    steps=HEADS // GROUP,
):
    return pl.pallas_call(
        kernel,
        grid=(steps,),
        out_shape=[jax.ShapeDtypeStruct(shape, dtype) for shape, dtype in outs],
        in_specs=in_specs,
        out_specs=out_specs,
        scratch_shapes=scratch,
        compiler_params=pltpu.CompilerParams(
            vmem_limit_bytes=VMEM_LIMIT, dimension_semantics=("arbitrary",)
        ),
        cost_estimate=pl.CostEstimate(
            flops=flops, bytes_accessed=bytes_moved, transcendentals=exps
        ),
    )(*ins)


def body(
    points_feat, neighbours, block_dest, lengths, conv_weight, norm_gain, qkv_weight, proj_weight,
    out_grad,
):
    feats = points_feat[0]
    cotangent = out_grad[0]
    nearby = neighbours[0]
    dest = block_dest[0]
    channels = feats.shape[1]
    scenes = lax.axis_size(SCENE)
    gain = norm_gain[None, :]
    rows_c = (PATCH, channels)
    square = (channels, channels)
    slots = (scenes, BLOCK, channels)

    low, high = halo(feats[:HALO], feats[PATCH - HALO :], SCENE)
    half = (2 * HALO, channels)
    work = PATCH * channels * (TAPS * channels + 9 * HALO)
    turned = nearby.T
    (inner_hidden,) = call(
        inner_kernel, [(half, BF16)], [feats, turned, conv_weight], flops=work, moved=4 << 20,
    )
    hidden, packed_hidden = call(
        outer_kernel, [(rows_c, BF16), (slots, BF16)],
        [dest, low, feats, high, turned, conv_weight, inner_hidden],
        smem=1, flops=work, moved=5 << 20,
    )
    got_hidden = moved(packed_hidden)
    cot_after, _ = lax.optimization_barrier((cotangent, hidden))
    packed_cot, gathered_t, qkv_weight_t = call(
        pack_kernel,
        [(slots, BF16), ((TAPS,) + square, BF16), ((3 * channels, channels), BF16)],
        [dest, cot_after, low, feats, high, turned, qkv_weight], smem=1, moved=8 << 20,
    )
    got_cot = moved(packed_cot)
    probs_shape = (HEADS, PATCH, PATCH)
    recip_shape = (HEADS, 1, PATCH)
    smem = pl.BlockSpec(memory_space=pltpu.SMEM)
    far = pl.BlockSpec(memory_space=pl.ANY)
    pair = HEADS * PATCH * PATCH
    packed_att, probs, recip, qkv, normed, xhat, inverse, heads = grid_call(
        forward_kernel,
        [dest, lengths, got_hidden, gain, qkv_weight_t, proj_weight],
        [smem, smem, whole(slots), whole((1, channels)), far, far],
        [(slots, BF16), (probs_shape, BF16), (recip_shape, F32), ((3 * channels, PATCH), BF16),
         ((channels, PATCH), BF16), ((channels, PATCH), F32), ((1, PATCH), F32),
         ((channels, PATCH), BF16)],
        [whole(slots), per_group((GROUP, PATCH, PATCH)), per_group((GROUP, 1, PATCH)),
         far, far, far, whole((1, PATCH)), whole((channels, PATCH))],
        [pltpu.VMEM(rows_c, F32), pltpu.VMEM(rows_c, BF16),
         pltpu.VMEM((3 * channels, channels), BF16), pltpu.VMEM(square, BF16),
         pltpu.VMEM((3 * channels, PATCH), BF16), pltpu.VMEM((channels, PATCH), BF16),
         pltpu.VMEM((channels, PATCH), F32), pltpu.SemaphoreType.DMA((2,)),
         pltpu.SemaphoreType.DMA((3,))],
        flops=2 * pair * 64 * 8, bytes_moved=32 << 20, exps=pair,
    )
    got_att = moved(packed_att)
    chips = scenes // 2
    shard = channels // scenes
    parts_shape = (4, chips, shard, channels)
    packed_dz, sent, kept = grid_call(
        backward_kernel,
        [dest, lengths, got_cot, probs, recip, qkv, normed, xhat, inverse, heads, gain, qkv_weight,
         proj_weight],
        [smem, smem, whole(slots), per_group((GROUP, PATCH, PATCH)), per_group((GROUP, 1, PATCH)),
         far, far, far, whole((1, PATCH)), whole((channels, PATCH)),
         whole((1, channels)), far, whole(square)],
        [(slots, BF16), (parts_shape, BF16), (parts_shape, BF16)],
        [far] * 3,
        [pltpu.VMEM((3 * channels, PATCH), BF16), pltpu.VMEM(rows_c, BF16),
         pltpu.VMEM((channels, PATCH), BF16), pltpu.VMEM(square, BF16),
         pltpu.VMEM((channels, PATCH), BF16), pltpu.VMEM((channels, PATCH), F32),
         pltpu.VMEM((channels, 3 * channels), BF16), pltpu.VMEM((3 * channels, PATCH), BF16),
         pltpu.VMEM(slots, BF16), pltpu.VMEM(parts_shape, BF16), pltpu.VMEM(parts_shape, BF16),
         pltpu.SemaphoreType.DMA((4,)), pltpu.SemaphoreType.DMA((5, 2))],
        flops=4 * pair * 64 * 8, bytes_moved=32 << 20, exps=0,
    )
    packed_dz, got_att = lax.optimization_barrier((packed_dz, got_att))
    got_dz = moved(packed_dz)
    tile_rows = tile_parts(over_cores(sent, kept))
    got_dz, received = lax.optimization_barrier((got_dz, across_tiles(tile_rows)))
    conv_shape = (chips, TAPS, shard, channels)
    by_tap = pl.BlockSpec((chips, 1, shard, channels), lambda step: (0, step, 0, 0))
    d_hidden_b, conv_sent, conv_kept = grid_call(
        conv_grad_kernel,
        [dest, got_dz, cotangent, gathered_t],
        [smem, whole(slots), whole(rows_c), per_group((1,) + square)],
        [(rows_c, BF16), (conv_shape, BF16), (conv_shape, BF16)],
        [whole(rows_c), by_tap, by_tap],
        [pltpu.VMEM(square, BF16)],
        flops=2 * TAPS * PATCH * channels * channels, bytes_moved=8 << 20, exps=0, steps=TAPS,
    )
    conv_other = lax.ppermute(conv_sent, "core", [(0, 1), (1, 0)])
    received, conv_kept = lax.optimization_barrier((received, conv_kept))
    mine = sum(one.astype(F32) for one in [tile_rows[0]] + received).astype(BF16)
    mine = lax.optimization_barrier(mine)
    rows_here = TAPS * shard
    ahead = ((0, 0, 0), (0, shard, 0), (0, 0, 0))
    behind = ((0, 0, 0), (rows_here, 0, 0), (0, 0, 0))
    zero = jnp.zeros((), BF16)
    chip_parts = sum(
        lax.pad(one.reshape(chips, -1, channels), zero, where).astype(F32)
        for one, where in ((conv_kept, ahead), (conv_other, ahead), (mine, behind))
    ).astype(BF16)
    total = summed(chip_parts, ("x", "z"))
    edge = (HALO, channels)
    feat_kept, to_previous, to_next, block_out = call(
        feat_grad_kernel, [(rows_c, F32), (edge, BF16), (edge, BF16), (rows_c, BF16)],
        [dest, turned, d_hidden_b, conv_weight, cotangent, got_dz, hidden, got_att],
        smem=1, flops=3 * work, moved=8 << 20,
        scratch=[
            pltpu.VMEM((PATCH + 2 * HALO, channels), BF16),
            pltpu.VMEM((PATCH + 2 * HALO, channels), F32),
        ],
    )
    from_previous, from_next = halo(to_previous, to_next, SCENE)
    total, feat_kept, block_out = lax.optimization_barrier((total, feat_kept, block_out))
    arrived = from_others(total)
    zero = jnp.zeros((), BF16)
    top = lax.pad(from_previous, zero, ((0, PATCH - HALO, 0), (0, 0, 0)))
    bottom = lax.pad(from_next, zero, ((PATCH - HALO, 0, 0), (0, 0, 0)))
    feat_grad = (feat_kept + top.astype(F32) + bottom.astype(F32)).astype(BF16)
    rank = lax.axis_index("dp").astype(jnp.int32)
    near = pl.BlockSpec(memory_space=pltpu.VMEM)
    grads = [(TAPS, shard, channels), (shard, 3 * channels), (shard, channels)]
    conv_grad, qkv_grad, proj_grad = pl.pallas_call(
        last_kernel,
        out_shape=[jax.ShapeDtypeStruct(shape, F32) for shape in grads],
        in_specs=[smem] + [near] * 4,
        out_specs=[far] * 3,
        scratch_shapes=[pltpu.VMEM(shape, F32) for shape in grads]
        + [pltpu.SemaphoreType.DMA((3,))],
        compiler_params=pltpu.CompilerParams(vmem_limit_bytes=8 << 20),
        cost_estimate=pl.CostEstimate(flops=1 << 20, bytes_accessed=1 << 20, transcendentals=0),
    )(rank[None], total, *arrived)
    return (block_out[None], feat_grad[None], conv_grad, qkv_grad, proj_grad)


def solution(mesh):
    fine = Mesh(mesh.devices.reshape(4, 4, 2, 4), ("x", "z", "core", "dp"))
    return jax.shard_map(
        body,
        mesh=fine,
        in_specs=(
            P("dp", SCENE, None),
            P("dp", SCENE, None),
            P("dp", None),
            P("dp", SCENE),
            P(),
            P(),
            P(),
            P(),
            P("dp", SCENE, None),
        ),
        out_specs=(
            P("dp", SCENE, None),
            P("dp", SCENE, None),
            P(None, SCENE, None),
            P(SCENE, None),
            P(SCENE, None),
        ),
        check_vma=False,
    )
```

```python
import jax
import jax.numpy as jnp
from jax import lax
from jax.experimental import pallas as pl
from jax.experimental.pallas import tpu as pltpu
from jax.sharding import Mesh
from jax.sharding import PartitionSpec as P

HEADS = 32
HEAD = 16
PATCH = 512
BLOCK = 32
BLOCKS = 16
HALO = 128
TAPS = 4
GROUP = 4
EPS = 1e-05
F32 = jnp.float32
BF16 = jnp.bfloat16
SCENE = ("x", "z", "core")


def dot(left, right, left_dim=1, right_dim=0):
    return lax.dot_general(
        left, right, (((left_dim,), (right_dim,)), ((), ())), preferred_element_type=F32
    )


VMEM_LIMIT = 60 << 20


def whole(shape):
    return pl.BlockSpec(shape, lambda step: (0,) * len(shape))


def per_group(shape):
    return pl.BlockSpec(shape, lambda step: (step,) + (0,) * (len(shape) - 1))


def call(kernel, outs, operands, smem=0, flops=0, moved=0, scratch=(), limit=VMEM_LIMIT):
    in_specs = [pl.BlockSpec(memory_space=pltpu.SMEM)] * smem
    in_specs += [whole(operand.shape) for operand in operands[smem:]]
    return pl.pallas_call(
        kernel,
        grid=(1,),
        out_shape=[jax.ShapeDtypeStruct(shape, dtype) for shape, dtype in outs],
        in_specs=in_specs,
        out_specs=[whole(shape) for shape, _ in outs],
        scratch_shapes=list(scratch),
        compiler_params=pltpu.CompilerParams(
            vmem_limit_bytes=limit, dimension_semantics=("arbitrary",)
        ),
        cost_estimate=pl.CostEstimate(flops=flops, bytes_accessed=moved, transcendentals=0),
    )(*operands)


def own_call(kernel, outs, operands, kinds, scratch, limit, flops=0, moved=0):
    spaces = {"s": pltpu.SMEM, "v": pltpu.VMEM, "a": pltpu.HBM}
    return pl.pallas_call(
        kernel,
        out_shape=[jax.ShapeDtypeStruct(shape, dtype) for shape, dtype in outs],
        in_specs=[pl.BlockSpec(memory_space=spaces[kind]) for kind in kinds],
        out_specs=[pl.BlockSpec(memory_space=pltpu.HBM)] * len(outs),
        scratch_shapes=scratch,
        compiler_params=pltpu.CompilerParams(vmem_limit_bytes=limit),
        cost_estimate=pl.CostEstimate(flops=flops, bytes_accessed=moved, transcendentals=0),
    )(*operands)


def scene_index():
    index = lax.axis_index(SCENE[0])
    for axis in SCENE[1:]:
        index = index * lax.axis_size(axis) + lax.axis_index(axis)
    return index


def target_of(dest, block):
    return dest[scene_index() * BLOCKS + block] // BLOCKS


def source_of(dest, block, scenes):
    shift = dest[block] // BLOCKS
    source = lax.rem(scene_index() - shift + scenes, scenes)
    return source, lax.rem(dest[source * BLOCKS + block], BLOCKS)


def split_parts(part, halves):
    core = lax.axis_index("core")
    shard = part.shape[0] // halves[0].shape[0] // 2
    for pair in range(halves[0].shape[0]):
        for half, owner in zip(halves, (1 - core, core)):
            start = pl.multiple_of((2 * pair + owner) * shard, shard)
            half[pair] = part[pl.ds(start, shard), :]


def column_of(row):
    return jnp.broadcast_to(row[...], (8, row.shape[1])).T[:, 0:1]


def columns_of(index):
    padded = jnp.concatenate([index, jnp.zeros((8 - TAPS, index.shape[1]), F32)], axis=0)
    return padded.T


def picked_rows(part, window, columns, tap):
    spots = lax.broadcasted_iota(jnp.int32, (HALO, 3 * HALO), 1).astype(F32)
    index = columns[part * HALO : (part + 1) * HALO, tap : tap + 1] - part * HALO
    return dot(jnp.where(spots == index, 1.0, 0.0).astype(BF16), window).astype(BF16)


def window_of(part, low, feats, high):
    if part == 0:
        return jnp.concatenate([low[...], feats[0 : 2 * HALO, :]], axis=0)
    if part == PATCH // HALO - 1:
        return jnp.concatenate([feats[PATCH - 2 * HALO :, :], high[...]], axis=0)
    return feats[pl.ds((part - 1) * HALO, 3 * HALO), :]


def conv_rows(part, own, window, columns, weight):
    total = own.astype(F32) + dot(own, weight[0])
    for tap in range(1, TAPS):
        total = total + dot(picked_rows(part, window, columns, tap), weight[tap])
    return total.astype(BF16)


def inner_kernel(feats, nearby, weight, hidden):
    columns = columns_of(nearby[...].astype(F32))
    for part in (1, 2):
        hidden[pl.ds((part - 1) * HALO, HALO), :] = conv_rows(
            part, feats[pl.ds(part * HALO, HALO), :], window_of(part, None, feats, None),
            columns, weight,
        )


def outer_kernel(
    dest, low, feats_far, high, nearby, weight_far, inner_far, hidden_far, packed_far,
    feats, weight, hidden, packed, arrivals, departures,
):
    middle = pl.ds(HALO, 2 * HALO)
    arriving = [
        pltpu.make_async_copy(feats_far, feats, arrivals.at[0]),
        pltpu.make_async_copy(inner_far, hidden.at[middle], arrivals.at[1]),
    ] + [
        pltpu.make_async_copy(weight_far.at[tap], weight.at[tap], arrivals.at[2 + tap])
        for tap in range(TAPS)
    ]
    for copy in arriving:
        copy.start()
    packed[...] = jnp.zeros_like(packed)
    columns = columns_of(nearby[...].astype(F32))
    arriving[0].wait()
    for at, part in enumerate((0, 3)):
        rows = pl.ds(part * HALO, HALO)
        window = window_of(part, low, feats, high)
        own = feats[rows, :]
        picked = [own] + [picked_rows(part, window, columns, tap) for tap in range(1, TAPS)]
        total = own.astype(F32)
        for tap in range(TAPS):
            if at == 0:
                arriving[2 + tap].wait()
            total = total + dot(picked[tap], weight[tap])
        hidden[rows, :] = total.astype(BF16)
    arriving[1].wait()
    for block in range(BLOCKS):
        packed[target_of(dest, block)] = hidden[pl.ds(block * BLOCK, BLOCK), :]
    leaving = [
        pltpu.make_async_copy(packed, packed_far, departures.at[0]),
        pltpu.make_async_copy(hidden, hidden_far, departures.at[1]),
    ]
    for copy in leaving:
        copy.start()
    for copy in leaving:
        copy.wait()


def pack_kernel(
    dest, blocks, low, feats, high, nearby, qkv_weight, packed, theirs, ours, qkv_weight_t,
    gathered_t,
):
    packed[...] = jnp.zeros_like(packed)
    for block in range(BLOCKS):
        packed[target_of(dest, block)] = blocks[pl.ds(block * BLOCK, BLOCK), :]
    columns = columns_of(nearby[...].astype(F32))
    gathered_t[0] = feats[...].T
    for part in range(PATCH // HALO):
        window = window_of(part, low, feats, high)
        for tap in range(1, TAPS):
            picked = picked_rows(part, window, columns, tap)
            gathered_t[tap, :, pl.ds(part * HALO, HALO)] = picked.T
    for tap in range(TAPS):
        split_parts(gathered_t.at[tap], [theirs.at[tap], ours.at[tap]])
    qkv_weight_t[...] = qkv_weight[...].T


def forward_kernel(
    dest, lengths, got, gain, weight_far, proj_far,
    packed, probs, recip, qkv_far, normed_far, xhat_far, inverse, heads,
    rows_f, attended, qkv_weight_t, proj_weight, qkv, normed, xhat, arrivals, departures,
):
    step = pl.program_id(0)
    arriving = [
        pltpu.make_async_copy(far, near, arrivals.at[at])
        for at, (far, near) in enumerate(((weight_far, qkv_weight_t), (proj_far, proj_weight)))
    ]
    leaving = [
        pltpu.make_async_copy(near, far, departures.at[at])
        for at, (near, far) in enumerate(
            ((xhat, xhat_far), (normed, normed_far), (qkv, qkv_far))
        )
    ]
    scenes = got.shape[0]
    length = lengths[0, 0]

    @pl.when(step == 0)
    def _():
        for copy in arriving:
            copy.start()
        for block in range(BLOCKS):
            source, slot = source_of(dest, block, scenes)
            rows = pl.ds(pl.multiple_of(slot * BLOCK, BLOCK), BLOCK)
            rows_f[rows, :] = got[source].astype(F32)
        rows_t = rows_f[...].T
        centred = rows_t - jnp.mean(rows_t, axis=0, keepdims=True)
        scale = lax.rsqrt(jnp.mean(centred * centred, axis=0, keepdims=True) + EPS)
        standard = centred * scale
        inverse[...] = scale
        xhat[...] = standard
        normed[...] = (standard * column_of(gain)).astype(BF16)
        leaving[0].start()
        leaving[1].start()
        arriving[0].wait()
        qkv[...] = dot(qkv_weight_t[...], normed[...]).astype(BF16)
        leaving[2].start()

    sub = lax.broadcasted_iota(jnp.int32, (HEAD, PATCH), 0)
    spot = lax.broadcasted_iota(jnp.int32, (HEAD, PATCH), 1)
    dead = jnp.where((sub == 0) & (spot >= length), -1e30, 0.0).astype(BF16)
    ones = jnp.where(sub == 0, 1.0, 0.0).astype(BF16)
    live = lax.broadcasted_iota(jnp.int32, (1, PATCH), 1) < length
    channels = HEADS * HEAD

    def scores_of(one):
        row = pl.multiple_of((step * GROUP + one) * HEAD, HEAD)
        query = (qkv[pl.ds(row, HEAD), :].astype(F32) * HEAD ** (-0.5)).astype(BF16)
        key = qkv[pl.ds(channels + row, HEAD), :]
        return dot(
            jnp.concatenate([key, dead], axis=0), jnp.concatenate([query, ones], axis=0), 0, 0
        )

    scores = scores_of(0)
    for one in range(GROUP):
        following = scores_of(one + 1) if one + 1 < GROUP else None
        row = pl.multiple_of((step * GROUP + one) * HEAD, HEAD)
        value = qkv[pl.ds(2 * channels + row, HEAD), :]
        raised = jnp.exp(scores - jnp.max(scores, axis=0, keepdims=True)).astype(BF16)
        probs[one] = raised
        out = dot(jnp.concatenate([value, ones], axis=0), raised)
        over = 1.0 / out[HEAD : HEAD + 1]
        recip[one] = over
        heads[pl.ds(row, HEAD), :] = jnp.where(live, out[:HEAD] * over, 0.0).astype(BF16)
        scores = following

    @pl.when(step == pl.num_programs(0) - 1)
    def _():
        packed[...] = jnp.zeros_like(packed)
        arriving[1].wait()
        attended[...] = dot(heads[...], proj_weight[...], 0, 0).astype(BF16)
        for block in range(BLOCKS):
            source, slot = source_of(dest, block, scenes)
            rows = pl.ds(pl.multiple_of(slot * BLOCK, BLOCK), BLOCK)
            packed[source] = attended[rows, :]
        for copy in leaving:
            copy.wait()


def backward_kernel(
    dest, lengths, got_cot, probs, recip, qkv_far, normed, xhat, inverse, heads, gain,
    qkv_weight, proj_weight,
    packed_far, sent_far, kept_far,
    d_qkv, d_rows, d_heads, part, normed_here, xhat_here, weight_here, qkv, packed, sent, kept,
    arrivals, departures,
):
    step = pl.program_id(0)
    scenes = packed.shape[0]
    leaving = [
        pltpu.make_async_copy(near.at[at], far.at[at], departures.at[at, half])
        for at in range(sent.shape[0])
        for half, (near, far) in enumerate(((sent, sent_far), (kept, kept_far)))
    ]
    leaving.append(pltpu.make_async_copy(packed, packed_far, departures.at[sent.shape[0], 0]))
    channels = HEADS * HEAD

    late = [
        pltpu.make_async_copy(far, near, arrivals.at[at])
        for at, (far, near) in enumerate(
            (
                (qkv_far, qkv), (normed, normed_here), (xhat, xhat_here),
                (qkv_weight, weight_here),
            )
        )
    ]

    @pl.when(step == 0)
    def _():
        late[0].start()
        for block in range(BLOCKS):
            source, slot = source_of(dest, block, scenes)
            rows = pl.ds(pl.multiple_of(slot * BLOCK, BLOCK), BLOCK)
            d_rows[rows, :] = got_cot[source]
        live = lax.broadcasted_iota(jnp.int32, (1, PATCH), 1) < lengths[0, 0]
        d_full = dot(proj_weight[...], d_rows[...], 1, 1)
        d_heads[...] = jnp.where(live, d_full, 0.0).astype(BF16)
        part[...] = dot(heads[...], d_rows[...]).astype(BF16)
        split_parts(part, [sent.at[3], kept.at[3]])
        leaving[6].start()
        leaving[7].start()
        late[0].wait()
        for copy in late[1:]:
            copy.start()

    sub = lax.broadcasted_iota(jnp.int32, (HEAD, PATCH), 0)
    ones = jnp.where(sub < 3, 1.0, 0.0).astype(BF16)

    def d_probs_of(one):
        row = pl.multiple_of((step * GROUP + one) * HEAD, HEAD)
        value = qkv[pl.ds(2 * channels + row, HEAD), :]
        d_out = d_heads[pl.ds(row, HEAD), :]
        row_dot = jnp.sum(
            d_out.astype(F32) * heads[pl.ds(row, HEAD), :].astype(F32), axis=0, keepdims=True
        )
        first = row_dot.astype(BF16).astype(F32)
        second = (row_dot - first).astype(BF16).astype(F32)
        third = row_dot - first - second
        split = jnp.where(sub == 0, first, jnp.where(sub == 1, second, third))
        minus = jnp.where(sub < 3, -split, 0.0).astype(BF16)
        return dot(
            jnp.concatenate([value, ones], axis=0), jnp.concatenate([d_out, minus], axis=0), 0, 0
        )

    d_probs = d_probs_of(0)
    for one in range(GROUP):
        following = d_probs_of(one + 1) if one + 1 < GROUP else None
        row = pl.multiple_of((step * GROUP + one) * HEAD, HEAD)
        query = qkv[pl.ds(row, HEAD), :].astype(F32)
        key = qkv[pl.ds(channels + row, HEAD), :]
        over = recip[one]
        raised = probs[one]
        d_scores = (raised.astype(F32) * d_probs).astype(BF16)
        d_out = (d_heads[pl.ds(row, HEAD), :].astype(F32) * over).astype(BF16)
        d_qkv[pl.ds(2 * channels + row, HEAD), :] = dot(d_out, raised, 1, 1).astype(BF16)
        scaled = over * HEAD ** (-0.5)
        d_qkv[pl.ds(row, HEAD), :] = (dot(key, d_scores) * scaled).astype(BF16)
        d_key = dot((query * scaled).astype(BF16), d_scores, 1, 1)
        d_qkv[pl.ds(channels + row, HEAD), :] = d_key.astype(BF16)
        d_probs = following

    @pl.when(step == pl.num_programs(0) - 1)
    def _():
        for copy in late[1:]:
            copy.wait()
        spread = dot(weight_here[...], d_qkv[...]) * column_of(gain)
        standard = xhat_here[...]
        row_gradient = inverse[...] * (
            spread
            - jnp.mean(spread, axis=0, keepdims=True)
            - standard * jnp.mean(spread * standard, axis=0, keepdims=True)
        )
        d_rows[...] = row_gradient.T.astype(BF16)
        packed[...] = jnp.zeros_like(packed)
        for block in range(BLOCKS):
            source, slot = source_of(dest, block, scenes)
            packed[source] = d_rows[pl.ds(pl.multiple_of(slot * BLOCK, BLOCK), BLOCK), :]
        leaving[8].start()
        for third in range(3):
            columns = d_qkv[pl.ds(third * channels, channels), :]
            part[...] = dot(normed_here[...], columns, 1, 1).astype(BF16)
            split_parts(part, [sent.at[third], kept.at[third]])
            leaving[2 * third].start()
            leaving[2 * third + 1].start()
        for copy in leaving:
            copy.wait()


def tile_parts_kernel(other, kept_far, *rest):
    count = lax.axis_size("dp")
    parts_far, (kept, parts, arrivals, departures) = rest[:count], rest[count:]
    rank = lax.axis_index("dp")
    groups = [lax.rem(rank + step, count) for step in range(count)]
    arriving = [
        pltpu.make_async_copy(kept_far.at[group], kept.at[step], arrivals.at[step])
        for step, group in enumerate(groups)
    ]
    for copy in arriving[1:] + arriving[:1]:
        copy.start()
    leaving = [
        pltpu.make_async_copy(parts.at[step], parts_far[step], departures.at[step])
        for step in range(count)
    ]
    for step in [*range(1, count), 0]:
        arriving[step].wait()
        parts[step] = (kept[step].astype(F32) + other[groups[step]].astype(F32)).astype(BF16)
        leaving[step].start()
    for copy in leaving:
        copy.wait()


def hidden_grad_kernel(dest, got, cot_far, d_hidden_far, cot, d_hidden_b, sems):
    arriving = pltpu.make_async_copy(cot_far, cot, sems.at[0])
    arriving.start()
    arriving.wait()
    for block in range(BLOCKS):
        rows = pl.ds(block * BLOCK, BLOCK)
        total = cot[rows, :].astype(F32) + got[target_of(dest, block)].astype(F32)
        d_hidden_b[rows, :] = total.astype(BF16)
    leaving = pltpu.make_async_copy(d_hidden_b, d_hidden_far, sems.at[1])
    leaving.start()
    leaving.wait()


def conv_grad_kernel(
    d_other, d_own_far, ours_far, others_far, q_part, out_far,
    d_own, ours, others, out, arrivals, departures,
):
    taps, chips, shard, rows = ours.shape
    arriving = [pltpu.make_async_copy(d_own_far, d_own, arrivals.at[TAPS, 0])]
    for tap in range(taps):
        arriving += [
            pltpu.make_async_copy(ours_far.at[tap], ours.at[tap], arrivals.at[tap, 0]),
            pltpu.make_async_copy(others_far.at[tap], others.at[tap], arrivals.at[tap, 1]),
        ]
    for copy in arriving:
        copy.start()
    out[TAPS] = q_part[...]
    leaving = [
        pltpu.make_async_copy(
            out.at[tap], out_far.at[:, pl.ds(tap * shard, shard)], departures.at[tap]
        )
        for tap in range(TAPS + 1)
    ]
    leaving[TAPS].start()
    arriving[0].wait()
    for tap in range(taps):
        arriving[1 + 2 * tap].wait()
        arriving[2 + 2 * tap].wait()
        part = dot(ours[tap].reshape(chips * shard, rows), d_own[...])
        part = part + dot(others[tap].reshape(chips * shard, rows), d_other[...])
        out[tap] = part.astype(BF16).reshape(chips, shard, part.shape[1])
        leaving[tap].start()
    for copy in leaving:
        copy.wait()


def feat_grad_kernel(
    dest, nearby, d_hidden_b, weight, cot, got_dz, hidden, got,
    kept, to_previous, to_next, block_out, spread, landed,
):
    spots = lax.broadcasted_iota(jnp.int32, (HALO, 3 * HALO), 0)
    landing = PATCH // HALO + 2
    landed[...] = jnp.zeros_like(landed)
    for tap in range(1, TAPS):
        for part in range(landing):
            start, stop = max(0, part - 2) * HALO, min(PATCH // HALO, part + 1) * HALO
            index = nearby[pl.ds(tap, 1), pl.ds(start, stop - start)] - part * HALO
            chosen = jnp.where(spots[:, : stop - start] == index, 1.0, 0.0).astype(BF16)
            spread[pl.ds(part * HALO, HALO), :] = dot(
                chosen, d_hidden_b[pl.ds(start, stop - start), :]
            ).astype(BF16)
        landed[...] += dot(spread[...], weight[tap], 1, 1)
    to_previous[...] = landed[0:HALO, :].astype(BF16)
    to_next[...] = landed[HALO + PATCH :, :].astype(BF16)
    landed[HALO : HALO + PATCH, :] += dot(d_hidden_b[...], weight[0], 1, 1)
    for block in range(BLOCKS):
        rows = pl.ds(block * BLOCK, BLOCK)
        d_hidden = cot[rows, :].astype(F32) + got_dz[target_of(dest, block)].astype(F32)
        kept[rows, :] = d_hidden + landed[pl.ds(HALO + block * BLOCK, BLOCK), :]
        block_out[rows, :] = (
            hidden[rows, :].astype(F32) + got[target_of(dest, block)].astype(F32)
        ).astype(BF16)


def last_kernel(
    rank, mine, first, second, third, conv_far, qkv_far, proj_far, conv_grad, qkv_grad, proj_grad,
    sems,
):
    arrived = [mine, first, second, third]
    shard = proj_grad.shape[0]
    channels = proj_grad.shape[1]
    for tap in range(TAPS):
        rows = pl.ds(tap * shard, shard)
        conv_grad[tap] = sum(one[rows, :].astype(F32) for one in arrived)
    copies = [
        pltpu.make_async_copy(near, far, sems.at[at])
        for at, (near, far) in enumerate(
            ((conv_grad, conv_far), (qkv_grad, qkv_far), (proj_grad, proj_far))
        )
    ]
    copies[0].start()
    for step, one in enumerate(arrived):
        block = one[pl.ds(TAPS * shard, shard), :].astype(F32)
        origin = lax.rem(rank[0] - step + len(arrived), len(arrived))
        for third_at in range(3):
            @pl.when(origin == third_at)
            def _(block=block, third_at=third_at):
                qkv_grad[:, pl.ds(third_at * channels, channels)] = block

        @pl.when(origin == 3)
        def _(block=block):
            proj_grad[...] = block
    copies[1].start()
    copies[2].start()
    for copy in copies:
        copy.wait()


def halo(first, last, axis):
    count = lax.axis_size(axis)
    forward = [(i, i + 1) for i in range(count - 1)]
    backward = [(i + 1, i) for i in range(count - 1)]
    return lax.ppermute(last, axis, forward), lax.ppermute(first, axis, backward)


def moved(packed):
    return lax.all_to_all(packed, SCENE, split_axis=0, concat_axis=0, tiled=True)


def summed(parts, axis, dtype=BF16):
    got = lax.all_to_all(parts, axis, split_axis=0, concat_axis=0, tiled=True)
    return jnp.sum(got.astype(F32), axis=0).astype(dtype)


def across_tiles(parts):
    count = len(parts)
    return [
        lax.ppermute(parts[step], "dp", [(i, (i + step) % count) for i in range(count)])
        for step in range(1, count)
    ]


def from_others(mine):
    count = lax.axis_size("dp")
    return [
        lax.ppermute(mine, "dp", [(i, (i + step) % count) for i in range(count)])
        for step in range(1, count)
    ]


def grid_call(
    kernel, ins, in_specs, outs, out_specs, scratch, flops, bytes_moved, exps,
    steps=HEADS // GROUP,
):
    return pl.pallas_call(
        kernel,
        grid=(steps,),
        out_shape=[jax.ShapeDtypeStruct(shape, dtype) for shape, dtype in outs],
        in_specs=in_specs,
        out_specs=out_specs,
        scratch_shapes=scratch,
        compiler_params=pltpu.CompilerParams(
            vmem_limit_bytes=VMEM_LIMIT, dimension_semantics=("arbitrary",)
        ),
        cost_estimate=pl.CostEstimate(
            flops=flops, bytes_accessed=bytes_moved, transcendentals=exps
        ),
    )(*ins)


def body(
    points_feat, neighbours, block_dest, lengths, conv_weight, norm_gain, qkv_weight, proj_weight,
    out_grad,
):
    feats = points_feat[0]
    cotangent = out_grad[0]
    nearby = neighbours[0]
    dest = block_dest[0]
    channels = feats.shape[1]
    scenes = lax.axis_size(SCENE)
    gain = norm_gain[None, :]
    rows_c = (PATCH, channels)
    square = (channels, channels)
    slots = (scenes, BLOCK, channels)

    low, high = halo(feats[:HALO], feats[PATCH - HALO :], SCENE)
    half = (2 * HALO, channels)
    work = PATCH * channels * (TAPS * channels + 9 * HALO)
    turned = nearby.T
    (inner_hidden,) = call(
        inner_kernel, [(half, BF16)], [feats, turned, conv_weight], flops=work, moved=4 << 20,
    )
    weights = (TAPS,) + square
    hidden, packed_hidden = own_call(
        outer_kernel, [(rows_c, BF16), (slots, BF16)],
        [dest, low, feats, high, turned, conv_weight, inner_hidden], "svavvaa",
        [pltpu.VMEM(rows_c, BF16), pltpu.VMEM(weights, BF16), pltpu.VMEM(rows_c, BF16),
         pltpu.VMEM(slots, BF16), pltpu.SemaphoreType.DMA((2 + TAPS,)),
         pltpu.SemaphoreType.DMA((2,))],
        limit=20 << 20, flops=work, moved=5 << 20,
    )
    got_hidden = moved(packed_hidden)
    cot_after, _ = lax.optimization_barrier((cotangent, hidden))
    chips = scenes // 2
    shard = channels // scenes
    halves = (TAPS, chips, shard, PATCH)
    packed_cot, theirs, ours, qkv_weight_t = call(
        pack_kernel,
        [(slots, BF16), (halves, BF16), (halves, BF16), ((3 * channels, channels), BF16)],
        [dest, cot_after, low, feats, high, turned, qkv_weight], smem=1, moved=8 << 20,
        scratch=[pltpu.VMEM(weights, BF16)],
    )
    others = lax.ppermute(theirs, "core", [(0, 1), (1, 0)])
    got_cot = moved(packed_cot)
    probs_shape = (HEADS, PATCH, PATCH)
    recip_shape = (HEADS, 1, PATCH)
    smem = pl.BlockSpec(memory_space=pltpu.SMEM)
    far = pl.BlockSpec(memory_space=pl.ANY)
    pair = HEADS * PATCH * PATCH
    packed_att, probs, recip, qkv, normed, xhat, inverse, heads = grid_call(
        forward_kernel,
        [dest, lengths, got_hidden, gain, qkv_weight_t, proj_weight],
        [smem, smem, whole(slots), whole((1, channels)), far, far],
        [(slots, BF16), (probs_shape, BF16), (recip_shape, F32), ((3 * channels, PATCH), BF16),
         ((channels, PATCH), BF16), ((channels, PATCH), F32), ((1, PATCH), F32),
         ((channels, PATCH), BF16)],
        [whole(slots), per_group((GROUP, PATCH, PATCH)), per_group((GROUP, 1, PATCH)),
         far, far, far, whole((1, PATCH)), whole((channels, PATCH))],
        [pltpu.VMEM(rows_c, F32), pltpu.VMEM(rows_c, BF16),
         pltpu.VMEM((3 * channels, channels), BF16), pltpu.VMEM(square, BF16),
         pltpu.VMEM((3 * channels, PATCH), BF16), pltpu.VMEM((channels, PATCH), BF16),
         pltpu.VMEM((channels, PATCH), F32), pltpu.SemaphoreType.DMA((2,)),
         pltpu.SemaphoreType.DMA((3,))],
        flops=2 * pair * 64 * 8, bytes_moved=32 << 20, exps=pair,
    )
    got_att = moved(packed_att)
    parts_shape = (4, chips, shard, channels)
    packed_dz, sent, kept = grid_call(
        backward_kernel,
        [dest, lengths, got_cot, probs, recip, qkv, normed, xhat, inverse, heads, gain, qkv_weight,
         proj_weight],
        [smem, smem, whole(slots), per_group((GROUP, PATCH, PATCH)), per_group((GROUP, 1, PATCH)),
         far, far, far, whole((1, PATCH)), whole((channels, PATCH)),
         whole((1, channels)), far, whole(square)],
        [(slots, BF16), (parts_shape, BF16), (parts_shape, BF16)],
        [far] * 3,
        [pltpu.VMEM((3 * channels, PATCH), BF16), pltpu.VMEM(rows_c, BF16),
         pltpu.VMEM((channels, PATCH), BF16), pltpu.VMEM(square, BF16),
         pltpu.VMEM((channels, PATCH), BF16), pltpu.VMEM((channels, PATCH), F32),
         pltpu.VMEM((channels, 3 * channels), BF16), pltpu.VMEM((3 * channels, PATCH), BF16),
         pltpu.VMEM(slots, BF16), pltpu.VMEM(parts_shape, BF16), pltpu.VMEM(parts_shape, BF16),
         pltpu.SemaphoreType.DMA((4,)), pltpu.SemaphoreType.DMA((5, 2))],
        flops=4 * pair * 64 * 8, bytes_moved=32 << 20, exps=0,
    )
    packed_dz, got_att = lax.optimization_barrier((packed_dz, got_att))
    got_dz = moved(packed_dz)
    tile_rows = own_call(
        tile_parts_kernel, [((chips, shard, channels), BF16)] * 4,
        [lax.ppermute(sent, "core", [(0, 1), (1, 0)]), kept], "va",
        [pltpu.VMEM(parts_shape, BF16), pltpu.VMEM(parts_shape, BF16),
         pltpu.SemaphoreType.DMA((4,)), pltpu.SemaphoreType.DMA((4,))],
        limit=8 << 20, moved=3 << 20,
    )
    got_dz, received = lax.optimization_barrier((got_dz, across_tiles(tile_rows)))
    mine = sum(one.astype(F32) for one in [tile_rows[0]] + received).astype(BF16)
    (d_hidden_b,) = own_call(
        hidden_grad_kernel, [(rows_c, BF16)], [dest, got_dz, cotangent], "sva",
        [pltpu.VMEM(rows_c, BF16), pltpu.VMEM(rows_c, BF16), pltpu.SemaphoreType.DMA((2,))],
        limit=8 << 20, moved=2 << 20,
    )
    d_other = lax.ppermute(d_hidden_b, "core", [(0, 1), (1, 0)])
    rows_here = TAPS * shard
    (chip_parts,) = own_call(
        conv_grad_kernel, [((chips, rows_here + shard, channels), BF16)],
        [d_other, d_hidden_b, ours, others, mine], "vaaav",
        [pltpu.VMEM(rows_c, BF16), pltpu.VMEM(halves, BF16), pltpu.VMEM(halves, BF16),
         pltpu.VMEM((TAPS + 1, chips, shard, channels), BF16),
         pltpu.SemaphoreType.DMA((TAPS + 1, 2)), pltpu.SemaphoreType.DMA((TAPS + 1,))],
        limit=20 << 20, flops=2 * TAPS * PATCH * channels * channels, moved=8 << 20,
    )
    total = summed(chip_parts, ("x", "z"))
    edge = (HALO, channels)
    feat_kept, to_previous, to_next, block_out = call(
        feat_grad_kernel, [(rows_c, F32), (edge, BF16), (edge, BF16), (rows_c, BF16)],
        [dest, turned, d_hidden_b, conv_weight, cotangent, got_dz, hidden, got_att],
        smem=1, flops=3 * work, moved=8 << 20,
        scratch=[
            pltpu.VMEM((PATCH + 2 * HALO, channels), BF16),
            pltpu.VMEM((PATCH + 2 * HALO, channels), F32),
        ],
    )
    from_previous, from_next = halo(to_previous, to_next, SCENE)
    total, feat_kept, block_out = lax.optimization_barrier((total, feat_kept, block_out))
    arrived = from_others(total)
    zero = jnp.zeros((), BF16)
    top = lax.pad(from_previous, zero, ((0, PATCH - HALO, 0), (0, 0, 0)))
    bottom = lax.pad(from_next, zero, ((PATCH - HALO, 0, 0), (0, 0, 0)))
    feat_grad = (feat_kept + top.astype(F32) + bottom.astype(F32)).astype(BF16)
    rank = lax.axis_index("dp").astype(jnp.int32)
    near = pl.BlockSpec(memory_space=pltpu.VMEM)
    grads = [(TAPS, shard, channels), (shard, 3 * channels), (shard, channels)]
    conv_grad, qkv_grad, proj_grad = pl.pallas_call(
        last_kernel,
        out_shape=[jax.ShapeDtypeStruct(shape, F32) for shape in grads],
        in_specs=[smem] + [near] * 4,
        out_specs=[far] * 3,
        scratch_shapes=[pltpu.VMEM(shape, F32) for shape in grads]
        + [pltpu.SemaphoreType.DMA((3,))],
        compiler_params=pltpu.CompilerParams(vmem_limit_bytes=8 << 20),
        cost_estimate=pl.CostEstimate(flops=1 << 20, bytes_accessed=1 << 20, transcendentals=0),
    )(rank[None], total, *arrived)
    return (block_out[None], feat_grad[None], conv_grad, qkv_grad, proj_grad)


def solution(mesh):
    fine = Mesh(mesh.devices.reshape(4, 4, 2, 4), ("x", "z", "core", "dp"))
    return jax.shard_map(
        body,
        mesh=fine,
        in_specs=(
            P("dp", SCENE, None),
            P("dp", SCENE, None),
            P("dp", None),
            P("dp", SCENE),
            P(),
            P(),
            P(),
            P(),
            P("dp", SCENE, None),
        ),
        out_specs=(
            P("dp", SCENE, None),
            P("dp", SCENE, None),
            P(None, SCENE, None),
            P(SCENE, None),
            P(SCENE, None),
        ),
        check_vma=False,
    )
```

```python
import jax
import jax.numpy as jnp
from jax import lax
from jax.experimental import pallas as pl
from jax.experimental.pallas import tpu as pltpu
from jax.sharding import Mesh
from jax.sharding import PartitionSpec as P

HEADS = 32
HEAD = 16
PATCH = 512
BLOCK = 32
BLOCKS = 16
HALO = 128
TAPS = 4
GROUP = 4
EPS = 1e-05
F32 = jnp.float32
BF16 = jnp.bfloat16
SCENE = ("x", "z", "core")


def dot(left, right, left_dim=1, right_dim=0):
    return lax.dot_general(
        left, right, (((left_dim,), (right_dim,)), ((), ())), preferred_element_type=F32
    )


VMEM_LIMIT = 60 << 20


def whole(shape):
    return pl.BlockSpec(shape, lambda step: (0,) * len(shape))


def per_group(shape):
    return pl.BlockSpec(shape, lambda step: (step,) + (0,) * (len(shape) - 1))


def call(kernel, outs, operands, smem=0, flops=0, moved=0, scratch=(), limit=VMEM_LIMIT):
    in_specs = [pl.BlockSpec(memory_space=pltpu.SMEM)] * smem
    in_specs += [whole(operand.shape) for operand in operands[smem:]]
    return pl.pallas_call(
        kernel,
        grid=(1,),
        out_shape=[jax.ShapeDtypeStruct(shape, dtype) for shape, dtype in outs],
        in_specs=in_specs,
        out_specs=[whole(shape) for shape, _ in outs],
        scratch_shapes=list(scratch),
        compiler_params=pltpu.CompilerParams(
            vmem_limit_bytes=limit, dimension_semantics=("arbitrary",)
        ),
        cost_estimate=pl.CostEstimate(flops=flops, bytes_accessed=moved, transcendentals=0),
    )(*operands)


def own_call(kernel, outs, operands, kinds, scratch, limit, flops=0, moved=0):
    spaces = {"s": pltpu.SMEM, "v": pltpu.VMEM, "a": pltpu.HBM}
    return pl.pallas_call(
        kernel,
        out_shape=[jax.ShapeDtypeStruct(shape, dtype) for shape, dtype in outs],
        in_specs=[pl.BlockSpec(memory_space=spaces[kind]) for kind in kinds],
        out_specs=[pl.BlockSpec(memory_space=pltpu.HBM)] * len(outs),
        scratch_shapes=scratch,
        compiler_params=pltpu.CompilerParams(vmem_limit_bytes=limit),
        cost_estimate=pl.CostEstimate(flops=flops, bytes_accessed=moved, transcendentals=0),
    )(*operands)


def scene_index():
    index = lax.axis_index(SCENE[0])
    for axis in SCENE[1:]:
        index = index * lax.axis_size(axis) + lax.axis_index(axis)
    return index


def target_of(dest, block):
    return dest[scene_index() * BLOCKS + block] // BLOCKS


def source_of(dest, block, scenes):
    shift = dest[block] // BLOCKS
    source = lax.rem(scene_index() - shift + scenes, scenes)
    return source, lax.rem(dest[source * BLOCKS + block], BLOCKS)


def split_parts(part, halves):
    core = lax.axis_index("core")
    shard = part.shape[0] // halves[0].shape[0] // 2
    for pair in range(halves[0].shape[0]):
        for half, owner in zip(halves, (1 - core, core)):
            start = pl.multiple_of((2 * pair + owner) * shard, shard)
            half[pair] = part[pl.ds(start, shard), :]


def column_of(row):
    return jnp.broadcast_to(row[...], (8, row.shape[1])).T[:, 0:1]


def columns_of(index):
    padded = jnp.concatenate([index, jnp.zeros((8 - TAPS, index.shape[1]), F32)], axis=0)
    return padded.T


def picked_rows(part, window, columns, tap):
    spots = lax.broadcasted_iota(jnp.int32, (HALO, 3 * HALO), 1).astype(F32)
    index = columns[part * HALO : (part + 1) * HALO, tap : tap + 1] - part * HALO
    return dot(jnp.where(spots == index, 1.0, 0.0).astype(BF16), window).astype(BF16)


def window_of(part, low, feats, high):
    if part == 0:
        return jnp.concatenate([low[...], feats[0 : 2 * HALO, :]], axis=0)
    if part == PATCH // HALO - 1:
        return jnp.concatenate([feats[PATCH - 2 * HALO :, :], high[...]], axis=0)
    return feats[pl.ds((part - 1) * HALO, 3 * HALO), :]


def conv_rows(part, own, window, columns, weight):
    total = own.astype(F32) + dot(own, weight[0])
    for tap in range(1, TAPS):
        total = total + dot(picked_rows(part, window, columns, tap), weight[tap])
    return total.astype(BF16)


def inner_kernel(feats, nearby, weight, hidden):
    columns = columns_of(nearby[...].astype(F32))
    for part in (1, 2):
        hidden[pl.ds((part - 1) * HALO, HALO), :] = conv_rows(
            part, feats[pl.ds(part * HALO, HALO), :], window_of(part, None, feats, None),
            columns, weight,
        )


def outer_kernel(
    dest, low, feats_far, high, nearby, weight_far, inner_far,
    packed_far,
    feats, weight, hidden, packed, arrivals, departures,
):
    middle = pl.ds(HALO, 2 * HALO)
    arriving = [
        pltpu.make_async_copy(feats_far, feats, arrivals.at[0]),
        pltpu.make_async_copy(inner_far, hidden.at[middle], arrivals.at[1]),
    ] + [
        pltpu.make_async_copy(weight_far.at[tap], weight.at[tap], arrivals.at[2 + tap])
        for tap in range(TAPS)
    ]
    for copy in arriving:
        copy.start()
    packed[...] = jnp.zeros_like(packed)
    columns = columns_of(nearby[...].astype(F32))
    arriving[0].wait()
    for at, part in enumerate((0, 3)):
        rows = pl.ds(part * HALO, HALO)
        window = window_of(part, low, feats, high)
        own = feats[rows, :]
        picked = [own] + [picked_rows(part, window, columns, tap) for tap in range(1, TAPS)]
        total = own.astype(F32)
        for tap in range(TAPS):
            if at == 0:
                arriving[2 + tap].wait()
            total = total + dot(picked[tap], weight[tap])
        hidden[rows, :] = total.astype(BF16)
    arriving[1].wait()
    for block in range(BLOCKS):
        packed[target_of(dest, block)] = hidden[pl.ds(block * BLOCK, BLOCK), :]
    leaving = pltpu.make_async_copy(packed, packed_far, departures.at[0])
    leaving.start()
    leaving.wait()


def pack_kernel(
    dest, blocks, low, feats, high, nearby, qkv_weight, packed, theirs, ours, qkv_weight_t,
    gathered_t,
):
    packed[...] = jnp.zeros_like(packed)
    for block in range(BLOCKS):
        packed[target_of(dest, block)] = blocks[pl.ds(block * BLOCK, BLOCK), :]
    columns = columns_of(nearby[...].astype(F32))
    gathered_t[0] = feats[...].T
    for part in range(PATCH // HALO):
        window = window_of(part, low, feats, high)
        for tap in range(1, TAPS):
            picked = picked_rows(part, window, columns, tap)
            gathered_t[tap, :, pl.ds(part * HALO, HALO)] = picked.T
    for tap in range(TAPS):
        split_parts(gathered_t.at[tap], [theirs.at[tap], ours.at[tap]])
    qkv_weight_t[...] = qkv_weight[...].T


def forward_kernel(
    dest, lengths, got, gain, weight_far, proj_far,
    packed, probs, recip, qkv_far, normed_far, xhat_far, inverse, heads,
    rows_f, attended, qkv_weight_t, proj_weight, qkv, normed, xhat, arrivals, departures,
):
    step = pl.program_id(0)
    arriving = [
        pltpu.make_async_copy(far, near, arrivals.at[at])
        for at, (far, near) in enumerate(((weight_far, qkv_weight_t), (proj_far, proj_weight)))
    ]
    leaving = [
        pltpu.make_async_copy(near, far, departures.at[at])
        for at, (near, far) in enumerate(
            ((xhat, xhat_far), (normed, normed_far), (qkv, qkv_far))
        )
    ]
    scenes = got.shape[0]
    length = lengths[0, 0]

    @pl.when(step == 0)
    def _():
        for copy in arriving:
            copy.start()
        for block in range(BLOCKS):
            source, slot = source_of(dest, block, scenes)
            rows = pl.ds(pl.multiple_of(slot * BLOCK, BLOCK), BLOCK)
            rows_f[rows, :] = got[source].astype(F32)
        rows_t = rows_f[...].T
        centred = rows_t - jnp.mean(rows_t, axis=0, keepdims=True)
        scale = lax.rsqrt(jnp.mean(centred * centred, axis=0, keepdims=True) + EPS)
        standard = centred * scale
        inverse[...] = scale
        xhat[...] = standard
        normed[...] = (standard * column_of(gain)).astype(BF16)
        leaving[0].start()
        leaving[1].start()
        arriving[0].wait()
        qkv[...] = dot(qkv_weight_t[...], normed[...]).astype(BF16)
        leaving[2].start()

    sub = lax.broadcasted_iota(jnp.int32, (HEAD, PATCH), 0)
    spot = lax.broadcasted_iota(jnp.int32, (HEAD, PATCH), 1)
    dead = jnp.where((sub == 0) & (spot >= length), -1e30, 0.0).astype(BF16)
    ones = jnp.where(sub == 0, 1.0, 0.0).astype(BF16)
    live = lax.broadcasted_iota(jnp.int32, (1, PATCH), 1) < length
    channels = HEADS * HEAD

    def scores_of(one):
        row = pl.multiple_of((step * GROUP + one) * HEAD, HEAD)
        query = (qkv[pl.ds(row, HEAD), :].astype(F32) * HEAD ** (-0.5)).astype(BF16)
        key = qkv[pl.ds(channels + row, HEAD), :]
        return dot(
            jnp.concatenate([key, dead], axis=0), jnp.concatenate([query, ones], axis=0), 0, 0
        )

    scores = scores_of(0)
    for one in range(GROUP):
        following = scores_of(one + 1) if one + 1 < GROUP else None
        row = pl.multiple_of((step * GROUP + one) * HEAD, HEAD)
        value = qkv[pl.ds(2 * channels + row, HEAD), :]
        raised = jnp.exp(scores - jnp.max(scores, axis=0, keepdims=True)).astype(BF16)
        probs[one] = raised
        out = dot(jnp.concatenate([value, ones], axis=0), raised)
        over = 1.0 / out[HEAD : HEAD + 1]
        recip[one] = over
        heads[pl.ds(row, HEAD), :] = jnp.where(live, out[:HEAD] * over, 0.0).astype(BF16)
        scores = following

    @pl.when(step == pl.num_programs(0) - 1)
    def _():
        packed[...] = jnp.zeros_like(packed)
        arriving[1].wait()
        attended[...] = dot(heads[...], proj_weight[...], 0, 0).astype(BF16)
        for block in range(BLOCKS):
            source, slot = source_of(dest, block, scenes)
            rows = pl.ds(pl.multiple_of(slot * BLOCK, BLOCK), BLOCK)
            packed[source] = attended[rows, :]
        for copy in leaving:
            copy.wait()


def backward_kernel(
    dest, lengths, got_cot, probs, recip, qkv, normed, xhat, inverse, heads, gain,
    qkv_weight, proj_weight,
    packed, sent, kept,
    d_qkv, d_rows, d_heads, part, normed_here, xhat_here, weight_here, arrivals,
):
    step = pl.program_id(0)
    scenes = packed.shape[0]
    channels = HEADS * HEAD

    late = [
        pltpu.make_async_copy(far, near, arrivals.at[at])
        for at, (far, near) in enumerate(
            ((normed, normed_here), (xhat, xhat_here), (qkv_weight, weight_here))
        )
    ]

    @pl.when(step == 0)
    def _():
        for copy in late:
            copy.start()
        for block in range(BLOCKS):
            source, slot = source_of(dest, block, scenes)
            rows = pl.ds(pl.multiple_of(slot * BLOCK, BLOCK), BLOCK)
            d_rows[rows, :] = got_cot[source]
        live = lax.broadcasted_iota(jnp.int32, (1, PATCH), 1) < lengths[0, 0]
        d_full = dot(proj_weight[...], d_rows[...], 1, 1)
        d_heads[...] = jnp.where(live, d_full, 0.0).astype(BF16)
        part[...] = dot(heads[...], d_rows[...]).astype(BF16)
        split_parts(part, [sent.at[3], kept.at[3]])

    sub = lax.broadcasted_iota(jnp.int32, (HEAD, PATCH), 0)
    ones = jnp.where(sub < 3, 1.0, 0.0).astype(BF16)

    def d_probs_of(one):
        row = pl.multiple_of((step * GROUP + one) * HEAD, HEAD)
        value = qkv[pl.ds(2 * channels + row, HEAD), :]
        d_out = d_heads[pl.ds(row, HEAD), :]
        row_dot = jnp.sum(
            d_out.astype(F32) * heads[pl.ds(row, HEAD), :].astype(F32), axis=0, keepdims=True
        )
        first = row_dot.astype(BF16).astype(F32)
        second = (row_dot - first).astype(BF16).astype(F32)
        third = row_dot - first - second
        split = jnp.where(sub == 0, first, jnp.where(sub == 1, second, third))
        minus = jnp.where(sub < 3, -split, 0.0).astype(BF16)
        return dot(
            jnp.concatenate([value, ones], axis=0), jnp.concatenate([d_out, minus], axis=0), 0, 0
        )

    d_probs = d_probs_of(0)
    for one in range(GROUP):
        following = d_probs_of(one + 1) if one + 1 < GROUP else None
        row = pl.multiple_of((step * GROUP + one) * HEAD, HEAD)
        query = qkv[pl.ds(row, HEAD), :].astype(F32)
        key = qkv[pl.ds(channels + row, HEAD), :]
        over = recip[one]
        raised = probs[one]
        d_scores = (raised.astype(F32) * d_probs).astype(BF16)
        d_out = (d_heads[pl.ds(row, HEAD), :].astype(F32) * over).astype(BF16)
        d_qkv[pl.ds(2 * channels + row, HEAD), :] = dot(d_out, raised, 1, 1).astype(BF16)
        scaled = over * HEAD ** (-0.5)
        d_qkv[pl.ds(row, HEAD), :] = (dot(key, d_scores) * scaled).astype(BF16)
        d_key = dot((query * scaled).astype(BF16), d_scores, 1, 1)
        d_qkv[pl.ds(channels + row, HEAD), :] = d_key.astype(BF16)
        d_probs = following

    @pl.when(step == pl.num_programs(0) - 1)
    def _():
        for copy in late:
            copy.wait()
        spread = dot(weight_here[...], d_qkv[...]) * column_of(gain)
        standard = xhat_here[...]
        row_gradient = inverse[...] * (
            spread
            - jnp.mean(spread, axis=0, keepdims=True)
            - standard * jnp.mean(spread * standard, axis=0, keepdims=True)
        )
        d_rows[...] = row_gradient.T.astype(BF16)
        packed[...] = jnp.zeros_like(packed)
        for block in range(BLOCKS):
            source, slot = source_of(dest, block, scenes)
            packed[source] = d_rows[pl.ds(pl.multiple_of(slot * BLOCK, BLOCK), BLOCK), :]
        for third in range(3):
            columns = d_qkv[pl.ds(third * channels, channels), :]
            part[...] = dot(normed_here[...], columns, 1, 1).astype(BF16)
            split_parts(part, [sent.at[third], kept.at[third]])


def tile_parts_kernel(other, kept_far, *rest):
    count = lax.axis_size("dp")
    parts_far, (kept, parts, arrivals, departures) = rest[:count], rest[count:]
    rank = lax.axis_index("dp")
    groups = [lax.rem(rank + step, count) for step in range(count)]
    arriving = [
        pltpu.make_async_copy(kept_far.at[group], kept.at[step], arrivals.at[step])
        for step, group in enumerate(groups)
    ]
    for copy in arriving[1:] + arriving[:1]:
        copy.start()
    leaving = [
        pltpu.make_async_copy(parts.at[step], parts_far[step], departures.at[step])
        for step in range(count)
    ]
    for step in [*range(1, count), 0]:
        arriving[step].wait()
        parts[step] = (kept[step].astype(F32) + other[groups[step]].astype(F32)).astype(BF16)
        leaving[step].start()
    for copy in leaving:
        copy.wait()


def hidden_grad_kernel(dest, got, cot_far, d_hidden_far, cot, d_hidden_b, sems):
    arriving = pltpu.make_async_copy(cot_far, cot, sems.at[0])
    arriving.start()
    arriving.wait()
    for block in range(BLOCKS):
        rows = pl.ds(block * BLOCK, BLOCK)
        total = cot[rows, :].astype(F32) + got[target_of(dest, block)].astype(F32)
        d_hidden_b[rows, :] = total.astype(BF16)
    leaving = pltpu.make_async_copy(d_hidden_b, d_hidden_far, sems.at[1])
    leaving.start()
    leaving.wait()


def conv_grad_kernel(
    d_other, d_own_far, ours_far, others_far, q_part, out_far,
    d_own, ours, others, out, arrivals, departures,
):
    taps, chips, shard, rows = ours.shape
    arriving = [pltpu.make_async_copy(d_own_far, d_own, arrivals.at[TAPS, 0])]
    for tap in range(taps):
        arriving += [
            pltpu.make_async_copy(ours_far.at[tap], ours.at[tap], arrivals.at[tap, 0]),
            pltpu.make_async_copy(others_far.at[tap], others.at[tap], arrivals.at[tap, 1]),
        ]
    for copy in arriving:
        copy.start()
    out[TAPS] = q_part[...]
    leaving = [
        pltpu.make_async_copy(
            out.at[tap], out_far.at[:, pl.ds(tap * shard, shard)], departures.at[tap]
        )
        for tap in range(TAPS + 1)
    ]
    leaving[TAPS].start()
    arriving[0].wait()
    for tap in range(taps):
        arriving[1 + 2 * tap].wait()
        arriving[2 + 2 * tap].wait()
        part = dot(ours[tap].reshape(chips * shard, rows), d_own[...])
        part = part + dot(others[tap].reshape(chips * shard, rows), d_other[...])
        out[tap] = part.astype(BF16).reshape(chips, shard, part.shape[1])
        leaving[tap].start()
    for copy in leaving:
        copy.wait()


def feat_grad_kernel(
    dest, nearby, d_hidden_b, weight, cot, got_dz, hidden, got,
    kept, to_previous, to_next, block_out, spread, landed,
):
    spots = lax.broadcasted_iota(jnp.int32, (HALO, 3 * HALO), 0)
    landing = PATCH // HALO + 2
    landed[...] = jnp.zeros_like(landed)
    for tap in range(1, TAPS):
        for part in range(landing):
            start, stop = max(0, part - 2) * HALO, min(PATCH // HALO, part + 1) * HALO
            index = nearby[pl.ds(tap, 1), pl.ds(start, stop - start)] - part * HALO
            chosen = jnp.where(spots[:, : stop - start] == index, 1.0, 0.0).astype(BF16)
            spread[pl.ds(part * HALO, HALO), :] = dot(
                chosen, d_hidden_b[pl.ds(start, stop - start), :]
            ).astype(BF16)
        landed[...] += dot(spread[...], weight[tap], 1, 1)
    to_previous[...] = landed[0:HALO, :].astype(BF16)
    to_next[...] = landed[HALO + PATCH :, :].astype(BF16)
    landed[HALO : HALO + PATCH, :] += dot(d_hidden_b[...], weight[0], 1, 1)
    for block in range(BLOCKS):
        rows = pl.ds(block * BLOCK, BLOCK)
        d_hidden = cot[rows, :].astype(F32) + got_dz[target_of(dest, block)].astype(F32)
        kept[rows, :] = d_hidden + landed[pl.ds(HALO + block * BLOCK, BLOCK), :]
        block_out[rows, :] = (
            hidden[target_of(dest, block)].astype(F32) + got[target_of(dest, block)].astype(F32)
        ).astype(BF16)


def last_kernel(
    rank, mine, first, second, third, conv_far, qkv_far, proj_far, conv_grad, qkv_grad, proj_grad,
    sems,
):
    arrived = [mine, first, second, third]
    shard = proj_grad.shape[0]
    channels = proj_grad.shape[1]
    for tap in range(TAPS):
        rows = pl.ds(tap * shard, shard)
        conv_grad[tap] = sum(one[rows, :].astype(F32) for one in arrived)
    copies = [
        pltpu.make_async_copy(near, far, sems.at[at])
        for at, (near, far) in enumerate(
            ((conv_grad, conv_far), (qkv_grad, qkv_far), (proj_grad, proj_far))
        )
    ]
    copies[0].start()
    for step, one in enumerate(arrived):
        block = one[pl.ds(TAPS * shard, shard), :].astype(F32)
        origin = lax.rem(rank[0] - step + len(arrived), len(arrived))
        for third_at in range(3):
            @pl.when(origin == third_at)
            def _(block=block, third_at=third_at):
                qkv_grad[:, pl.ds(third_at * channels, channels)] = block

        @pl.when(origin == 3)
        def _(block=block):
            proj_grad[...] = block
    copies[1].start()
    copies[2].start()
    for copy in copies:
        copy.wait()


def halo(first, last, axis):
    count = lax.axis_size(axis)
    forward = [(i, i + 1) for i in range(count - 1)]
    backward = [(i + 1, i) for i in range(count - 1)]
    return lax.ppermute(last, axis, forward), lax.ppermute(first, axis, backward)


def moved(packed):
    return lax.all_to_all(packed, SCENE, split_axis=0, concat_axis=0, tiled=True)


def summed(parts, axis, dtype=BF16):
    got = lax.all_to_all(parts, axis, split_axis=0, concat_axis=0, tiled=True)
    return jnp.sum(got.astype(F32), axis=0).astype(dtype)


def across_tiles(parts):
    count = len(parts)
    return [
        lax.ppermute(parts[step], "dp", [(i, (i + step) % count) for i in range(count)])
        for step in range(1, count)
    ]


def from_others(mine):
    count = lax.axis_size("dp")
    return [
        lax.ppermute(mine, "dp", [(i, (i + step) % count) for i in range(count)])
        for step in range(1, count)
    ]


def grid_call(
    kernel, ins, in_specs, outs, out_specs, scratch, flops, bytes_moved, exps,
    steps=HEADS // GROUP,
):
    return pl.pallas_call(
        kernel,
        grid=(steps,),
        out_shape=[jax.ShapeDtypeStruct(shape, dtype) for shape, dtype in outs],
        in_specs=in_specs,
        out_specs=out_specs,
        scratch_shapes=scratch,
        compiler_params=pltpu.CompilerParams(
            vmem_limit_bytes=VMEM_LIMIT, dimension_semantics=("arbitrary",)
        ),
        cost_estimate=pl.CostEstimate(
            flops=flops, bytes_accessed=bytes_moved, transcendentals=exps
        ),
    )(*ins)


def body(
    points_feat, neighbours, block_dest, lengths, conv_weight, norm_gain, qkv_weight, proj_weight,
    out_grad,
):
    feats = points_feat[0]
    cotangent = out_grad[0]
    nearby = neighbours[0]
    dest = block_dest[0]
    channels = feats.shape[1]
    scenes = lax.axis_size(SCENE)
    gain = norm_gain[None, :]
    rows_c = (PATCH, channels)
    square = (channels, channels)
    slots = (scenes, BLOCK, channels)

    low, high = halo(feats[:HALO], feats[PATCH - HALO :], SCENE)
    half = (2 * HALO, channels)
    work = PATCH * channels * (TAPS * channels + 9 * HALO)
    turned = nearby.T
    (inner_hidden,) = call(
        inner_kernel, [(half, BF16)], [feats, turned, conv_weight], flops=work, moved=4 << 20,
    )
    weights = (TAPS,) + square
    (packed_hidden,) = own_call(
        outer_kernel, [(slots, BF16)],
        [dest, low, feats, high, turned, conv_weight, inner_hidden], "svavvaa",
        [pltpu.VMEM(rows_c, BF16), pltpu.VMEM(weights, BF16), pltpu.VMEM(rows_c, BF16),
         pltpu.VMEM(slots, BF16), pltpu.SemaphoreType.DMA((2 + TAPS,)),
         pltpu.SemaphoreType.DMA((1,))],
        limit=20 << 20, flops=work, moved=5 << 20,
    )
    got_hidden = moved(packed_hidden)
    cot_after, _ = lax.optimization_barrier((cotangent, packed_hidden))
    chips = scenes // 2
    shard = channels // scenes
    halves = (TAPS, chips, shard, PATCH)
    packed_cot, theirs, ours, qkv_weight_t = call(
        pack_kernel,
        [(slots, BF16), (halves, BF16), (halves, BF16), ((3 * channels, channels), BF16)],
        [dest, cot_after, low, feats, high, turned, qkv_weight], smem=1, moved=8 << 20,
        scratch=[pltpu.VMEM(weights, BF16)],
    )
    others = lax.ppermute(theirs, "core", [(0, 1), (1, 0)])
    got_cot = moved(packed_cot)
    probs_shape = (HEADS, PATCH, PATCH)
    recip_shape = (HEADS, 1, PATCH)
    smem = pl.BlockSpec(memory_space=pltpu.SMEM)
    far = pl.BlockSpec(memory_space=pl.ANY)
    pair = HEADS * PATCH * PATCH
    packed_att, probs, recip, qkv, normed, xhat, inverse, heads = grid_call(
        forward_kernel,
        [dest, lengths, got_hidden, gain, qkv_weight_t, proj_weight],
        [smem, smem, whole(slots), whole((1, channels)), far, far],
        [(slots, BF16), (probs_shape, BF16), (recip_shape, F32), ((3 * channels, PATCH), BF16),
         ((channels, PATCH), BF16), ((channels, PATCH), F32), ((1, PATCH), F32),
         ((channels, PATCH), BF16)],
        [whole(slots), per_group((GROUP, PATCH, PATCH)), per_group((GROUP, 1, PATCH)),
         far, far, far, whole((1, PATCH)), whole((channels, PATCH))],
        [pltpu.VMEM(rows_c, F32), pltpu.VMEM(rows_c, BF16),
         pltpu.VMEM((3 * channels, channels), BF16), pltpu.VMEM(square, BF16),
         pltpu.VMEM((3 * channels, PATCH), BF16), pltpu.VMEM((channels, PATCH), BF16),
         pltpu.VMEM((channels, PATCH), F32), pltpu.SemaphoreType.DMA((2,)),
         pltpu.SemaphoreType.DMA((3,))],
        flops=2 * pair * 64 * 8, bytes_moved=32 << 20, exps=pair,
    )
    got_att = moved(packed_att)
    parts_shape = (4, chips, shard, channels)
    packed_dz, sent, kept = grid_call(
        backward_kernel,
        [dest, lengths, got_cot, probs, recip, qkv, normed, xhat, inverse, heads, gain, qkv_weight,
         proj_weight],
        [smem, smem, whole(slots), per_group((GROUP, PATCH, PATCH)), per_group((GROUP, 1, PATCH)),
         whole((3 * channels, PATCH)), far, far, whole((1, PATCH)), whole((channels, PATCH)),
         whole((1, channels)), far, whole(square)],
        [(slots, BF16), (parts_shape, BF16), (parts_shape, BF16)],
        [whole(slots), whole(parts_shape), whole(parts_shape)],
        [pltpu.VMEM((3 * channels, PATCH), BF16), pltpu.VMEM(rows_c, BF16),
         pltpu.VMEM((channels, PATCH), BF16), pltpu.VMEM(square, BF16),
         pltpu.VMEM((channels, PATCH), BF16), pltpu.VMEM((channels, PATCH), F32),
         pltpu.VMEM((channels, 3 * channels), BF16), pltpu.SemaphoreType.DMA((3,))],
        flops=4 * pair * 64 * 8, bytes_moved=32 << 20, exps=0,
    )
    packed_dz, got_att = lax.optimization_barrier((packed_dz, got_att))
    got_dz = moved(packed_dz)
    tile_rows = own_call(
        tile_parts_kernel, [((chips, shard, channels), BF16)] * 4,
        [lax.ppermute(sent, "core", [(0, 1), (1, 0)]), kept], "va",
        [pltpu.VMEM(parts_shape, BF16), pltpu.VMEM(parts_shape, BF16),
         pltpu.SemaphoreType.DMA((4,)), pltpu.SemaphoreType.DMA((4,))],
        limit=8 << 20, moved=3 << 20,
    )
    got_dz, received = lax.optimization_barrier((got_dz, across_tiles(tile_rows)))
    mine = sum(one.astype(F32) for one in [tile_rows[0]] + received).astype(BF16)
    (d_hidden_b,) = own_call(
        hidden_grad_kernel, [(rows_c, BF16)], [dest, got_dz, cotangent], "sva",
        [pltpu.VMEM(rows_c, BF16), pltpu.VMEM(rows_c, BF16), pltpu.SemaphoreType.DMA((2,))],
        limit=8 << 20, moved=2 << 20,
    )
    d_other = lax.ppermute(d_hidden_b, "core", [(0, 1), (1, 0)])
    rows_here = TAPS * shard
    (chip_parts,) = own_call(
        conv_grad_kernel, [((chips, rows_here + shard, channels), BF16)],
        [d_other, d_hidden_b, ours, others, mine], "vaaav",
        [pltpu.VMEM(rows_c, BF16), pltpu.VMEM(halves, BF16), pltpu.VMEM(halves, BF16),
         pltpu.VMEM((TAPS + 1, chips, shard, channels), BF16),
         pltpu.SemaphoreType.DMA((TAPS + 1, 2)), pltpu.SemaphoreType.DMA((TAPS + 1,))],
        limit=20 << 20, flops=2 * TAPS * PATCH * channels * channels, moved=8 << 20,
    )
    total = summed(chip_parts, ("x", "z"))
    edge = (HALO, channels)
    feat_kept, to_previous, to_next, block_out = call(
        feat_grad_kernel, [(rows_c, F32), (edge, BF16), (edge, BF16), (rows_c, BF16)],
        [dest, turned, d_hidden_b, conv_weight, cotangent, got_dz, packed_hidden, got_att],
        smem=1, flops=3 * work, moved=8 << 20,
        scratch=[
            pltpu.VMEM((PATCH + 2 * HALO, channels), BF16),
            pltpu.VMEM((PATCH + 2 * HALO, channels), F32),
        ],
    )
    from_previous, from_next = halo(to_previous, to_next, SCENE)
    total, feat_kept, block_out = lax.optimization_barrier((total, feat_kept, block_out))
    arrived = from_others(total)
    zero = jnp.zeros((), BF16)
    top = lax.pad(from_previous, zero, ((0, PATCH - HALO, 0), (0, 0, 0)))
    bottom = lax.pad(from_next, zero, ((PATCH - HALO, 0, 0), (0, 0, 0)))
    feat_grad = (feat_kept + top.astype(F32) + bottom.astype(F32)).astype(BF16)
    rank = lax.axis_index("dp").astype(jnp.int32)
    near = pl.BlockSpec(memory_space=pltpu.VMEM)
    grads = [(TAPS, shard, channels), (shard, 3 * channels), (shard, channels)]
    conv_grad, qkv_grad, proj_grad = pl.pallas_call(
        last_kernel,
        out_shape=[jax.ShapeDtypeStruct(shape, F32) for shape in grads],
        in_specs=[smem] + [near] * 4,
        out_specs=[far] * 3,
        scratch_shapes=[pltpu.VMEM(shape, F32) for shape in grads]
        + [pltpu.SemaphoreType.DMA((3,))],
        compiler_params=pltpu.CompilerParams(vmem_limit_bytes=8 << 20),
        cost_estimate=pl.CostEstimate(flops=1 << 20, bytes_accessed=1 << 20, transcendentals=0),
    )(rank[None], total, *arrived)
    return (block_out[None], feat_grad[None], conv_grad, qkv_grad, proj_grad)


def solution(mesh):
    fine = Mesh(mesh.devices.reshape(4, 4, 2, 4), ("x", "z", "core", "dp"))
    return jax.shard_map(
        body,
        mesh=fine,
        in_specs=(
            P("dp", SCENE, None),
            P("dp", SCENE, None),
            P("dp", None),
            P("dp", SCENE),
            P(),
            P(),
            P(),
            P(),
            P("dp", SCENE, None),
        ),
        out_specs=(
            P("dp", SCENE, None),
            P("dp", SCENE, None),
            P(None, SCENE, None),
            P(SCENE, None),
            P(SCENE, None),
        ),
        check_vma=False,
    )
```

```python
import jax
import jax.numpy as jnp
from jax import lax
from jax.experimental import pallas as pl
from jax.experimental.pallas import tpu as pltpu
from jax.sharding import Mesh
from jax.sharding import PartitionSpec as P

HEADS = 32
HEAD = 16
PATCH = 512
BLOCK = 32
BLOCKS = 16
HALO = 128
TAPS = 4
GROUP = 4
EPS = 1e-05
F32 = jnp.float32
BF16 = jnp.bfloat16
SCENE = ("x", "z", "core")


def dot(left, right, left_dim=1, right_dim=0):
    return lax.dot_general(
        left, right, (((left_dim,), (right_dim,)), ((), ())), preferred_element_type=F32
    )


VMEM_LIMIT = 60 << 20


def whole(shape):
    return pl.BlockSpec(shape, lambda step: (0,) * len(shape))


def per_group(shape):
    return pl.BlockSpec(shape, lambda step: (step,) + (0,) * (len(shape) - 1))


def call(kernel, outs, operands, smem=0, flops=0, moved=0, scratch=(), limit=VMEM_LIMIT):
    in_specs = [pl.BlockSpec(memory_space=pltpu.SMEM)] * smem
    in_specs += [whole(operand.shape) for operand in operands[smem:]]
    return pl.pallas_call(
        kernel,
        grid=(1,),
        out_shape=[jax.ShapeDtypeStruct(shape, dtype) for shape, dtype in outs],
        in_specs=in_specs,
        out_specs=[whole(shape) for shape, _ in outs],
        scratch_shapes=list(scratch),
        compiler_params=pltpu.CompilerParams(
            vmem_limit_bytes=limit, dimension_semantics=("arbitrary",)
        ),
        cost_estimate=pl.CostEstimate(flops=flops, bytes_accessed=moved, transcendentals=0),
    )(*operands)


def own_call(kernel, outs, operands, kinds, scratch, limit, flops=0, moved=0):
    spaces = {"s": pltpu.SMEM, "v": pltpu.VMEM, "a": pltpu.HBM}
    return pl.pallas_call(
        kernel,
        out_shape=[jax.ShapeDtypeStruct(shape, dtype) for shape, dtype in outs],
        in_specs=[pl.BlockSpec(memory_space=spaces[kind]) for kind in kinds],
        out_specs=[pl.BlockSpec(memory_space=pltpu.HBM)] * len(outs),
        scratch_shapes=scratch,
        compiler_params=pltpu.CompilerParams(vmem_limit_bytes=limit),
        cost_estimate=pl.CostEstimate(flops=flops, bytes_accessed=moved, transcendentals=0),
    )(*operands)


def scene_index():
    index = lax.axis_index(SCENE[0])
    for axis in SCENE[1:]:
        index = index * lax.axis_size(axis) + lax.axis_index(axis)
    return index


def target_of(dest, block):
    return dest[scene_index() * BLOCKS + block] // BLOCKS


def source_of(dest, block, scenes):
    shift = dest[block] // BLOCKS
    source = lax.rem(scene_index() - shift + scenes, scenes)
    return source, lax.rem(dest[source * BLOCKS + block], BLOCKS)


def split_parts(part, halves):
    core = lax.axis_index("core")
    shard = part.shape[0] // halves[0].shape[0] // 2
    for pair in range(halves[0].shape[0]):
        for half, owner in zip(halves, (1 - core, core)):
            start = pl.multiple_of((2 * pair + owner) * shard, shard)
            half[pair] = part[pl.ds(start, shard), :]


def column_of(row):
    return jnp.broadcast_to(row[...], (8, row.shape[1])).T[:, 0:1]


def columns_of(index):
    padded = jnp.concatenate([index, jnp.zeros((8 - TAPS, index.shape[1]), F32)], axis=0)
    return padded.T


def picked_rows(part, window, columns, tap):
    spots = lax.broadcasted_iota(jnp.int32, (HALO, 3 * HALO), 1).astype(F32)
    index = columns[part * HALO : (part + 1) * HALO, tap : tap + 1] - part * HALO
    return dot(jnp.where(spots == index, 1.0, 0.0).astype(BF16), window).astype(BF16)


def window_of(part, low, feats, high):
    if part == 0:
        return jnp.concatenate([low[...], feats[0 : 2 * HALO, :]], axis=0)
    if part == PATCH // HALO - 1:
        return jnp.concatenate([feats[PATCH - 2 * HALO :, :], high[...]], axis=0)
    return feats[pl.ds((part - 1) * HALO, 3 * HALO), :]


def conv_rows(part, own, window, columns, weight):
    total = own.astype(F32) + dot(own, weight[0])
    for tap in range(1, TAPS):
        total = total + dot(picked_rows(part, window, columns, tap), weight[tap])
    return total.astype(BF16)


def inner_kernel(feats, nearby, weight, hidden):
    columns = columns_of(nearby[...].astype(F32))
    for part in (1, 2):
        hidden[pl.ds((part - 1) * HALO, HALO), :] = conv_rows(
            part, feats[pl.ds(part * HALO, HALO), :], window_of(part, None, feats, None),
            columns, weight,
        )


def outer_kernel(
    dest, low, feats_far, high, nearby, weight_far, inner_far,
    packed_far,
    feats, weight, hidden, packed, arrivals, departures,
):
    middle = pl.ds(HALO, 2 * HALO)
    arriving = [
        pltpu.make_async_copy(feats_far, feats, arrivals.at[0]),
        pltpu.make_async_copy(inner_far, hidden.at[middle], arrivals.at[1]),
    ] + [
        pltpu.make_async_copy(weight_far.at[tap], weight.at[tap], arrivals.at[2 + tap])
        for tap in range(TAPS)
    ]
    for copy in arriving:
        copy.start()
    packed[...] = jnp.zeros_like(packed)
    columns = columns_of(nearby[...].astype(F32))
    arriving[0].wait()
    for at, part in enumerate((0, 3)):
        rows = pl.ds(part * HALO, HALO)
        window = window_of(part, low, feats, high)
        own = feats[rows, :]
        picked = [own] + [picked_rows(part, window, columns, tap) for tap in range(1, TAPS)]
        total = own.astype(F32)
        for tap in range(TAPS):
            if at == 0:
                arriving[2 + tap].wait()
            total = total + dot(picked[tap], weight[tap])
        hidden[rows, :] = total.astype(BF16)
    arriving[1].wait()
    for block in range(BLOCKS):
        packed[target_of(dest, block)] = hidden[pl.ds(block * BLOCK, BLOCK), :]
    leaving = pltpu.make_async_copy(packed, packed_far, departures.at[0])
    leaving.start()
    leaving.wait()


def pack_kernel(
    dest, blocks, low, feats, high, nearby, qkv_weight, packed, theirs, ours, qkv_weight_t,
    gathered_t,
):
    packed[...] = jnp.zeros_like(packed)
    for block in range(BLOCKS):
        packed[target_of(dest, block)] = blocks[pl.ds(block * BLOCK, BLOCK), :]
    columns = columns_of(nearby[...].astype(F32))
    gathered_t[0] = feats[...].T
    for part in range(PATCH // HALO):
        window = window_of(part, low, feats, high)
        for tap in range(1, TAPS):
            picked = picked_rows(part, window, columns, tap)
            gathered_t[tap, :, pl.ds(part * HALO, HALO)] = picked.T
    for tap in range(TAPS):
        split_parts(gathered_t.at[tap], [theirs.at[tap], ours.at[tap]])
    qkv_weight_t[...] = qkv_weight[...].T


def forward_kernel(
    dest, lengths, got, gain, weight_far, proj_far,
    packed, probs, recip, qkv_far, normed_far, xhat_far, inverse, heads,
    rows_f, attended, qkv_weight_t, proj_weight, qkv, normed, xhat, arrivals, departures,
):
    step = pl.program_id(0)
    arriving = [
        pltpu.make_async_copy(far, near, arrivals.at[at])
        for at, (far, near) in enumerate(((weight_far, qkv_weight_t), (proj_far, proj_weight)))
    ]
    leaving = [
        pltpu.make_async_copy(near, far, departures.at[at])
        for at, (near, far) in enumerate(
            ((xhat, xhat_far), (normed, normed_far), (qkv, qkv_far))
        )
    ]
    scenes = got.shape[0]
    length = lengths[0, 0]

    @pl.when(step == 0)
    def _():
        for copy in arriving:
            copy.start()
        for block in range(BLOCKS):
            source, slot = source_of(dest, block, scenes)
            rows = pl.ds(pl.multiple_of(slot * BLOCK, BLOCK), BLOCK)
            rows_f[rows, :] = got[source].astype(F32)
        rows_t = rows_f[...].T
        centred = rows_t - jnp.mean(rows_t, axis=0, keepdims=True)
        scale = lax.rsqrt(jnp.mean(centred * centred, axis=0, keepdims=True) + EPS)
        standard = centred * scale
        inverse[...] = scale
        xhat[...] = standard
        normed[...] = (standard * column_of(gain)).astype(BF16)
        leaving[0].start()
        leaving[1].start()
        arriving[0].wait()
        qkv[...] = dot(qkv_weight_t[...], normed[...]).astype(BF16)
        leaving[2].start()

    sub = lax.broadcasted_iota(jnp.int32, (HEAD, PATCH), 0)
    spot = lax.broadcasted_iota(jnp.int32, (HEAD, PATCH), 1)
    dead = jnp.where((sub == 0) & (spot >= length), -1e30, 0.0).astype(BF16)
    ones = jnp.where(sub == 0, 1.0, 0.0).astype(BF16)
    live = lax.broadcasted_iota(jnp.int32, (1, PATCH), 1) < length
    channels = HEADS * HEAD

    def scores_of(one):
        row = pl.multiple_of((step * GROUP + one) * HEAD, HEAD)
        query = (qkv[pl.ds(row, HEAD), :].astype(F32) * HEAD ** (-0.5)).astype(BF16)
        key = qkv[pl.ds(channels + row, HEAD), :]
        return dot(
            jnp.concatenate([key, dead], axis=0), jnp.concatenate([query, ones], axis=0), 0, 0
        )

    scores = scores_of(0)
    for one in range(GROUP):
        following = scores_of(one + 1) if one + 1 < GROUP else None
        row = pl.multiple_of((step * GROUP + one) * HEAD, HEAD)
        value = qkv[pl.ds(2 * channels + row, HEAD), :]
        raised = jnp.exp(scores - jnp.max(scores, axis=0, keepdims=True)).astype(BF16)
        probs[one] = raised
        out = dot(jnp.concatenate([value, ones], axis=0), raised)
        over = 1.0 / out[HEAD : HEAD + 1]
        recip[one] = over
        heads[pl.ds(row, HEAD), :] = jnp.where(live, out[:HEAD] * over, 0.0).astype(BF16)
        scores = following

    @pl.when(step == pl.num_programs(0) - 1)
    def _():
        packed[...] = jnp.zeros_like(packed)
        arriving[1].wait()
        attended[...] = dot(heads[...], proj_weight[...], 0, 0).astype(BF16)
        for block in range(BLOCKS):
            source, slot = source_of(dest, block, scenes)
            rows = pl.ds(pl.multiple_of(slot * BLOCK, BLOCK), BLOCK)
            packed[source] = attended[rows, :]
        for copy in leaving:
            copy.wait()


def backward_kernel(
    dest, lengths, got_cot, probs, recip, qkv, normed, xhat, inverse, heads, gain,
    qkv_weight, proj_weight,
    packed_far, sent_far, kept_far,
    d_qkv, d_rows, d_heads, part, normed_here, xhat_here, weight_here, arrivals,
    packed, sent, kept, departures,
):
    step = pl.program_id(0)
    scenes = packed.shape[0]
    leaving = [
        pltpu.make_async_copy(near.at[at], far.at[at], departures.at[at, half])
        for at in range(sent.shape[0])
        for half, (near, far) in enumerate(((sent, sent_far), (kept, kept_far)))
    ]
    leaving.append(pltpu.make_async_copy(packed, packed_far, departures.at[sent.shape[0], 0]))
    channels = HEADS * HEAD

    late = [
        pltpu.make_async_copy(far, near, arrivals.at[at])
        for at, (far, near) in enumerate(
            ((normed, normed_here), (xhat, xhat_here), (qkv_weight, weight_here))
        )
    ]

    @pl.when(step == 0)
    def _():
        for copy in late:
            copy.start()
        for block in range(BLOCKS):
            source, slot = source_of(dest, block, scenes)
            rows = pl.ds(pl.multiple_of(slot * BLOCK, BLOCK), BLOCK)
            d_rows[rows, :] = got_cot[source]
        live = lax.broadcasted_iota(jnp.int32, (1, PATCH), 1) < lengths[0, 0]
        d_full = dot(proj_weight[...], d_rows[...], 1, 1)
        d_heads[...] = jnp.where(live, d_full, 0.0).astype(BF16)
        part[...] = dot(heads[...], d_rows[...]).astype(BF16)
        split_parts(part, [sent.at[3], kept.at[3]])
        leaving[6].start()
        leaving[7].start()

    sub = lax.broadcasted_iota(jnp.int32, (HEAD, PATCH), 0)
    ones = jnp.where(sub < 3, 1.0, 0.0).astype(BF16)

    def d_probs_of(one):
        row = pl.multiple_of((step * GROUP + one) * HEAD, HEAD)
        value = qkv[pl.ds(2 * channels + row, HEAD), :]
        d_out = d_heads[pl.ds(row, HEAD), :]
        row_dot = jnp.sum(
            d_out.astype(F32) * heads[pl.ds(row, HEAD), :].astype(F32), axis=0, keepdims=True
        )
        first = row_dot.astype(BF16).astype(F32)
        second = (row_dot - first).astype(BF16).astype(F32)
        third = row_dot - first - second
        split = jnp.where(sub == 0, first, jnp.where(sub == 1, second, third))
        minus = jnp.where(sub < 3, -split, 0.0).astype(BF16)
        return dot(
            jnp.concatenate([value, ones], axis=0), jnp.concatenate([d_out, minus], axis=0), 0, 0
        )

    d_probs = d_probs_of(0)
    for one in range(GROUP):
        following = d_probs_of(one + 1) if one + 1 < GROUP else None
        row = pl.multiple_of((step * GROUP + one) * HEAD, HEAD)
        query = qkv[pl.ds(row, HEAD), :].astype(F32)
        key = qkv[pl.ds(channels + row, HEAD), :]
        over = recip[one]
        raised = probs[one]
        d_scores = (raised.astype(F32) * d_probs).astype(BF16)
        d_out = (d_heads[pl.ds(row, HEAD), :].astype(F32) * over).astype(BF16)
        d_qkv[pl.ds(2 * channels + row, HEAD), :] = dot(d_out, raised, 1, 1).astype(BF16)
        scaled = over * HEAD ** (-0.5)
        d_qkv[pl.ds(row, HEAD), :] = (dot(key, d_scores) * scaled).astype(BF16)
        d_key = dot((query * scaled).astype(BF16), d_scores, 1, 1)
        d_qkv[pl.ds(channels + row, HEAD), :] = d_key.astype(BF16)
        d_probs = following

    @pl.when(step == pl.num_programs(0) - 1)
    def _():
        for copy in late:
            copy.wait()
        spread = dot(weight_here[...], d_qkv[...]) * column_of(gain)
        standard = xhat_here[...]
        row_gradient = inverse[...] * (
            spread
            - jnp.mean(spread, axis=0, keepdims=True)
            - standard * jnp.mean(spread * standard, axis=0, keepdims=True)
        )
        d_rows[...] = row_gradient.T.astype(BF16)
        packed[...] = jnp.zeros_like(packed)
        for block in range(BLOCKS):
            source, slot = source_of(dest, block, scenes)
            packed[source] = d_rows[pl.ds(pl.multiple_of(slot * BLOCK, BLOCK), BLOCK), :]
        leaving[8].start()
        for third in range(3):
            columns = d_qkv[pl.ds(third * channels, channels), :]
            part[...] = dot(normed_here[...], columns, 1, 1).astype(BF16)
            split_parts(part, [sent.at[third], kept.at[third]])
            leaving[2 * third].start()
            leaving[2 * third + 1].start()
        for copy in leaving:
            copy.wait()


def tile_parts_kernel(other, kept_far, *rest):
    count = lax.axis_size("dp")
    parts_far, (kept, parts, arrivals, departures) = rest[:count], rest[count:]
    rank = lax.axis_index("dp")
    groups = [lax.rem(rank + step, count) for step in range(count)]
    arriving = [
        pltpu.make_async_copy(kept_far.at[group], kept.at[step], arrivals.at[step])
        for step, group in enumerate(groups)
    ]
    for copy in arriving[1:] + arriving[:1]:
        copy.start()
    leaving = [
        pltpu.make_async_copy(parts.at[step], parts_far[step], departures.at[step])
        for step in range(count)
    ]
    for step in [*range(1, count), 0]:
        arriving[step].wait()
        parts[step] = (kept[step].astype(F32) + other[groups[step]].astype(F32)).astype(BF16)
        leaving[step].start()
    for copy in leaving:
        copy.wait()


def hidden_grad_kernel(dest, got, cot_far, d_hidden_far, cot, d_hidden_b, sems):
    arriving = pltpu.make_async_copy(cot_far, cot, sems.at[0])
    arriving.start()
    arriving.wait()
    for block in range(BLOCKS):
        rows = pl.ds(block * BLOCK, BLOCK)
        total = cot[rows, :].astype(F32) + got[target_of(dest, block)].astype(F32)
        d_hidden_b[rows, :] = total.astype(BF16)
    leaving = pltpu.make_async_copy(d_hidden_b, d_hidden_far, sems.at[1])
    leaving.start()
    leaving.wait()


def conv_grad_kernel(
    d_other, d_own_far, ours_far, others_far, q_part, out_far,
    d_own, ours, others, out, arrivals, departures,
):
    taps, chips, shard, rows = ours.shape
    arriving = [pltpu.make_async_copy(d_own_far, d_own, arrivals.at[TAPS, 0])]
    for tap in range(taps):
        arriving += [
            pltpu.make_async_copy(ours_far.at[tap], ours.at[tap], arrivals.at[tap, 0]),
            pltpu.make_async_copy(others_far.at[tap], others.at[tap], arrivals.at[tap, 1]),
        ]
    for copy in arriving:
        copy.start()
    out[TAPS] = q_part[...]
    leaving = [
        pltpu.make_async_copy(
            out.at[tap], out_far.at[:, pl.ds(tap * shard, shard)], departures.at[tap]
        )
        for tap in range(TAPS + 1)
    ]
    leaving[TAPS].start()
    arriving[0].wait()
    for tap in range(taps):
        arriving[1 + 2 * tap].wait()
        arriving[2 + 2 * tap].wait()
        part = dot(ours[tap].reshape(chips * shard, rows), d_own[...])
        part = part + dot(others[tap].reshape(chips * shard, rows), d_other[...])
        out[tap] = part.astype(BF16).reshape(chips, shard, part.shape[1])
        leaving[tap].start()
    for copy in leaving:
        copy.wait()


def feat_grad_kernel(
    dest, nearby, d_hidden_b, weight, cot, got_dz, hidden, got,
    kept, to_previous, to_next, block_out, spread, landed,
):
    spots = lax.broadcasted_iota(jnp.int32, (HALO, 3 * HALO), 0)
    landing = PATCH // HALO + 2
    landed[...] = jnp.zeros_like(landed)
    for tap in range(1, TAPS):
        for part in range(landing):
            start, stop = max(0, part - 2) * HALO, min(PATCH // HALO, part + 1) * HALO
            index = nearby[pl.ds(tap, 1), pl.ds(start, stop - start)] - part * HALO
            chosen = jnp.where(spots[:, : stop - start] == index, 1.0, 0.0).astype(BF16)
            spread[pl.ds(part * HALO, HALO), :] = dot(
                chosen, d_hidden_b[pl.ds(start, stop - start), :]
            ).astype(BF16)
        landed[...] += dot(spread[...], weight[tap], 1, 1)
    to_previous[...] = landed[0:HALO, :].astype(BF16)
    to_next[...] = landed[HALO + PATCH :, :].astype(BF16)
    landed[HALO : HALO + PATCH, :] += dot(d_hidden_b[...], weight[0], 1, 1)
    for block in range(BLOCKS):
        rows = pl.ds(block * BLOCK, BLOCK)
        d_hidden = cot[rows, :].astype(F32) + got_dz[target_of(dest, block)].astype(F32)
        kept[rows, :] = d_hidden + landed[pl.ds(HALO + block * BLOCK, BLOCK), :]
        block_out[rows, :] = (
            hidden[target_of(dest, block)].astype(F32) + got[target_of(dest, block)].astype(F32)
        ).astype(BF16)


def last_kernel(
    rank, mine, first, second, third, conv_far, qkv_far, proj_far, conv_grad, qkv_grad, proj_grad,
    sems,
):
    arrived = [mine, first, second, third]
    shard = proj_grad.shape[0]
    channels = proj_grad.shape[1]
    for tap in range(TAPS):
        rows = pl.ds(tap * shard, shard)
        conv_grad[tap] = sum(one[rows, :].astype(F32) for one in arrived)
    copies = [
        pltpu.make_async_copy(near, far, sems.at[at])
        for at, (near, far) in enumerate(
            ((conv_grad, conv_far), (qkv_grad, qkv_far), (proj_grad, proj_far))
        )
    ]
    copies[0].start()
    for step, one in enumerate(arrived):
        block = one[pl.ds(TAPS * shard, shard), :].astype(F32)
        origin = lax.rem(rank[0] - step + len(arrived), len(arrived))
        for third_at in range(3):
            @pl.when(origin == third_at)
            def _(block=block, third_at=third_at):
                qkv_grad[:, pl.ds(third_at * channels, channels)] = block

        @pl.when(origin == 3)
        def _(block=block):
            proj_grad[...] = block
    copies[1].start()
    copies[2].start()
    for copy in copies:
        copy.wait()


def halo(first, last, axis):
    count = lax.axis_size(axis)
    forward = [(i, i + 1) for i in range(count - 1)]
    backward = [(i + 1, i) for i in range(count - 1)]
    return lax.ppermute(last, axis, forward), lax.ppermute(first, axis, backward)


def moved(packed):
    return lax.all_to_all(packed, SCENE, split_axis=0, concat_axis=0, tiled=True)


def summed(parts, axis, dtype=BF16):
    got = lax.all_to_all(parts, axis, split_axis=0, concat_axis=0, tiled=True)
    return jnp.sum(got.astype(F32), axis=0).astype(dtype)


def across_tiles(parts):
    count = len(parts)
    return [
        lax.ppermute(parts[step], "dp", [(i, (i + step) % count) for i in range(count)])
        for step in range(1, count)
    ]


def from_others(mine):
    count = lax.axis_size("dp")
    return [
        lax.ppermute(mine, "dp", [(i, (i + step) % count) for i in range(count)])
        for step in range(1, count)
    ]


def grid_call(
    kernel, ins, in_specs, outs, out_specs, scratch, flops, bytes_moved, exps,
    steps=HEADS // GROUP,
):
    return pl.pallas_call(
        kernel,
        grid=(steps,),
        out_shape=[jax.ShapeDtypeStruct(shape, dtype) for shape, dtype in outs],
        in_specs=in_specs,
        out_specs=out_specs,
        scratch_shapes=scratch,
        compiler_params=pltpu.CompilerParams(
            vmem_limit_bytes=VMEM_LIMIT, dimension_semantics=("arbitrary",)
        ),
        cost_estimate=pl.CostEstimate(
            flops=flops, bytes_accessed=bytes_moved, transcendentals=exps
        ),
    )(*ins)


def body(
    points_feat, neighbours, block_dest, lengths, conv_weight, norm_gain, qkv_weight, proj_weight,
    out_grad,
):
    feats = points_feat[0]
    cotangent = out_grad[0]
    nearby = neighbours[0]
    dest = block_dest[0]
    channels = feats.shape[1]
    scenes = lax.axis_size(SCENE)
    gain = norm_gain[None, :]
    rows_c = (PATCH, channels)
    square = (channels, channels)
    slots = (scenes, BLOCK, channels)

    low, high = halo(feats[:HALO], feats[PATCH - HALO :], SCENE)
    half = (2 * HALO, channels)
    work = PATCH * channels * (TAPS * channels + 9 * HALO)
    turned = nearby.T
    (inner_hidden,) = call(
        inner_kernel, [(half, BF16)], [feats, turned, conv_weight], flops=work, moved=4 << 20,
    )
    weights = (TAPS,) + square
    (packed_hidden,) = own_call(
        outer_kernel, [(slots, BF16)],
        [dest, low, feats, high, turned, conv_weight, inner_hidden], "svavvaa",
        [pltpu.VMEM(rows_c, BF16), pltpu.VMEM(weights, BF16), pltpu.VMEM(rows_c, BF16),
         pltpu.VMEM(slots, BF16), pltpu.SemaphoreType.DMA((2 + TAPS,)),
         pltpu.SemaphoreType.DMA((1,))],
        limit=20 << 20, flops=work, moved=5 << 20,
    )
    got_hidden = moved(packed_hidden)
    cot_after, _ = lax.optimization_barrier((cotangent, packed_hidden))
    chips = scenes // 2
    shard = channels // scenes
    halves = (TAPS, chips, shard, PATCH)
    packed_cot, theirs, ours, qkv_weight_t = call(
        pack_kernel,
        [(slots, BF16), (halves, BF16), (halves, BF16), ((3 * channels, channels), BF16)],
        [dest, cot_after, low, feats, high, turned, qkv_weight], smem=1, moved=8 << 20,
        scratch=[pltpu.VMEM(weights, BF16)],
    )
    others = lax.ppermute(theirs, "core", [(0, 1), (1, 0)])
    got_cot = moved(packed_cot)
    probs_shape = (HEADS, PATCH, PATCH)
    recip_shape = (HEADS, 1, PATCH)
    smem = pl.BlockSpec(memory_space=pltpu.SMEM)
    far = pl.BlockSpec(memory_space=pl.ANY)
    pair = HEADS * PATCH * PATCH
    packed_att, probs, recip, qkv, normed, xhat, inverse, heads = grid_call(
        forward_kernel,
        [dest, lengths, got_hidden, gain, qkv_weight_t, proj_weight],
        [smem, smem, whole(slots), whole((1, channels)), far, far],
        [(slots, BF16), (probs_shape, BF16), (recip_shape, F32), ((3 * channels, PATCH), BF16),
         ((channels, PATCH), BF16), ((channels, PATCH), F32), ((1, PATCH), F32),
         ((channels, PATCH), BF16)],
        [whole(slots), per_group((GROUP, PATCH, PATCH)), per_group((GROUP, 1, PATCH)),
         far, far, far, whole((1, PATCH)), whole((channels, PATCH))],
        [pltpu.VMEM(rows_c, F32), pltpu.VMEM(rows_c, BF16),
         pltpu.VMEM((3 * channels, channels), BF16), pltpu.VMEM(square, BF16),
         pltpu.VMEM((3 * channels, PATCH), BF16), pltpu.VMEM((channels, PATCH), BF16),
         pltpu.VMEM((channels, PATCH), F32), pltpu.SemaphoreType.DMA((2,)),
         pltpu.SemaphoreType.DMA((3,))],
        flops=2 * pair * 64 * 8, bytes_moved=32 << 20, exps=pair,
    )
    got_att = moved(packed_att)
    parts_shape = (4, chips, shard, channels)
    packed_dz, sent, kept = grid_call(
        backward_kernel,
        [dest, lengths, got_cot, probs, recip, qkv, normed, xhat, inverse, heads, gain, qkv_weight,
         proj_weight],
        [smem, smem, whole(slots), per_group((GROUP, PATCH, PATCH)), per_group((GROUP, 1, PATCH)),
         whole((3 * channels, PATCH)), far, far, whole((1, PATCH)), whole((channels, PATCH)),
         whole((1, channels)), far, whole(square)],
        [(slots, BF16), (parts_shape, BF16), (parts_shape, BF16)],
        [far] * 3,
        [pltpu.VMEM((3 * channels, PATCH), BF16), pltpu.VMEM(rows_c, BF16),
         pltpu.VMEM((channels, PATCH), BF16), pltpu.VMEM(square, BF16),
         pltpu.VMEM((channels, PATCH), BF16), pltpu.VMEM((channels, PATCH), F32),
         pltpu.VMEM((channels, 3 * channels), BF16), pltpu.SemaphoreType.DMA((3,)),
         pltpu.VMEM(slots, BF16), pltpu.VMEM(parts_shape, BF16), pltpu.VMEM(parts_shape, BF16),
         pltpu.SemaphoreType.DMA((5, 2))],
        flops=4 * pair * 64 * 8, bytes_moved=32 << 20, exps=0,
    )
    packed_dz, got_att = lax.optimization_barrier((packed_dz, got_att))
    got_dz = moved(packed_dz)
    tile_rows = own_call(
        tile_parts_kernel, [((chips, shard, channels), BF16)] * 4,
        [lax.ppermute(sent, "core", [(0, 1), (1, 0)]), kept], "va",
        [pltpu.VMEM(parts_shape, BF16), pltpu.VMEM(parts_shape, BF16),
         pltpu.SemaphoreType.DMA((4,)), pltpu.SemaphoreType.DMA((4,))],
        limit=8 << 20, moved=3 << 20,
    )
    got_dz, received = lax.optimization_barrier((got_dz, across_tiles(tile_rows)))
    mine = sum(one.astype(F32) for one in [tile_rows[0]] + received).astype(BF16)
    (d_hidden_b,) = own_call(
        hidden_grad_kernel, [(rows_c, BF16)], [dest, got_dz, cotangent], "sva",
        [pltpu.VMEM(rows_c, BF16), pltpu.VMEM(rows_c, BF16), pltpu.SemaphoreType.DMA((2,))],
        limit=8 << 20, moved=2 << 20,
    )
    d_other = lax.ppermute(d_hidden_b, "core", [(0, 1), (1, 0)])
    rows_here = TAPS * shard
    (chip_parts,) = own_call(
        conv_grad_kernel, [((chips, rows_here + shard, channels), BF16)],
        [d_other, d_hidden_b, ours, others, mine], "vaaav",
        [pltpu.VMEM(rows_c, BF16), pltpu.VMEM(halves, BF16), pltpu.VMEM(halves, BF16),
         pltpu.VMEM((TAPS + 1, chips, shard, channels), BF16),
         pltpu.SemaphoreType.DMA((TAPS + 1, 2)), pltpu.SemaphoreType.DMA((TAPS + 1,))],
        limit=20 << 20, flops=2 * TAPS * PATCH * channels * channels, moved=8 << 20,
    )
    total = summed(chip_parts, ("x", "z"))
    edge = (HALO, channels)
    feat_kept, to_previous, to_next, block_out = call(
        feat_grad_kernel, [(rows_c, F32), (edge, BF16), (edge, BF16), (rows_c, BF16)],
        [dest, turned, d_hidden_b, conv_weight, cotangent, got_dz, packed_hidden, got_att],
        smem=1, flops=3 * work, moved=8 << 20,
        scratch=[
            pltpu.VMEM((PATCH + 2 * HALO, channels), BF16),
            pltpu.VMEM((PATCH + 2 * HALO, channels), F32),
        ],
    )
    from_previous, from_next = halo(to_previous, to_next, SCENE)
    total, feat_kept, block_out = lax.optimization_barrier((total, feat_kept, block_out))
    arrived = from_others(total)
    zero = jnp.zeros((), BF16)
    top = lax.pad(from_previous, zero, ((0, PATCH - HALO, 0), (0, 0, 0)))
    bottom = lax.pad(from_next, zero, ((PATCH - HALO, 0, 0), (0, 0, 0)))
    feat_grad = (feat_kept + top.astype(F32) + bottom.astype(F32)).astype(BF16)
    rank = lax.axis_index("dp").astype(jnp.int32)
    near = pl.BlockSpec(memory_space=pltpu.VMEM)
    grads = [(TAPS, shard, channels), (shard, 3 * channels), (shard, channels)]
    conv_grad, qkv_grad, proj_grad = pl.pallas_call(
        last_kernel,
        out_shape=[jax.ShapeDtypeStruct(shape, F32) for shape in grads],
        in_specs=[smem] + [near] * 4,
        out_specs=[far] * 3,
        scratch_shapes=[pltpu.VMEM(shape, F32) for shape in grads]
        + [pltpu.SemaphoreType.DMA((3,))],
        compiler_params=pltpu.CompilerParams(vmem_limit_bytes=8 << 20),
        cost_estimate=pl.CostEstimate(flops=1 << 20, bytes_accessed=1 << 20, transcendentals=0),
    )(rank[None], total, *arrived)
    return (block_out[None], feat_grad[None], conv_grad, qkv_grad, proj_grad)


def solution(mesh):
    fine = Mesh(mesh.devices.reshape(4, 4, 2, 4), ("x", "z", "core", "dp"))
    return jax.shard_map(
        body,
        mesh=fine,
        in_specs=(
            P("dp", SCENE, None),
            P("dp", SCENE, None),
            P("dp", None),
            P("dp", SCENE),
            P(),
            P(),
            P(),
            P(),
            P("dp", SCENE, None),
        ),
        out_specs=(
            P("dp", SCENE, None),
            P("dp", SCENE, None),
            P(None, SCENE, None),
            P(SCENE, None),
            P(SCENE, None),
        ),
        check_vma=False,
    )
```
